32 devices in a mesh: dp: 16 (over z, y, core), tensor: 2 (over x).
Axes of the slice: x: 2, y: 2, z: 4, core: 2. Of those that a mesh axis runs over, the one named last changes fastest.
Arguments:
- tokens: bfloat16 [3, 2048, 2048], P(None, 'dp'), may hold values from -6 to 6
- doc_position: int32 [3, 2048], P(None, 'dp'), may hold values from 0 to 1023, as said below
- attn_gain: bfloat16 [2048], P('dp'), may hold values from 0.25 to 1.75
- w_query: bfloat16 [2048, 2048], P('dp', 'tensor'), may hold values from -0.125 to 0.125
- w_key: bfloat16 [2048, 256], P('dp', 'tensor'), may hold values from -0.125 to 0.125
- w_value: bfloat16 [2048, 256], P('dp', 'tensor'), may hold values from -0.125 to 0.125
- w_out: bfloat16 [2048, 2048], P('tensor', 'dp'), may hold values from -0.75 to 0.75
- ffn_gain: bfloat16 [2048], P('dp'), may hold values from 0.25 to 1.75
- w_gate: bfloat16 [2048, 5632], P('dp', 'tensor'), may hold values from -0.125 to 0.125
- w_up: bfloat16 [2048, 5632], P('dp', 'tensor'), may hold values from -0.125 to 0.125
- w_down: bfloat16 [5632, 2048], P('tensor', 'dp'), may hold values from -0.078125 to 0.078125
- cotangent: bfloat16 [3, 2048, 2048], P(None, 'dp'), may hold values from -6 to 6
Outputs:
- output: bfloat16 [3, 2048, 2048], P(None, 'dp')
- grad_tokens: float32 [3, 2048, 2048], P(None, 'dp')
- grad_attn_gain: float32 [2048], P('dp')
- grad_w_query: float32 [2048, 2048], P('dp', 'tensor')
- grad_w_key: float32 [2048, 256], P('dp', 'tensor')
- grad_w_value: float32 [2048, 256], P('dp', 'tensor')
- grad_w_out: float32 [2048, 2048], P('tensor', 'dp')
- grad_ffn_gain: float32 [2048], P('dp')
- grad_w_gate: float32 [2048, 5632], P('dp', 'tensor')
- grad_w_up: float32 [2048, 5632], P('dp', 'tensor')
- grad_w_down: float32 [5632, 2048], P('tensor', 'dp')
The draws below stay inside these ranges and needn't reach their ends.
Inputs may be any that keep to these rules, and one draw needn't show every extreme that they name: `doc_position`: each micro-batch is one packed sequence of documents. Documents start at every multiple of 1024 tokens and never cross one; positions count up by one within a document and restart at 0 where a new one begins; in each micro-batch one aligned span of 1024 tokens is a single document.
All inputs are finite; a program needn't handle non-finite values.
Results may differ from the reference program's by a relative error of at most 0.015.
Values may be sent and summed in bfloat16 or wider, within the bound.
A program may use at most 256 MiB of HBM per device.

```python
import jax
import jax.numpy as jnp
from jax import lax

D = 2048
HEADS = 32
KV_HEADS = 4
HEAD_DIM = 64
FF = 5632
SEQ_LEN = 1024
MICRO = 3
TOK_MB = 2048
SEQS_MB = 2


def draw_doc_position(key, part):
    key = jax.random.fold_in(key, 11)
    first_key, second_key = jax.random.split(key)
    starts = jax.random.randint(first_key, (MICRO, SEQS_MB, SEQ_LEN), 0, SEQ_LEN) < 6
    whole = jax.random.randint(second_key, (MICRO, 1, 1), 0, SEQS_MB)
    seq_ids = jnp.arange(SEQS_MB)[None, :, None]
    starts = jnp.where(seq_ids == whole, False, starts)
    places = jnp.arange(SEQ_LEN)[None, None, :]
    starts = starts | (places == 0)
    marked = jnp.where(starts, places, 0) + jnp.zeros((MICRO, SEQS_MB, SEQ_LEN), jnp.int32)
    latest = lax.cummax(marked, axis=2)
    return (places - latest).reshape(MICRO, SEQS_MB * SEQ_LEN).astype(jnp.int32)


def levels(key, extent, cuts, smallest, largest):
    level, own = 1.0, jax.random.fold_in(key, 6)
    for dim, parts in cuts:
        heights = jnp.exp(jax.random.uniform(jax.random.fold_in(own, dim), (parts,), jnp.float32, smallest / len(cuts), largest / len(cuts)))
        level = level * jnp.repeat(heights, extent[dim] // parts).reshape([-1 if axis == dim else 1 for axis in range(len(extent))])
    return level


def normal_values(key, shape, spread, most, shards=(), held_as=jnp.bfloat16):
    array = spread * jax.random.normal(key, shape, jnp.float32)
    if shards:
        array = array * levels(key, shape, shards, -0.22, 0.18)
    return jnp.clip(array, -most, most).astype(held_as)


def setup_inputs(seed: int = 0) -> dict:
    seeds = jax.random.split(jax.random.key(seed), 13)
    tokens = normal_values(seeds[0], (MICRO, TOK_MB, D), 1.0, 6.0, ((1, 16),))
    doc_position = draw_doc_position(jax.random.fold_in(seeds[12], 71), 0)
    attn_gain = jnp.clip(1.0 + 0.15 * jax.random.normal(seeds[2], (D,), jnp.float32), 0.25, 1.75).astype(jnp.bfloat16)
    w_query = normal_values(seeds[3], (D, HEADS * HEAD_DIM), D ** -0.5, 0.125, ((0, 16), (1, 2)))
    w_key = normal_values(seeds[4], (D, KV_HEADS * HEAD_DIM), D ** -0.5, 0.125, ((0, 16), (1, 2)))
    w_value = normal_values(seeds[5], (D, KV_HEADS * HEAD_DIM), D ** -0.5, 0.125, ((0, 16), (1, 2)))
    w_out = normal_values(seeds[6], (HEADS * HEAD_DIM, D), (HEADS * HEAD_DIM // 32) ** -0.5, 0.75, ((0, 2), (1, 16)))
    ffn_gain = jnp.clip(1.0 + 0.15 * jax.random.normal(seeds[7], (D,), jnp.float32), 0.25, 1.75).astype(jnp.bfloat16)
    w_gate = normal_values(seeds[8], (D, FF), D ** -0.5, 0.125, ((0, 16), (1, 2)))
    w_up = normal_values(seeds[9], (D, FF), D ** -0.5, 0.125, ((0, 16), (1, 2)))
    w_down = normal_values(seeds[10], (FF, D), FF ** -0.5, 0.078125, ((0, 2), (1, 16)))
    cotangent = normal_values(seeds[11], (MICRO, TOK_MB, D), 1.0, 6.0, ((1, 16),))
    return {"tokens": tokens, "doc_position": doc_position, "attn_gain": attn_gain, "w_query": w_query, "w_key": w_key, "w_value": w_value, "w_out": w_out, "ffn_gain": ffn_gain, "w_gate": w_gate, "w_up": w_up, "w_down": w_down, "cotangent": cotangent}


@jax.custom_vjp
def low(v):
    return lax.optimization_barrier(v.astype(jnp.bfloat16)).astype(jnp.float32)

@jax.custom_vjp
def low_back(v):
    return v

def low_keep(v):
    return (low(v), None)

def low_pass(kept, grad):
    return (grad,)

def back_keep(v):
    return (v, None)

def back_low(kept, grad):
    return (low(grad),)
low.defvjp(low_keep, low_pass)
low_back.defvjp(back_keep, back_low)
epsilon = 1e-05
highest = lax.Precision.HIGHEST

def product(left, right):
    return jnp.dot(left, right, precision=highest, preferred_element_type=jnp.float32)

def normalize(value, gain):
    return value * lax.rsqrt(lax.optimization_barrier(jnp.mean(value * value, axis=-1, keepdims=True)) + epsilon) * gain

def angles(position):
    power = jnp.arange(HEAD_DIM // 2, dtype=jnp.float32) * (2.0 / HEAD_DIM)
    inverse = 10000.0 ** (-power)
    turned = position.astype(jnp.float32)[:, None] * inverse[None, :]
    return (jnp.cos(turned)[:, None, :], jnp.sin(turned)[:, None, :])

def rotate(value, cosine, sine):
    half_dim = value.shape[-1] // 2
    first_half = value[..., :half_dim]
    second_half = value[..., half_dim:]
    return jnp.concatenate([first_half * cosine - second_half * sine, second_half * cosine + first_half * sine], axis=-1)

def attend_sequence(queries, keys, values, position):
    length = queries.shape[0]
    grouped = queries.reshape(length, KV_HEADS, HEADS // KV_HEADS, HEAD_DIM)
    scores = low_back(jnp.einsum('tkgd,jkd->kgtj', grouped, keys, precision=highest) * HEAD_DIM ** (-0.5))
    places = jnp.arange(length)
    distance = places[:, None] - places[None, :]
    allowed = (distance >= 0) & (distance <= position[:, None])
    scores = jnp.where(allowed, scores, -1e+30)
    shifted = scores - lax.optimization_barrier(jnp.max(scores, axis=-1, keepdims=True))
    expon = jnp.exp(shifted)
    probs = low(expon / lax.optimization_barrier(jnp.sum(expon, axis=-1, keepdims=True)))
    mixed = jnp.einsum('kgtj,jkd->tkgd', probs, values, precision=highest)
    return mixed.reshape(length, HEADS * HEAD_DIM)

def attend_item(item):
    return attend_sequence(item[0], item[1], item[2], item[3])

def layer_block(hidden_in, position, gain_one, query_w, key_w, value_w, out_w, gain_two, gate_w, up_w, down_w):
    count = hidden_in.shape[0]
    normed = low(normalize(hidden_in, gain_one))
    cosine, sine = angles(position)
    query_raw = low_back(product(normed, query_w)).reshape(count, HEADS, HEAD_DIM)
    queries = low(rotate(query_raw, cosine, sine))
    key_raw = low_back(product(normed, key_w)).reshape(count, KV_HEADS, HEAD_DIM)
    keys = low(rotate(key_raw, cosine, sine))
    values = low(low_back(product(normed, value_w))).reshape(count, KV_HEADS, HEAD_DIM)
    sequences = count // SEQ_LEN
    mixed = lax.map(jax.checkpoint(attend_item), (queries.reshape(sequences, SEQ_LEN, HEADS, HEAD_DIM), keys.reshape(sequences, SEQ_LEN, KV_HEADS, HEAD_DIM), values.reshape(sequences, SEQ_LEN, KV_HEADS, HEAD_DIM), position.reshape(sequences, SEQ_LEN)))
    mixed = low(low_back(mixed.reshape(count, HEADS * HEAD_DIM)))
    middle = hidden_in + low_back(product(mixed, out_w))
    normed_two = low(normalize(middle, gain_two))
    gate = low_back(product(normed_two, gate_w))
    upward = low_back(product(normed_two, up_w))
    activated = low(jax.nn.silu(gate) * upward)
    return middle + low_back(product(activated, down_w))

def reference(tokens, doc_position, attn_gain, w_query, w_key, w_value, w_out, ffn_gain, w_gate, w_up, w_down, cotangent):

    def forward(hidden_all, gain_one, query_w, key_w, value_w, out_w, gain_two, gate_w, up_w, down_w):

        def one_batch(item):
            return layer_block(item[0], item[1], gain_one, query_w, key_w, value_w, out_w, gain_two, gate_w, up_w, down_w)
        return lax.map(one_batch, (hidden_all, doc_position))
    inputs = tuple((entry.astype(jnp.float32) for entry in (tokens, attn_gain, w_query, w_key, w_value, w_out, ffn_gain, w_gate, w_up, w_down)))
    final, pull_back = jax.vjp(forward, *inputs)
    grads = pull_back(cotangent.astype(jnp.float32))
    return (final.astype(jnp.bfloat16), grads[0], grads[1], grads[2], grads[3], grads[4], grads[5], grads[6], grads[7], grads[8], grads[9])
```

```python
import functools

import jax
import jax.numpy as jnp
from jax import lax
from jax.experimental import pallas as pl
from jax.experimental.pallas import tpu as pltpu
from jax.sharding import PartitionSpec as P

HEAD_DIM = 64
SEQ_LEN = 1024
BF = jnp.bfloat16
F32 = jnp.float32
epsilon = 1e-05
VMEM_LIMIT = 48 * 1024 * 1024


def swap_core(block):
    size = lax.axis_size("dp")
    return lax.ppermute(block, "dp", [(i, i ^ 1) for i in range(size)])


def swap_chip(block, distance):
    size = lax.axis_size("dp")
    return lax.ppermute(block, "dp", [(i, i ^ (2 * distance)) for i in range(size)])


def swap_tensor(block):
    return lax.ppermute(block, "tensor", [(0, 1), (1, 0)])


def gather_blocks(own, order):
    held = {0: own}
    for bit in order:
        came = {key | bit: swap_chip(block, bit) for key, block in held.items()}
        held.update(came)
    return held


def scatter_blocks(blocks, order):
    held = dict(blocks)
    for bit in reversed(order):
        kept = {}
        for key in sorted(held):
            if key & bit:
                came = swap_chip(held[key].astype(BF), bit)
                kept[key ^ bit] = came
        held = {key: held[key].astype(F32) + came.astype(F32) for key, came in kept.items()}
    return held[0]


def dot_plain(left, right):
    return jnp.dot(left, right, preferred_element_type=F32)


def dot_first(left, right):
    return lax.dot_general(left, right, (((0,), (0,)), ((), ())), preferred_element_type=F32)


def dot_last(left, right):
    return lax.dot_general(left, right, (((1,), (1,)), ((), ())), preferred_element_type=F32)


def norm_back(grad, value, ratio, gain):
    scaled = grad * gain
    inner = jnp.mean(scaled * value, axis=-1, keepdims=True)
    return (ratio * scaled - value * ratio**3 * inner, jnp.sum(grad * value * ratio, axis=0))


def turn(value, cosine, sine, back):
    tiles = []
    lane = lax.broadcasted_iota(jnp.int32, (value.shape[0], 128), 1)
    first = (lane % 64) < 32
    for start in range(0, value.shape[1], 128):
        tile = value[:, start : start + 128]
        up = pltpu.roll(tile, 96, 1)
        down = pltpu.roll(tile, 32, 1)
        if back:
            other = jnp.where(first, up, -down)
        else:
            other = jnp.where(first, -up, down)
        tiles.append(tile * cosine + other * sine)
    return tiles[0] if len(tiles) == 1 else jnp.concatenate(tiles, axis=1)


def project_kernel(n_ref, w_ref, cos_ref, sin_ref, q_ref, kv_ref):
    raw = jnp.dot(n_ref[...], w_ref[...], preferred_element_type=F32)
    heads = raw.shape[1] - 128
    cosine, sine = cos_ref[...], sin_ref[...]
    q_ref[...] = (turn(raw[:, :heads], cosine, sine, False) * HEAD_DIM ** (-0.5)).astype(BF)
    both = raw[:, heads:]
    turned = turn(both, cosine, sine, False)
    lane = lax.broadcasted_iota(jnp.int32, both.shape, 1)
    kv_ref[...] = jnp.where(lane < HEAD_DIM, turned, both).astype(BF)


def project(normed, weight, cosine, sine):
    rows, depth = normed.shape
    cols = weight.shape[1]
    step = 256
    return pl.pallas_call(
        project_kernel,
        grid=(rows // step,),
        in_specs=[
            pl.BlockSpec((step, depth), lambda i: (i, 0)),
            pl.BlockSpec((depth, cols), lambda i: (0, 0)),
            pl.BlockSpec((step, 128), lambda i: (i, 0)),
            pl.BlockSpec((step, 128), lambda i: (i, 0)),
        ],
        out_specs=[
            pl.BlockSpec((step, cols - 128), lambda i: (i, 0)),
            pl.BlockSpec((step, 128), lambda i: (i, 0)),
        ],
        out_shape=[
            jax.ShapeDtypeStruct((rows, cols - 128), BF),
            jax.ShapeDtypeStruct((rows, 128), BF),
        ],
        compiler_params=pltpu.CompilerParams(vmem_limit_bytes=VMEM_LIMIT),
        cost_estimate=pl.CostEstimate(
            flops=2 * rows * depth * cols,
            bytes_accessed=2 * (rows * depth + depth * cols + rows * cols) + 8 * rows * 128,
            transcendentals=0,
        ),
        name="project",
    )(normed, weight, cosine, sine)


def mask_bias(kpos_ref, row_ref):
    row = row_ref[0]
    place, floor = row[0:1, :], row[1:2, :]
    kpos = kpos_ref[...]
    allowed = (kpos <= place) & (kpos >= floor)
    return jnp.where(allowed, 0.0, -1e30).astype(F32)


def attend_kernel(count, kpos_ref, row_ref, q_ref, *refs):
    kv_refs, (mixed_ref, lse_ref, bias_ref) = refs[:count], refs[count:]
    rows = 256
    kv = jnp.concatenate([ref[...].reshape(rows, 128) for ref in kv_refs], axis=0)
    keys = kv[:, :HEAD_DIM]
    values_t = kv.T[HEAD_DIM:, :]
    bias_ref[...] = mask_bias(kpos_ref, row_ref)
    queries = q_ref[...].reshape(rows, q_ref.shape[-1])
    parts = []
    sums = []
    for head in range(queries.shape[1] // HEAD_DIM):
        q_head = queries[:, head * HEAD_DIM : (head + 1) * HEAD_DIM]
        scores = dot_last(keys, q_head) + bias_ref[...]
        peak = jnp.max(scores, axis=0, keepdims=True)
        expon = jnp.exp(scores - peak)
        total = jnp.sum(expon, axis=0, keepdims=True)
        mixed = dot_plain(values_t, expon.astype(BF)) * (1.0 / total)
        parts.append(mixed)
        sums.append(peak + jnp.log(total))
    mixed_t = jnp.concatenate(parts, axis=0)
    mixed_ref[...] = mixed_t.T.astype(BF).reshape(mixed_ref.shape)
    lse_ref[0] = jnp.concatenate(sums, axis=0)


def attend(kpos, rowinfo, queries, kvs):
    half, micro, rows, cols = queries.shape
    heads = cols // HEAD_DIM
    span = kpos.shape[0]
    tokens = half * rows
    kv_spec = pl.BlockSpec((half, 1, rows, 128), lambda i: (0, i, 0, 0))
    q_spec = pl.BlockSpec((half, 1, rows, cols), lambda i: (0, i, 0, 0))
    return pl.pallas_call(
        functools.partial(attend_kernel, len(kvs)),
        grid=(micro,),
        in_specs=[
            pl.BlockSpec((span, 1), lambda i: (0, 0)),
            pl.BlockSpec((1, 2, tokens), lambda i: (i, 0, 0)),
            q_spec,
        ]
        + [kv_spec] * len(kvs),
        out_specs=[q_spec, pl.BlockSpec((1, heads, tokens), lambda i: (i, 0, 0))],
        out_shape=[
            jax.ShapeDtypeStruct(queries.shape, BF),
            jax.ShapeDtypeStruct((micro, heads, tokens), F32),
        ],
        scratch_shapes=[pltpu.VMEM((span, tokens), F32)],
        compiler_params=pltpu.CompilerParams(vmem_limit_bytes=VMEM_LIMIT),
        cost_estimate=pl.CostEstimate(
            flops=16 * micro * heads * tokens * span * HEAD_DIM,
            bytes_accessed=4 * micro * tokens * cols,
            transcendentals=micro * heads * tokens * span,
        ),
        name="attend",
    )(kpos, rowinfo, queries, *kvs)


def attend_back_kernel(
    count, kpos_ref, row_ref, cos_ref, sin_ref, q_ref, go_ref, lse_ref, *refs
):
    kv_refs = refs[:count]
    dq_ref = refs[count]
    dkv_refs = refs[count + 1 : 2 * count + 1]
    bias_ref, dk_ref, dv_ref = refs[2 * count + 1 :]
    rows = 256
    kv = jnp.concatenate([ref[...].reshape(rows, 128) for ref in kv_refs], axis=0)
    keys = kv[:, :HEAD_DIM]
    values = kv[:, HEAD_DIM:]
    keys_t = kv.T[:HEAD_DIM, :]
    bias_ref[...] = mask_bias(kpos_ref, row_ref)
    queries = q_ref[...].reshape(rows, q_ref.shape[-1])
    grads = go_ref[...].reshape(rows, q_ref.shape[-1])
    parts = []
    for head in range(queries.shape[1] // HEAD_DIM):
        q_head = queries[:, head * HEAD_DIM : (head + 1) * HEAD_DIM]
        g_head = grads[:, head * HEAD_DIM : (head + 1) * HEAD_DIM]
        scores = dot_last(keys, q_head) + bias_ref[...]
        probs = jnp.exp(scores - lse_ref[0, head : head + 1, :])
        grad_probs = dot_last(values, g_head)
        inner = jnp.sum(probs * grad_probs, axis=0, keepdims=True)
        grad_scores = (probs * (grad_probs - inner)).astype(BF)
        grad_values = dot_plain(probs.astype(BF), g_head)
        grad_keys = dot_plain(grad_scores, q_head)
        if head == 0:
            dv_ref[...] = grad_values
            dk_ref[...] = grad_keys
        else:
            dv_ref[...] += grad_values
            dk_ref[...] += grad_keys
        parts.append(dot_plain(keys_t, grad_scores))
    grad_queries = jnp.concatenate(parts, axis=0).T * HEAD_DIM ** (-0.5)
    cosine = cos_ref[...].reshape(rows, 128)
    sine = sin_ref[...].reshape(rows, 128)
    dq_ref[...] = turn(grad_queries, cosine, sine, True).astype(BF).reshape(dq_ref.shape)
    both = jnp.concatenate([dk_ref[...], dv_ref[...]], axis=1)
    for place, ref in enumerate(dkv_refs):
        ref[...] = both[place * rows : (place + 1) * rows].astype(ref.dtype).reshape(ref.shape)


def attend_back(kpos, rowinfo, cosine, sine, queries, grads, lse, kvs):
    half, micro, rows, cols = queries.shape
    heads = cols // HEAD_DIM
    span = kpos.shape[0]
    tokens = half * rows
    kv_spec = pl.BlockSpec((half, 1, rows, 128), lambda i: (0, i, 0, 0))
    q_spec = pl.BlockSpec((half, 1, rows, cols), lambda i: (0, i, 0, 0))
    return pl.pallas_call(
        functools.partial(attend_back_kernel, len(kvs)),
        grid=(micro,),
        in_specs=[
            pl.BlockSpec((span, 1), lambda i: (0, 0)),
            pl.BlockSpec((1, 2, tokens), lambda i: (i, 0, 0)),
            kv_spec,
            kv_spec,
            q_spec,
            q_spec,
            pl.BlockSpec((1, heads, tokens), lambda i: (i, 0, 0)),
        ]
        + [kv_spec] * len(kvs),
        out_specs=[q_spec] + [kv_spec] * len(kvs),
        out_shape=[jax.ShapeDtypeStruct(queries.shape, BF)]
        + [
            jax.ShapeDtypeStruct((half, micro, rows, 128), F32 if place == 0 else BF)
            for place in range(len(kvs))
        ],
        scratch_shapes=[
            pltpu.VMEM((span, tokens), F32),
            pltpu.VMEM((span, HEAD_DIM), F32),
            pltpu.VMEM((span, HEAD_DIM), F32),
        ],
        compiler_params=pltpu.CompilerParams(vmem_limit_bytes=VMEM_LIMIT),
        cost_estimate=pl.CostEstimate(
            flops=40 * micro * heads * tokens * span * HEAD_DIM,
            bytes_accessed=8 * micro * tokens * cols,
            transcendentals=micro * heads * tokens * span,
        ),
        name="attend_back",
    )(kpos, rowinfo, cosine, sine, queries, grads, lse, *kvs)


def body(
    tokens,
    doc_position,
    attn_gain,
    w_query,
    w_key,
    w_value,
    w_out,
    ffn_gain,
    w_gate,
    w_up,
    w_down,
    cotangent,
):
    size = lax.axis_size("dp")
    chips = size // 2
    bits = [1 << place for place in range(chips.bit_length() - 1)]
    me = lax.axis_index("dp")
    core = me % 2
    chip = me // 2
    micro, stretch, width = tokens.shape
    count = micro * stretch
    block = width // chips

    late_first = bits[::-1]
    span_chips = SEQ_LEN // (2 * stretch)
    in_span = chip % span_chips

    keys_order = [0]
    for bit in late_first:
        keys_order = keys_order + [key | bit for key in keys_order]

    def rearranged(array):
        return jnp.concatenate(
            [
                lax.dynamic_slice_in_dim(array, (chip ^ key) * block, block, array.ndim - 1)
                for key in keys_order
            ],
            axis=-1,
        )

    def restored(array):
        where = [keys_order.index(key) for key in range(chips)]
        places = jnp.array(where, jnp.int32)
        return jnp.concatenate(
            [
                lax.dynamic_slice_in_dim(
                    array, places[chip ^ natural] * block, block, array.ndim - 1
                )
                for natural in range(chips)
            ],
            axis=-1,
        )

    def split_core(weight):
        half = weight.shape[1] // 2
        first, second = weight[:, :half], weight[:, half:]
        mine = jnp.where(core == 0, first, second)
        other = jnp.where(core == 0, second, first)
        return mine, other

    def joined_core(mine, came):
        return jnp.where(
            core == 0,
            jnp.concatenate([mine, came], axis=0),
            jnp.concatenate([came, mine], axis=0),
        )

    attn_parts = [split_core(w) for w in (w_query, w_key, w_value, w_out.T)]
    attn_mine = jnp.concatenate([p[0] for p in attn_parts], axis=1)
    attn_other = jnp.concatenate([p[1] for p in attn_parts], axis=1)
    attn_own = joined_core(attn_mine, swap_core(attn_other))
    gate_parts = split_core(w_gate)
    gate_own = joined_core(gate_parts[0], swap_core(gate_parts[1]))
    up_parts = split_core(w_up)
    up_own = joined_core(up_parts[0], swap_core(up_parts[1]))
    down_parts = split_core(w_down.T)
    down_own = joined_core(down_parts[0], swap_core(down_parts[1]))

    def whole(own, order):
        held = gather_blocks(own, order)
        return jnp.concatenate([held[key] for key in keys_order], axis=0)

    gains = jnp.stack([attn_gain, ffn_gain])
    gains = lax.all_gather(gains, "dp", axis=1, tiled=True).astype(F32)
    gains = rearranged(gains)
    gain_one, gain_two = gains[0:1], gains[1:2]

    hidden = rearranged(tokens.reshape(count, width))
    grad_final = rearranged(cotangent.reshape(count, width))
    hidden_f = hidden.astype(F32)
    ratio_one = lax.rsqrt(jnp.mean(hidden_f * hidden_f, axis=-1, keepdims=True) + epsilon)
    normed_own = (hidden_f * ratio_one * gain_one).astype(BF)
    normed = jnp.concatenate([normed_own, swap_core(normed_own)], axis=0)
    grad_final_both = jnp.concatenate([grad_final, swap_core(grad_final)], axis=0)
    position_both = jnp.stack([doc_position, swap_core(doc_position)])

    power = jnp.arange(HEAD_DIM // 2, dtype=F32) * (2.0 / HEAD_DIM)
    inverse = 10000.0 ** (-power)
    turned = position_both.reshape(2 * count).astype(F32)[:, None] * jnp.tile(inverse, 4)[None, :]
    cosine, sine = jnp.cos(turned), jnp.sin(turned)

    inner = jnp.arange(2 * stretch, dtype=jnp.int32) ^ (core * stretch)
    row_place = in_span * (2 * stretch) + inner
    kpos = jnp.concatenate(
        [(in_span ^ key) * (2 * stretch) + inner for key in range(span_chips)]
    ).reshape(-1, 1)
    row_position = position_both.transpose(1, 0, 2).reshape(micro, 2 * stretch)
    row_places = jnp.broadcast_to(row_place[None, :], row_position.shape)
    rowinfo = jnp.stack([row_places, row_places - row_position], axis=1)

    attn_w = whole(attn_own, late_first)
    n_q = w_query.shape[1] // 2
    n_kv = w_key.shape[1] // 2
    qkv_w = attn_w[:, : n_q + 2 * n_kv]
    out_wt = attn_w[:, n_q + 2 * n_kv :]
    queries, kv_own = project(normed, qkv_w, cosine, sine)
    kv_shape = (2, micro, stretch, 2 * n_kv)
    kvs = [kv_own.reshape(kv_shape)] + [
        swap_chip(kv_own, key).reshape(kv_shape) for key in range(1, span_chips)
    ]
    queries = queries.reshape(2, micro, stretch, n_q)
    mixed, lse = attend(kpos, rowinfo, queries, kvs)
    mixed = mixed.reshape(2 * count, n_q)

    def summed(partial):
        partial = partial.astype(BF)
        mine = (partial[:count].astype(F32) + swap_core(partial[count:]).astype(F32)).astype(BF)
        return mine.astype(F32) + swap_tensor(mine).astype(F32)

    attended = summed(dot_last(mixed, out_wt))
    middle = hidden_f + attended
    ratio_two = lax.rsqrt(jnp.mean(middle * middle, axis=-1, keepdims=True) + epsilon)
    normed_two_own = (middle * ratio_two * gain_two).astype(BF)
    normed_two = jnp.concatenate([normed_two_own, swap_core(normed_two_own)], axis=0)

    gate_w = whole(gate_own, late_first)
    up_w = whole(up_own, late_first)
    down_wt = whole(down_own, late_first)
    gate = dot_plain(normed_two, gate_w)
    upward = dot_plain(normed_two, up_w)
    sigmoid = jax.nn.sigmoid(gate)
    silu = gate * sigmoid
    activated = (silu * upward).astype(BF)

    def weight_grad(left, right, order):
        first = order[-1]
        top = [place for place, key in enumerate(keys_order) if key & first]
        half = chips // 2
        assert top == list(range(half, chips))
        sent = dot_first(left[:, half * block :], right).astype(BF)
        kept = dot_first(left[:, : half * block], right)
        blocks = {}
        for place in range(half):
            blocks[keys_order[place]] = kept[place * block : (place + 1) * block]
            blocks[keys_order[place + half]] = sent[place * block : (place + 1) * block]
        return scatter_blocks(blocks, order)

    def unsplit_core(total):
        half = block // 2
        mine = jnp.where(core == 0, total[:half], total[half:])
        other = jnp.where(core == 0, total[half:], total[:half])
        came = swap_core(other)
        return mine, came

    def columns(mine, came):
        return jnp.where(
            core == 0,
            jnp.concatenate([mine, came], axis=1),
            jnp.concatenate([came, mine], axis=1),
        )

    grad_down = weight_grad(grad_final_both, activated, late_first)
    feed = summed(dot_last(activated, down_wt))
    output = restored((middle + feed).astype(BF))

    grad_act = dot_plain(grad_final_both, down_wt)
    grad_gate_low = (grad_act * upward * sigmoid * (1.0 + gate * (1.0 - sigmoid))).astype(BF)
    grad_up_low = (grad_act * silu).astype(BF)
    grad_normed_two = summed(dot_last(grad_gate_low, gate_w) + dot_last(grad_up_low, up_w))
    grad_gate = weight_grad(normed_two, grad_gate_low, late_first)
    grad_up = weight_grad(normed_two, grad_up_low, late_first)
    grad_mid_norm, grad_gain_two = norm_back(grad_normed_two, middle, ratio_two, gain_two)
    grad_middle = grad_final.astype(F32) + grad_mid_norm
    grad_middle_low = grad_middle.astype(BF)
    grad_middle_both = jnp.concatenate([grad_middle_low, swap_core(grad_middle_low)], axis=0)

    grad_mixed = dot_plain(grad_middle_both, out_wt).astype(BF)
    results = attend_back(
        kpos,
        rowinfo,
        cosine.reshape(2, micro, stretch, 128),
        sine.reshape(2, micro, stretch, 128),
        queries,
        grad_mixed.reshape(queries.shape),
        lse,
        kvs,
    )
    grad_query_raw = results[0].reshape(2 * count, n_q)
    grad_kv = results[1].reshape(2 * count, 2 * n_kv)
    for key in range(1, span_chips):
        grad_kv = grad_kv + swap_chip(results[1 + key].reshape(2 * count, 2 * n_kv), key).astype(
            F32
        )
    grad_k, grad_v = grad_kv[:, :n_kv], grad_kv[:, n_kv:]
    half_dim = HEAD_DIM // 2
    cos_h, sin_h = cosine[:, :half_dim], sine[:, :half_dim]
    first_half, second_half = grad_k[:, :half_dim], grad_k[:, half_dim:]
    grad_raw = jnp.concatenate(
        [
            grad_query_raw,
            (first_half * cos_h + second_half * sin_h).astype(BF),
            (second_half * cos_h - first_half * sin_h).astype(BF),
            grad_v.astype(BF),
        ],
        axis=1,
    )
    grad_out_t = weight_grad(grad_middle_both, mixed, late_first)
    grad_qkv = weight_grad(normed, grad_raw, late_first)
    grad_normed = summed(dot_last(grad_raw, qkv_w))
    grad_in_norm, grad_gain_one = norm_back(grad_normed, hidden_f, ratio_one, gain_one)
    grad_tokens = restored(grad_middle + grad_in_norm)

    grad_gains = restored(jnp.stack([grad_gain_one, grad_gain_two]))
    grad_gains = lax.psum_scatter(grad_gains, "dp", scatter_dimension=1, tiled=True)

    def split_cols(pair, start, stop):
        return columns(pair[0][:, start:stop], pair[1][:, start:stop])

    pair = unsplit_core(grad_qkv)
    grad_w_query = split_cols(pair, 0, n_q)
    grad_w_key = split_cols(pair, n_q, n_q + n_kv)
    grad_w_value = split_cols(pair, n_q + n_kv, n_q + 2 * n_kv)
    grad_w_out = columns(*unsplit_core(grad_out_t)).T
    grad_w_gate = columns(*unsplit_core(grad_gate))
    grad_w_up = columns(*unsplit_core(grad_up))
    grad_w_down = columns(*unsplit_core(grad_down)).T
    return (
        output.reshape(tokens.shape),
        grad_tokens.reshape(tokens.shape),
        grad_gains[0],
        grad_w_query,
        grad_w_key,
        grad_w_value,
        grad_w_out,
        grad_gains[1],
        grad_w_gate,
        grad_w_up,
        grad_w_down,
    )


def solution(mesh):
    return jax.shard_map(
        body,
        mesh=mesh,
        in_specs=(
            P(None, "dp", None),
            P(None, "dp"),
            P("dp"),
            P("dp", "tensor"),
            P("dp", "tensor"),
            P("dp", "tensor"),
            P("tensor", "dp"),
            P("dp"),
            P("dp", "tensor"),
            P("dp", "tensor"),
            P("tensor", "dp"),
            P(None, "dp", None),
        ),
        out_specs=(
            P(None, "dp", None),
            P(None, "dp", None),
            P("dp"),
            P("dp", "tensor"),
            P("dp", "tensor"),
            P("dp", "tensor"),
            P("tensor", "dp"),
            P("dp"),
            P("dp", "tensor"),
            P("dp", "tensor"),
            P("tensor", "dp"),
        ),
        check_vma=False,
    )
```

```python
import functools

import jax
import jax.numpy as jnp
from jax import lax
from jax.experimental import pallas as pl
from jax.experimental.pallas import tpu as pltpu
from jax.sharding import PartitionSpec as P

HEAD_DIM = 64
SEQ_LEN = 1024
BF = jnp.bfloat16
F32 = jnp.float32
epsilon = 1e-05
VMEM_LIMIT = 48 * 1024 * 1024


def swap_core(block):
    size = lax.axis_size("dp")
    return lax.ppermute(block, "dp", [(i, i ^ 1) for i in range(size)])


def swap_chip(block, distance):
    size = lax.axis_size("dp")
    return lax.ppermute(block, "dp", [(i, i ^ (2 * distance)) for i in range(size)])


def swap_tensor(block):
    return lax.ppermute(block, "tensor", [(0, 1), (1, 0)])


def gather_blocks(own, order):
    held = {0: own}
    for bit in order:
        came = {key | bit: swap_chip(block, bit) for key, block in held.items()}
        held.update(came)
    return held


def scatter_blocks(blocks, order):
    held = dict(blocks)
    for bit in reversed(order):
        kept = {}
        for key in sorted(held):
            if key & bit:
                came = swap_chip(held[key].astype(BF), bit)
                kept[key ^ bit] = came
        held = {key: held[key].astype(F32) + came.astype(F32) for key, came in kept.items()}
    return held[0]


def flipped(index, distance):
    return index + distance * (1 - 2 * ((index // distance) % 2))


def peer(distance=0, core=False, tensor=False):
    place = lax.axis_index("dp")
    bit = 1
    while bit <= distance:
        if distance & bit:
            place = flipped(place, 2 * bit)
        bit *= 2
    if core:
        place = flipped(place, 1)
    half = lax.axis_index("tensor")
    if tensor:
        half = 1 - half
    return (place, half)


def greet(peers):
    barrier = pltpu.get_barrier_semaphore()
    for device in peers:
        pl.semaphore_signal(barrier, inc=1, device_id=device, device_id_type=pl.DeviceIdType.MESH)
    pl.semaphore_wait(barrier, len(peers))


def remote(src, dst, send, recv, device):
    return pltpu.make_async_remote_copy(
        src_ref=src,
        dst_ref=dst,
        send_sem=send,
        recv_sem=recv,
        device_id=device,
        device_id_type=pl.DeviceIdType.MESH,
    )


def cuts(cols, parts):
    tiles = cols // 128
    edges = [tiles * part // parts * 128 for part in range(parts + 1)]
    return [(edges[i], edges[i + 1] - edges[i]) for i in range(parts)]


class Spread:
    def __init__(self, src, dst, rows, start, cols, order, places, sems):
        self.src, self.dst, self.rows = src, dst, rows
        self.start, self.cols = start, cols
        self.order, self.places = order, places
        self.sems = sems
        self.copies = []
        self.count = 0
        self.core = lax.axis_index("dp") % 2

    def sem(self):
        self.count += 1
        return self.sems[0].at[self.count - 1], self.sems[1].at[self.count - 1]

    def begin(self):
        half = self.rows // 2
        width = self.dst.shape[1]
        if self.src.shape[1] == width:
            own = other = self.src
        else:
            span = pl.ds(pl.multiple_of(self.core * width + self.start, 128), self.cols)
            own = self.src.at[:, span]
            span = pl.ds(pl.multiple_of((1 - self.core) * width + self.start, 128), self.cols)
            other = self.src.at[:, span]
        mine = self.dst.at[
            pl.ds(pl.multiple_of(self.core * half, half), half), pl.ds(self.start, self.cols)
        ]
        send, recv = self.sem()
        self.local = pltpu.make_async_copy(own, mine, self.sems[2])
        self.local.start()
        copy = remote(other, mine, send, recv, peer(core=True))
        copy.start()
        self.stage = [copy]
        self.copies.append(copy)
        self.held = [0]
        self.level = 0

    def wait(self):
        for copy in self.stage:
            copy.wait_recv()
        if self.level == 0:
            self.local.wait()

    def block(self, key):
        return self.dst.at[
            pl.ds(self.places[key] * self.rows, self.rows), pl.ds(self.start, self.cols)
        ]

    def step(self):
        self.wait()
        if self.level == len(self.order):
            return False
        bit = self.order[self.level]
        self.stage = []
        for key in self.held:
            send, recv = self.sem()
            copy = remote(self.block(key), self.block(key | bit), send, recv, peer(bit))
            copy.start()
            self.stage.append(copy)
            self.copies.append(copy)
        self.held = self.held + [key | bit for key in self.held]
        self.level += 1
        return True

    def close(self):
        for copy in self.copies:
            copy.wait_send()


def gather_kernel(order, places, pieces, *refs):
    chips = len(places)
    n = len(pieces)
    srcs, (hid_src, cot_src) = refs[:n], refs[n : n + 2]
    dsts, (hid_dst, cot_dst) = refs[n + 2 : 2 * n + 2], refs[2 * n + 2 : 2 * n + 4]
    send, recv, local, side = refs[2 * n + 4 :]
    bits = [1 << place for place in range(chips.bit_length() - 1)]
    greet([peer(core=True)] + [peer(bit) for bit in bits])

    spreads = []
    for src, dst, (parts, rows, way) in zip(srcs, dsts, pieces):
        for start, cols in cuts(dst.shape[1], parts):
            at = len(spreads)
            spreads.append(
                Spread(
                    src, dst, rows, start, cols, way, places,
                    (send.at[at], recv.at[at], local.at[at]),
                )
            )
    count = hid_src.shape[0]
    extra = []
    for at, (src, dst) in enumerate(((hid_src, hid_dst), (cot_src, cot_dst))):
        own = pltpu.make_async_copy(src, dst.at[pl.ds(0, count)], side.at[3 * at])
        own.start()
        other = remote(
            src, dst.at[pl.ds(count, count)], side.at[3 * at + 1], side.at[3 * at + 2],
            peer(core=True),
        )
        other.start()
        extra += [own, other]
    for spread in spreads:
        spread.begin()
    levels = len(order)
    for tick in range(len(spreads) + levels):
        for level in range(levels + 1):
            if 0 <= tick - level < len(spreads):
                spreads[tick - level].step()
    for spread in spreads:
        spread.close()
    for copy in extra:
        copy.wait()


def gather_all(chips, order, places, sources, parts, ways, hidden, cotangent):
    pieces = []
    shapes = []
    for source, part, way in zip(sources, parts, ways):
        same = source.shape[1] == 128
        rows = 2 * source.shape[0]
        cols = source.shape[1] if same else source.shape[1] // 2
        pieces.append((part, rows, way))
        shapes.append(jax.ShapeDtypeStruct((rows * chips, cols), source.dtype))
    count, width = hidden.shape
    shapes += [jax.ShapeDtypeStruct((2 * count, width), BF)] * 2
    total = sum(parts)
    any_spec = pl.BlockSpec(memory_space=pl.ANY)
    return pl.pallas_call(
        functools.partial(gather_kernel, order, places, pieces),
        in_specs=[any_spec] * (len(sources) + 2),
        out_specs=[any_spec] * len(shapes),
        out_shape=shapes,
        scratch_shapes=[
            pltpu.SemaphoreType.DMA((total, chips)),
            pltpu.SemaphoreType.DMA((total, chips)),
            pltpu.SemaphoreType.DMA((total,)),
            pltpu.SemaphoreType.DMA((6,)),
        ],
        compiler_params=pltpu.CompilerParams(collective_id=0, has_side_effects=True),
        name="gather",
    )(*sources, hidden, cotangent)


def dot_plain(left, right):
    return jnp.dot(left, right, preferred_element_type=F32)


def dot_first(left, right):
    return lax.dot_general(left, right, (((0,), (0,)), ((), ())), preferred_element_type=F32)


def dot_last(left, right):
    return lax.dot_general(left, right, (((1,), (1,)), ((), ())), preferred_element_type=F32)


def norm_back(grad, value, ratio, gain):
    scaled = grad * gain
    inner = jnp.mean(scaled * value, axis=-1, keepdims=True)
    return (ratio * scaled - value * ratio**3 * inner, jnp.sum(grad * value * ratio, axis=0))


def turn(value, cosine, sine, back):
    tiles = []
    lane = lax.broadcasted_iota(jnp.int32, (value.shape[0], 128), 1)
    first = (lane % 64) < 32
    for start in range(0, value.shape[1], 128):
        tile = value[:, start : start + 128]
        up = pltpu.roll(tile, 96, 1)
        down = pltpu.roll(tile, 32, 1)
        if back:
            other = jnp.where(first, up, -down)
        else:
            other = jnp.where(first, -up, down)
        tiles.append(tile * cosine + other * sine)
    return tiles[0] if len(tiles) == 1 else jnp.concatenate(tiles, axis=1)


def project_kernel(n_ref, w_ref, cos_ref, sin_ref, q_ref, kv_ref):
    raw = jnp.dot(n_ref[...], w_ref[...], preferred_element_type=F32)
    heads = raw.shape[1] - 128
    cosine, sine = cos_ref[...], sin_ref[...]
    q_ref[...] = (turn(raw[:, :heads], cosine, sine, False) * HEAD_DIM ** (-0.5)).astype(BF)
    both = raw[:, heads:]
    turned = turn(both, cosine, sine, False)
    lane = lax.broadcasted_iota(jnp.int32, both.shape, 1)
    kv_ref[...] = jnp.where(lane < HEAD_DIM, turned, both).astype(BF)


def project(normed, weight, cosine, sine):
    rows, depth = normed.shape
    cols = weight.shape[1]
    step = 256
    return pl.pallas_call(
        project_kernel,
        grid=(rows // step,),
        in_specs=[
            pl.BlockSpec((step, depth), lambda i: (i, 0)),
            pl.BlockSpec((depth, cols), lambda i: (0, 0)),
            pl.BlockSpec((step, 128), lambda i: (i, 0)),
            pl.BlockSpec((step, 128), lambda i: (i, 0)),
        ],
        out_specs=[
            pl.BlockSpec((step, cols - 128), lambda i: (i, 0)),
            pl.BlockSpec((step, 128), lambda i: (i, 0)),
        ],
        out_shape=[
            jax.ShapeDtypeStruct((rows, cols - 128), BF),
            jax.ShapeDtypeStruct((rows, 128), BF),
        ],
        compiler_params=pltpu.CompilerParams(vmem_limit_bytes=VMEM_LIMIT),
        cost_estimate=pl.CostEstimate(
            flops=2 * rows * depth * cols,
            bytes_accessed=2 * (rows * depth + depth * cols + rows * cols) + 8 * rows * 128,
            transcendentals=0,
        ),
        name="project",
    )(normed, weight, cosine, sine)


def mask_bias(kpos_ref, row_ref):
    row = row_ref[0]
    place, floor = row[0:1, :], row[1:2, :]
    kpos = kpos_ref[...]
    allowed = (kpos <= place) & (kpos >= floor)
    return jnp.where(allowed, 0.0, -1e30).astype(F32)


def attend_kernel(count, kpos_ref, row_ref, q_ref, *refs):
    kv_refs, (mixed_ref, lse_ref, bias_ref) = refs[:count], refs[count:]
    rows = 256
    kv = jnp.concatenate([ref[...].reshape(rows, 128) for ref in kv_refs], axis=0)
    keys = kv[:, :HEAD_DIM]
    values_t = kv.T[HEAD_DIM:, :]
    bias_ref[...] = mask_bias(kpos_ref, row_ref)
    queries = q_ref[...].reshape(rows, q_ref.shape[-1])
    parts = []
    sums = []
    for head in range(queries.shape[1] // HEAD_DIM):
        q_head = queries[:, head * HEAD_DIM : (head + 1) * HEAD_DIM]
        scores = dot_last(keys, q_head) + bias_ref[...]
        peak = jnp.max(scores, axis=0, keepdims=True)
        expon = jnp.exp(scores - peak)
        total = jnp.sum(expon, axis=0, keepdims=True)
        mixed = dot_plain(values_t, expon.astype(BF)) * (1.0 / total)
        parts.append(mixed)
        sums.append(peak + jnp.log(total))
    mixed_t = jnp.concatenate(parts, axis=0)
    mixed_ref[...] = mixed_t.T.astype(BF).reshape(mixed_ref.shape)
    lse_ref[0] = jnp.concatenate(sums, axis=0)


def attend(kpos, rowinfo, queries, kvs):
    half, micro, rows, cols = queries.shape
    heads = cols // HEAD_DIM
    span = kpos.shape[0]
    tokens = half * rows
    kv_spec = pl.BlockSpec((half, 1, rows, 128), lambda i: (0, i, 0, 0))
    q_spec = pl.BlockSpec((half, 1, rows, cols), lambda i: (0, i, 0, 0))
    return pl.pallas_call(
        functools.partial(attend_kernel, len(kvs)),
        grid=(micro,),
        in_specs=[
            pl.BlockSpec((span, 1), lambda i: (0, 0)),
            pl.BlockSpec((1, 2, tokens), lambda i: (i, 0, 0)),
            q_spec,
        ]
        + [kv_spec] * len(kvs),
        out_specs=[q_spec, pl.BlockSpec((1, heads, tokens), lambda i: (i, 0, 0))],
        out_shape=[
            jax.ShapeDtypeStruct(queries.shape, BF),
            jax.ShapeDtypeStruct((micro, heads, tokens), F32),
        ],
        scratch_shapes=[pltpu.VMEM((span, tokens), F32)],
        compiler_params=pltpu.CompilerParams(vmem_limit_bytes=VMEM_LIMIT),
        cost_estimate=pl.CostEstimate(
            flops=16 * micro * heads * tokens * span * HEAD_DIM,
            bytes_accessed=4 * micro * tokens * cols,
            transcendentals=micro * heads * tokens * span,
        ),
        name="attend",
    )(kpos, rowinfo, queries, *kvs)


def attend_back_kernel(
    count, kpos_ref, row_ref, cos_ref, sin_ref, q_ref, go_ref, lse_ref, *refs
):
    kv_refs = refs[:count]
    dq_ref = refs[count]
    dkv_refs = refs[count + 1 : 2 * count + 1]
    bias_ref, dk_ref, dv_ref = refs[2 * count + 1 :]
    rows = 256
    kv = jnp.concatenate([ref[...].reshape(rows, 128) for ref in kv_refs], axis=0)
    keys = kv[:, :HEAD_DIM]
    values = kv[:, HEAD_DIM:]
    keys_t = kv.T[:HEAD_DIM, :]
    bias_ref[...] = mask_bias(kpos_ref, row_ref)
    queries = q_ref[...].reshape(rows, q_ref.shape[-1])
    grads = go_ref[...].reshape(rows, q_ref.shape[-1])
    parts = []
    for head in range(queries.shape[1] // HEAD_DIM):
        q_head = queries[:, head * HEAD_DIM : (head + 1) * HEAD_DIM]
        g_head = grads[:, head * HEAD_DIM : (head + 1) * HEAD_DIM]
        scores = dot_last(keys, q_head) + bias_ref[...]
        probs = jnp.exp(scores - lse_ref[0, head : head + 1, :])
        grad_probs = dot_last(values, g_head)
        inner = jnp.sum(probs * grad_probs, axis=0, keepdims=True)
        grad_scores = (probs * (grad_probs - inner)).astype(BF)
        grad_values = dot_plain(probs.astype(BF), g_head)
        grad_keys = dot_plain(grad_scores, q_head)
        if head == 0:
            dv_ref[...] = grad_values
            dk_ref[...] = grad_keys
        else:
            dv_ref[...] += grad_values
            dk_ref[...] += grad_keys
        parts.append(dot_plain(keys_t, grad_scores))
    grad_queries = jnp.concatenate(parts, axis=0).T * HEAD_DIM ** (-0.5)
    cosine = cos_ref[...].reshape(rows, 128)
    sine = sin_ref[...].reshape(rows, 128)
    dq_ref[...] = turn(grad_queries, cosine, sine, True).astype(BF).reshape(dq_ref.shape)
    both = jnp.concatenate([dk_ref[...], dv_ref[...]], axis=1)
    for place, ref in enumerate(dkv_refs):
        ref[...] = both[place * rows : (place + 1) * rows].astype(ref.dtype).reshape(ref.shape)


def attend_back(kpos, rowinfo, cosine, sine, queries, grads, lse, kvs):
    half, micro, rows, cols = queries.shape
    heads = cols // HEAD_DIM
    span = kpos.shape[0]
    tokens = half * rows
    kv_spec = pl.BlockSpec((half, 1, rows, 128), lambda i: (0, i, 0, 0))
    q_spec = pl.BlockSpec((half, 1, rows, cols), lambda i: (0, i, 0, 0))
    return pl.pallas_call(
        functools.partial(attend_back_kernel, len(kvs)),
        grid=(micro,),
        in_specs=[
            pl.BlockSpec((span, 1), lambda i: (0, 0)),
            pl.BlockSpec((1, 2, tokens), lambda i: (i, 0, 0)),
            kv_spec,
            kv_spec,
            q_spec,
            q_spec,
            pl.BlockSpec((1, heads, tokens), lambda i: (i, 0, 0)),
        ]
        + [kv_spec] * len(kvs),
        out_specs=[q_spec] + [kv_spec] * len(kvs),
        out_shape=[jax.ShapeDtypeStruct(queries.shape, BF)]
        + [
            jax.ShapeDtypeStruct((half, micro, rows, 128), F32 if place == 0 else BF)
            for place in range(len(kvs))
        ],
        scratch_shapes=[
            pltpu.VMEM((span, tokens), F32),
            pltpu.VMEM((span, HEAD_DIM), F32),
            pltpu.VMEM((span, HEAD_DIM), F32),
        ],
        compiler_params=pltpu.CompilerParams(vmem_limit_bytes=VMEM_LIMIT),
        cost_estimate=pl.CostEstimate(
            flops=40 * micro * heads * tokens * span * HEAD_DIM,
            bytes_accessed=8 * micro * tokens * cols,
            transcendentals=micro * heads * tokens * span,
        ),
        name="attend_back",
    )(kpos, rowinfo, cosine, sine, queries, grads, lse, *kvs)


def body(
    tokens,
    doc_position,
    attn_gain,
    w_query,
    w_key,
    w_value,
    w_out,
    ffn_gain,
    w_gate,
    w_up,
    w_down,
    cotangent,
):
    size = lax.axis_size("dp")
    chips = size // 2
    bits = [1 << place for place in range(chips.bit_length() - 1)]
    me = lax.axis_index("dp")
    core = me % 2
    chip = me // 2
    micro, stretch, width = tokens.shape
    count = micro * stretch
    block = width // chips

    late_first = bits[::-1]
    span_chips = SEQ_LEN // (2 * stretch)
    in_span = chip % span_chips

    keys_order = [0]
    for bit in late_first:
        keys_order = keys_order + [key | bit for key in keys_order]

    def rearranged(array):
        return jnp.concatenate(
            [
                lax.dynamic_slice_in_dim(array, (chip ^ key) * block, block, array.ndim - 1)
                for key in keys_order
            ],
            axis=-1,
        )

    def restored(array):
        where = [keys_order.index(key) for key in range(chips)]
        places = jnp.array(where, jnp.int32)
        return jnp.concatenate(
            [
                lax.dynamic_slice_in_dim(
                    array, places[chip ^ natural] * block, block, array.ndim - 1
                )
                for natural in range(chips)
            ],
            axis=-1,
        )

    def split_core(weight):
        half = weight.shape[1] // 2
        first, second = weight[:, :half], weight[:, half:]
        mine = jnp.where(core == 0, first, second)
        other = jnp.where(core == 0, second, first)
        return mine, other

    def joined_core(mine, came):
        return jnp.where(
            core == 0,
            jnp.concatenate([mine, came], axis=0),
            jnp.concatenate([came, mine], axis=0),
        )

    def interleaved(arrays):
        return jnp.concatenate(
            [
                w[:, side * (w.shape[1] // 2) : (side + 1) * (w.shape[1] // 2)]
                for side in range(2)
                for w in arrays
            ],
            axis=1,
        )

    attn_pack = interleaved((w_query, w_key, w_value, w_out.T))
    own_block = block // 2
    gain_pack = jnp.zeros((16, 128), BF).at[0, :own_block].set(attn_gain)
    gain_pack = gain_pack.at[1, :own_block].set(ffn_gain)
    hidden = rearranged(tokens.reshape(count, width))
    grad_final = rearranged(cotangent.reshape(count, width))
    places = {key: place for place, key in enumerate(keys_order)}
    early = [bits[0]] + late_first[:-1]
    gains_all, attn_w, gate_w, up_w, down_wt, hidden_both, grad_final_both = gather_all(
        chips,
        late_first,
        places,
        (gain_pack, attn_pack, w_gate, w_up, w_down.T),
        (1, 2, 2, 2, 2),
        (early, early, late_first, late_first, late_first),
        hidden,
        grad_final,
    )
    gains = gains_all.reshape(chips, 2, 16, 128)[:, :, :2, :own_block]
    gains = gains.transpose(2, 0, 1, 3).reshape(2, width).astype(F32)
    gain_one, gain_two = gains[0:1], gains[1:2]

    hidden_both_f = hidden_both.astype(F32)
    ratio_both = lax.rsqrt(
        jnp.mean(hidden_both_f * hidden_both_f, axis=-1, keepdims=True) + epsilon
    )
    normed = (hidden_both_f * ratio_both * gain_one).astype(BF)
    hidden_f = hidden.astype(F32)
    ratio_one = ratio_both[:count]
    position_both = jnp.stack([doc_position, swap_core(doc_position)])

    power = jnp.arange(HEAD_DIM // 2, dtype=F32) * (2.0 / HEAD_DIM)
    inverse = 10000.0 ** (-power)
    turned = position_both.reshape(2 * count).astype(F32)[:, None] * jnp.tile(inverse, 4)[None, :]
    cosine, sine = jnp.cos(turned), jnp.sin(turned)

    inner = jnp.arange(2 * stretch, dtype=jnp.int32) ^ (core * stretch)
    row_place = in_span * (2 * stretch) + inner
    kpos = jnp.concatenate(
        [(in_span ^ key) * (2 * stretch) + inner for key in range(span_chips)]
    ).reshape(-1, 1)
    row_position = position_both.transpose(1, 0, 2).reshape(micro, 2 * stretch)
    row_places = jnp.broadcast_to(row_place[None, :], row_position.shape)
    rowinfo = jnp.stack([row_places, row_places - row_position], axis=1)

    n_q = w_query.shape[1] // 2
    n_kv = w_key.shape[1] // 2
    qkv_w = attn_w[:, : n_q + 2 * n_kv]
    out_wt = attn_w[:, n_q + 2 * n_kv :]
    queries, kv_own = project(normed, qkv_w, cosine, sine)
    kv_shape = (2, micro, stretch, 2 * n_kv)
    kvs = [kv_own.reshape(kv_shape)] + [
        swap_chip(kv_own, key).reshape(kv_shape) for key in range(1, span_chips)
    ]
    queries = queries.reshape(2, micro, stretch, n_q)
    mixed, lse = attend(kpos, rowinfo, queries, kvs)
    mixed = mixed.reshape(2 * count, n_q)

    def summed(partial):
        partial = partial.astype(BF)
        mine = (partial[:count].astype(F32) + swap_core(partial[count:]).astype(F32)).astype(BF)
        return mine.astype(F32) + swap_tensor(mine).astype(F32)

    attended = summed(dot_last(mixed, out_wt))
    middle = hidden_f + attended
    ratio_two = lax.rsqrt(jnp.mean(middle * middle, axis=-1, keepdims=True) + epsilon)
    normed_two_own = (middle * ratio_two * gain_two).astype(BF)
    normed_two = jnp.concatenate([normed_two_own, swap_core(normed_two_own)], axis=0)

    gate = dot_plain(normed_two, gate_w)
    upward = dot_plain(normed_two, up_w)
    sigmoid = jax.nn.sigmoid(gate)
    silu = gate * sigmoid
    activated = (silu * upward).astype(BF)

    def weight_grad(left, right, order):
        first = order[-1]
        top = [place for place, key in enumerate(keys_order) if key & first]
        half = chips // 2
        assert top == list(range(half, chips))
        sent = dot_first(left[:, half * block :], right).astype(BF)
        kept = dot_first(left[:, : half * block], right)
        blocks = {}
        for place in range(half):
            blocks[keys_order[place]] = kept[place * block : (place + 1) * block]
            blocks[keys_order[place + half]] = sent[place * block : (place + 1) * block]
        return scatter_blocks(blocks, order)

    def unsplit_core(total):
        half = block // 2
        mine = jnp.where(core == 0, total[:half], total[half:])
        other = jnp.where(core == 0, total[half:], total[:half])
        came = swap_core(other)
        return mine, came

    def columns(mine, came):
        return jnp.where(
            core == 0,
            jnp.concatenate([mine, came], axis=1),
            jnp.concatenate([came, mine], axis=1),
        )

    grad_down = weight_grad(grad_final_both, activated, late_first)
    feed = summed(dot_last(activated, down_wt))
    output = restored((middle + feed).astype(BF))

    grad_act = dot_plain(grad_final_both, down_wt)
    grad_gate_low = (grad_act * upward * sigmoid * (1.0 + gate * (1.0 - sigmoid))).astype(BF)
    grad_up_low = (grad_act * silu).astype(BF)
    grad_normed_two = summed(dot_last(grad_gate_low, gate_w) + dot_last(grad_up_low, up_w))
    grad_gate = weight_grad(normed_two, grad_gate_low, late_first)
    grad_up = weight_grad(normed_two, grad_up_low, late_first)
    grad_mid_norm, grad_gain_two = norm_back(grad_normed_two, middle, ratio_two, gain_two)
    grad_middle = grad_final.astype(F32) + grad_mid_norm
    grad_middle_low = grad_middle.astype(BF)
    grad_middle_both = jnp.concatenate([grad_middle_low, swap_core(grad_middle_low)], axis=0)

    grad_mixed = dot_plain(grad_middle_both, out_wt).astype(BF)
    results = attend_back(
        kpos,
        rowinfo,
        cosine.reshape(2, micro, stretch, 128),
        sine.reshape(2, micro, stretch, 128),
        queries,
        grad_mixed.reshape(queries.shape),
        lse,
        kvs,
    )
    grad_query_raw = results[0].reshape(2 * count, n_q)
    grad_kv = results[1].reshape(2 * count, 2 * n_kv)
    for key in range(1, span_chips):
        grad_kv = grad_kv + swap_chip(results[1 + key].reshape(2 * count, 2 * n_kv), key).astype(
            F32
        )
    grad_k, grad_v = grad_kv[:, :n_kv], grad_kv[:, n_kv:]
    half_dim = HEAD_DIM // 2
    cos_h, sin_h = cosine[:, :half_dim], sine[:, :half_dim]
    first_half, second_half = grad_k[:, :half_dim], grad_k[:, half_dim:]
    grad_raw = jnp.concatenate(
        [
            grad_query_raw,
            (first_half * cos_h + second_half * sin_h).astype(BF),
            (second_half * cos_h - first_half * sin_h).astype(BF),
            grad_v.astype(BF),
        ],
        axis=1,
    )
    grad_out_t = weight_grad(grad_middle_both, mixed, late_first)
    grad_qkv = weight_grad(normed, grad_raw, late_first)
    grad_normed = summed(dot_last(grad_raw, qkv_w))
    grad_in_norm, grad_gain_one = norm_back(grad_normed, hidden_f, ratio_one, gain_one)
    grad_tokens = restored(grad_middle + grad_in_norm)

    grad_gains = restored(jnp.stack([grad_gain_one, grad_gain_two]))
    grad_gains = lax.psum_scatter(grad_gains, "dp", scatter_dimension=1, tiled=True)

    def split_cols(pair, start, stop):
        return columns(pair[0][:, start:stop], pair[1][:, start:stop])

    pair = unsplit_core(grad_qkv)
    grad_w_query = split_cols(pair, 0, n_q)
    grad_w_key = split_cols(pair, n_q, n_q + n_kv)
    grad_w_value = split_cols(pair, n_q + n_kv, n_q + 2 * n_kv)
    grad_w_out = columns(*unsplit_core(grad_out_t)).T
    grad_w_gate = columns(*unsplit_core(grad_gate))
    grad_w_up = columns(*unsplit_core(grad_up))
    grad_w_down = columns(*unsplit_core(grad_down)).T
    return (
        output.reshape(tokens.shape),
        grad_tokens.reshape(tokens.shape),
        grad_gains[0],
        grad_w_query,
        grad_w_key,
        grad_w_value,
        grad_w_out,
        grad_gains[1],
        grad_w_gate,
        grad_w_up,
        grad_w_down,
    )


def solution(mesh):
    return jax.shard_map(
        body,
        mesh=mesh,
        in_specs=(
            P(None, "dp", None),
            P(None, "dp"),
            P("dp"),
            P("dp", "tensor"),
            P("dp", "tensor"),
            P("dp", "tensor"),
            P("tensor", "dp"),
            P("dp"),
            P("dp", "tensor"),
            P("dp", "tensor"),
            P("tensor", "dp"),
            P(None, "dp", None),
        ),
        out_specs=(
            P(None, "dp", None),
            P(None, "dp", None),
            P("dp"),
            P("dp", "tensor"),
            P("dp", "tensor"),
            P("dp", "tensor"),
            P("tensor", "dp"),
            P("dp"),
            P("dp", "tensor"),
            P("dp", "tensor"),
            P("tensor", "dp"),
        ),
        check_vma=False,
    )
```

```python
import functools

import jax
import jax.numpy as jnp
from jax import lax
from jax.experimental import pallas as pl
from jax.experimental.pallas import tpu as pltpu
from jax.sharding import PartitionSpec as P

HEAD_DIM = 64
SEQ_LEN = 1024
BF = jnp.bfloat16
F32 = jnp.float32
epsilon = 1e-05
VMEM_LIMIT = 48 * 1024 * 1024
VMEM_BIG = 62 * 1024 * 1024


LOW = 2


def swap_core(block):
    size = lax.axis_size("dp")
    return lax.ppermute(block, "dp", [(i, i ^ 1) for i in range(size)])


def swap_chip(block, distance):
    size = lax.axis_size("dp")
    return lax.ppermute(block, "dp", [(i, i ^ (2 * distance)) for i in range(size)])


def flipped(index, distance):
    return index + distance * (1 - 2 * ((index // distance) % 2))


def peer(distance=0, core=False, tensor=False):
    place = lax.axis_index("dp")
    bit = 1
    while bit <= distance:
        if distance & bit:
            place = flipped(place, 2 * bit)
        bit *= 2
    if core:
        place = flipped(place, 1)
    half = lax.axis_index("tensor")
    if tensor:
        half = 1 - half
    return (place, half)


def greet(peers):
    barrier = pltpu.get_barrier_semaphore()
    for device in peers:
        pl.semaphore_signal(barrier, inc=1, device_id=device, device_id_type=pl.DeviceIdType.MESH)
    pl.semaphore_wait(barrier, len(peers))


class Links:
    def __init__(self, send, recv, local):
        self.send, self.recv, self.local = send, recv, local
        self.used = 0
        self.used_local = 0
        self.sent = []

    def push(self, src, dst, device):
        copy = pltpu.make_async_remote_copy(
            src_ref=src,
            dst_ref=dst,
            send_sem=self.send.at[self.used],
            recv_sem=self.recv.at[self.used],
            device_id=device,
            device_id_type=pl.DeviceIdType.MESH,
        )
        self.used += 1
        copy.start()
        self.sent.append(copy)
        return copy

    def copy(self, src, dst):
        copy = pltpu.make_async_copy(src, dst, self.local.at[self.used_local])
        self.used_local += 1
        copy.start()
        return copy

    def close(self):
        for copy in self.sent:
            copy.wait_send()


def link_scratch(copies, locals_):
    return [
        pltpu.SemaphoreType.DMA((copies,)),
        pltpu.SemaphoreType.DMA((copies,)),
        pltpu.SemaphoreType.DMA((locals_,)),
    ]


def low_bit():
    return (lax.axis_index("dp") // (2 * LOW)) % 2


def core_bit():
    return lax.axis_index("dp") % 2


def group_rows(height, low, core):
    return pl.ds(pl.multiple_of((low * 2 + core) * height, height), height)


class Spread:
    def __init__(self, links, src, column, dst, height, start, cols, far):
        self.links, self.src, self.column, self.dst = links, src, column, dst
        self.height, self.start, self.cols, self.far = height, start, cols, far
        self.level = 0

    def begin(self):
        low, core = low_bit(), core_bit()
        mine = self.dst.at[group_rows(self.height, low, core), pl.ds(self.start, self.cols)]

        def part(low, core):
            return self.src.at[:, pl.ds(pl.multiple_of(self.column(low, core), 128), self.cols)]

        self.local = self.links.copy(part(low, core), mine)
        self.stage = [
            self.links.push(part(1 - low, core), mine, peer(LOW)),
            self.links.push(part(1 - low, 1 - core), mine, peer(LOW, core=True)),
            self.links.push(part(low, 1 - core), mine, peer(core=True)),
        ]

    def step(self):
        for copy in self.stage:
            copy.wait_recv()
        if self.level == 0:
            self.local.wait()
        self.stage = []
        if self.level < len(self.far):
            unit = 4 * self.height * 2**self.level
            columns = pl.ds(self.start, self.cols)
            self.stage.append(
                self.links.push(
                    self.dst.at[pl.ds(0, unit), columns],
                    self.dst.at[pl.ds(unit, unit), columns],
                    peer(self.far[self.level]),
                )
            )
        self.level += 1


class Ticks:
    def __init__(self, spreads, levels):
        self.spreads, self.levels, self.now, self.begun = spreads, levels, 0, 0
        self.begin(2)

    def begin(self, upto):
        while self.begun < min(upto, len(self.spreads)):
            self.spreads[self.begun].begin()
            self.begun += 1

    def tick(self):
        self.begin(self.now + 3)
        for level in range(self.levels):
            if 0 <= self.now - level < len(self.spreads):
                self.spreads[self.now - level].step()
        self.now += 1

    def rest(self):
        while self.now < len(self.spreads) + self.levels - 1:
            self.tick()


class TokenSpread:
    def __init__(self, links, whole, count):
        self.links, self.whole, self.count = links, whole, count

    def rows(self, slot, half=None):
        if half is None:
            return self.whole.at[pl.ds(slot * self.count, self.count)]
        size = self.count // 2
        return self.whole.at[pl.ds(pl.multiple_of(slot * self.count + half * size, size), size)]

    def begin(self):
        half = lax.axis_index("tensor")
        self.side = self.links.push(self.rows(0), self.rows(1), peer(core=True))
        self.low = self.links.push(self.rows(0, half), self.rows(2, half), peer(LOW))

    def second(self):
        half = lax.axis_index("tensor")
        self.low.wait_recv()
        self.across = self.links.push(self.rows(2, half), self.rows(2, half), peer(tensor=True))
        self.first = self.links.push(self.rows(2, half), self.rows(3, half), peer(core=True))

    def third(self):
        other = 1 - lax.axis_index("tensor")
        self.across.wait_recv()
        self.last = self.links.push(self.rows(2, other), self.rows(3, other), peer(core=True))

    def wait(self):
        self.side.wait_recv()
        self.first.wait_recv()
        self.last.wait_recv()


def cuts(start, tiles, parts):
    edges = [start + tiles * part // parts * 128 for part in range(parts + 1)]
    return [(edges[i], edges[i + 1] - edges[i]) for i in range(parts)]


def by_rows(start, total, step, work):
    def go(i, carry):
        work(pl.multiple_of(start + i * step, step))
        return carry

    lax.fori_loop(0, total // step, go, 0)


ANY = pl.BlockSpec(memory_space=pl.ANY)
VMEM = pl.BlockSpec(memory_space=pltpu.VMEM)


def dot_plain(left, right):
    return jnp.dot(left, right, preferred_element_type=F32)


def dot_first(left, right):
    return lax.dot_general(left, right, (((0,), (0,)), ((), ())), preferred_element_type=F32)


def dot_last(left, right):
    return lax.dot_general(left, right, (((1,), (1,)), ((), ())), preferred_element_type=F32)


def norm_back(grad, value, ratio, gain):
    scaled = grad * gain
    inner = jnp.mean(scaled * value, axis=-1, keepdims=True)
    return (ratio * scaled - value * ratio**3 * inner, jnp.sum(grad * value * ratio, axis=0))


def turn(value, cosine, sine, back):
    tiles = []
    lane = lax.broadcasted_iota(jnp.int32, (value.shape[0], 128), 1)
    first = (lane % 64) < 32
    for start in range(0, value.shape[1], 128):
        tile = value[:, start : start + 128]
        up = pltpu.roll(tile, 96, 1)
        down = pltpu.roll(tile, 32, 1)
        if back:
            other = jnp.where(first, up, -down)
        else:
            other = jnp.where(first, -up, down)
        tiles.append(tile * cosine + other * sine)
    return tiles[0] if len(tiles) == 1 else jnp.concatenate(tiles, axis=1)


def project_kernel(n_ref, w_ref, cos_ref, sin_ref, q_ref, kv_ref):
    raw = jnp.dot(n_ref[...], w_ref[...], preferred_element_type=F32)
    heads = raw.shape[1] - 128
    cosine, sine = cos_ref[...], sin_ref[...]
    q_ref[...] = (turn(raw[:, :heads], cosine, sine, False) * HEAD_DIM ** (-0.5)).astype(BF)
    both = raw[:, heads:]
    turned = turn(both, cosine, sine, False)
    lane = lax.broadcasted_iota(jnp.int32, both.shape, 1)
    kv_ref[...] = jnp.where(lane < HEAD_DIM, turned, both).astype(BF)


def project(normed, weight, cosine, sine):
    rows, depth = normed.shape
    cols = weight.shape[1]
    step = 256
    return pl.pallas_call(
        project_kernel,
        grid=(rows // step,),
        in_specs=[
            pl.BlockSpec((step, depth), lambda i: (i, 0)),
            pl.BlockSpec((depth, cols), lambda i: (0, 0)),
            pl.BlockSpec((step, 128), lambda i: (i, 0)),
            pl.BlockSpec((step, 128), lambda i: (i, 0)),
        ],
        out_specs=[
            pl.BlockSpec((step, cols - 128), lambda i: (i, 0)),
            pl.BlockSpec((step, 128), lambda i: (i, 0)),
        ],
        out_shape=[
            jax.ShapeDtypeStruct((rows, cols - 128), BF),
            jax.ShapeDtypeStruct((rows, 128), BF),
        ],
        compiler_params=pltpu.CompilerParams(vmem_limit_bytes=VMEM_LIMIT),
        cost_estimate=pl.CostEstimate(
            flops=2 * rows * depth * cols,
            bytes_accessed=2 * (rows * depth + depth * cols + rows * cols) + 8 * rows * 128,
            transcendentals=0,
        ),
        name="project",
    )(normed, weight, cosine, sine)


def mask_bias(kpos_ref, row_ref):
    row = row_ref[0]
    place, floor = row[0:1, :], row[1:2, :]
    kpos = kpos_ref[...]
    allowed = (kpos <= place) & (kpos >= floor)
    return jnp.where(allowed, 0.0, -1e30).astype(F32)


def attend_kernel(count, kpos_ref, row_ref, q_ref, *refs):
    kv_refs, (mixed_ref, lse_ref, bias_ref) = refs[:count], refs[count:]
    rows = 256
    kv = jnp.concatenate([ref[...].reshape(rows, 128) for ref in kv_refs], axis=0)
    keys = kv[:, :HEAD_DIM]
    values_t = kv.T[HEAD_DIM:, :]
    bias_ref[...] = mask_bias(kpos_ref, row_ref)
    queries = q_ref[...].reshape(rows, q_ref.shape[-1])
    parts = []
    sums = []
    for head in range(queries.shape[1] // HEAD_DIM):
        q_head = queries[:, head * HEAD_DIM : (head + 1) * HEAD_DIM]
        scores = dot_last(keys, q_head) + bias_ref[...]
        peak = jnp.max(scores, axis=0, keepdims=True)
        expon = jnp.exp(scores - peak)
        total = jnp.sum(expon, axis=0, keepdims=True)
        mixed = dot_plain(values_t, expon.astype(BF)) * (1.0 / total)
        parts.append(mixed)
        sums.append(peak + jnp.log(total))
    mixed_t = jnp.concatenate(parts, axis=0)
    mixed_ref[...] = mixed_t.T.astype(BF).reshape(mixed_ref.shape)
    lse_ref[0] = jnp.concatenate(sums, axis=0)


def attend(kpos, rowinfo, queries, kvs):
    half, micro, rows, cols = queries.shape
    heads = cols // HEAD_DIM
    span = kpos.shape[0]
    tokens = half * rows
    kv_spec = pl.BlockSpec((half, 1, rows, 128), lambda i: (0, i, 0, 0))
    q_spec = pl.BlockSpec((half, 1, rows, cols), lambda i: (0, i, 0, 0))
    return pl.pallas_call(
        functools.partial(attend_kernel, len(kvs)),
        grid=(micro,),
        in_specs=[
            pl.BlockSpec((span, 1), lambda i: (0, 0)),
            pl.BlockSpec((1, 2, tokens), lambda i: (i, 0, 0)),
            q_spec,
        ]
        + [kv_spec] * len(kvs),
        out_specs=[q_spec, pl.BlockSpec((1, heads, tokens), lambda i: (i, 0, 0))],
        out_shape=[
            jax.ShapeDtypeStruct(queries.shape, BF),
            jax.ShapeDtypeStruct((micro, heads, tokens), F32),
        ],
        scratch_shapes=[pltpu.VMEM((span, tokens), F32)],
        compiler_params=pltpu.CompilerParams(vmem_limit_bytes=VMEM_LIMIT),
        cost_estimate=pl.CostEstimate(
            flops=16 * micro * heads * tokens * span * HEAD_DIM,
            bytes_accessed=4 * micro * tokens * cols,
            transcendentals=micro * heads * tokens * span,
        ),
        name="attend",
    )(kpos, rowinfo, queries, *kvs)


def attend_back_kernel(
    count, kpos_ref, row_ref, cos_ref, sin_ref, q_ref, go_ref, lse_ref, *refs
):
    kv_refs = refs[:count]
    dq_ref = refs[count]
    dkv_refs = refs[count + 1 : 2 * count + 1]
    bias_ref, dk_ref, dv_ref = refs[2 * count + 1 :]
    rows = 256
    kv = jnp.concatenate([ref[...].reshape(rows, 128) for ref in kv_refs], axis=0)
    keys = kv[:, :HEAD_DIM]
    values = kv[:, HEAD_DIM:]
    keys_t = kv.T[:HEAD_DIM, :]
    bias_ref[...] = mask_bias(kpos_ref, row_ref)
    queries = q_ref[...].reshape(rows, q_ref.shape[-1])
    grads = go_ref[...].reshape(rows, q_ref.shape[-1])
    parts = []
    for head in range(queries.shape[1] // HEAD_DIM):
        q_head = queries[:, head * HEAD_DIM : (head + 1) * HEAD_DIM]
        g_head = grads[:, head * HEAD_DIM : (head + 1) * HEAD_DIM]
        scores = dot_last(keys, q_head) + bias_ref[...]
        probs = jnp.exp(scores - lse_ref[0, head : head + 1, :])
        grad_probs = dot_last(values, g_head)
        inner = jnp.sum(probs * grad_probs, axis=0, keepdims=True)
        grad_scores = (probs * (grad_probs - inner)).astype(BF)
        grad_values = dot_plain(probs.astype(BF), g_head)
        grad_keys = dot_plain(grad_scores, q_head)
        if head == 0:
            dv_ref[...] = grad_values
            dk_ref[...] = grad_keys
        else:
            dv_ref[...] += grad_values
            dk_ref[...] += grad_keys
        parts.append(dot_plain(keys_t, grad_scores))
    grad_queries = jnp.concatenate(parts, axis=0).T * HEAD_DIM ** (-0.5)
    cosine = cos_ref[...].reshape(rows, 128)
    sine = sin_ref[...].reshape(rows, 128)
    dq_ref[...] = turn(grad_queries, cosine, sine, True).astype(BF).reshape(dq_ref.shape)
    both = jnp.concatenate([dk_ref[...], dv_ref[...]], axis=1)
    for place, ref in enumerate(dkv_refs):
        ref[...] = both[place * rows : (place + 1) * rows].astype(ref.dtype).reshape(ref.shape)


def attend_back(kpos, rowinfo, cosine, sine, queries, grads, lse, kvs):
    half, micro, rows, cols = queries.shape
    heads = cols // HEAD_DIM
    span = kpos.shape[0]
    tokens = half * rows
    kv_spec = pl.BlockSpec((half, 1, rows, 128), lambda i: (0, i, 0, 0))
    q_spec = pl.BlockSpec((half, 1, rows, cols), lambda i: (0, i, 0, 0))
    return pl.pallas_call(
        functools.partial(attend_back_kernel, len(kvs)),
        grid=(micro,),
        in_specs=[
            pl.BlockSpec((span, 1), lambda i: (0, 0)),
            pl.BlockSpec((1, 2, tokens), lambda i: (i, 0, 0)),
            kv_spec,
            kv_spec,
            q_spec,
            q_spec,
            pl.BlockSpec((1, heads, tokens), lambda i: (i, 0, 0)),
        ]
        + [kv_spec] * len(kvs),
        out_specs=[q_spec] + [kv_spec] * len(kvs),
        out_shape=[jax.ShapeDtypeStruct(queries.shape, BF)]
        + [
            jax.ShapeDtypeStruct((half, micro, rows, 128), F32 if place == 0 else BF)
            for place in range(len(kvs))
        ],
        scratch_shapes=[
            pltpu.VMEM((span, tokens), F32),
            pltpu.VMEM((span, HEAD_DIM), F32),
            pltpu.VMEM((span, HEAD_DIM), F32),
        ],
        compiler_params=pltpu.CompilerParams(vmem_limit_bytes=VMEM_LIMIT),
        cost_estimate=pl.CostEstimate(
            flops=40 * micro * heads * tokens * span * HEAD_DIM,
            bytes_accessed=8 * micro * tokens * cols,
            transcendentals=micro * heads * tokens * span,
        ),
        name="attend_back",
    )(kpos, rowinfo, cosine, sine, queries, grads, lse, *kvs)


def gather_kernel(far, gain_src, pack_src, hid_src, cot_src, gains, attn_w, hid, cot, *sems):
    links = Links(*sems)
    greet(
        [peer(core=True), peer(LOW), peer(LOW, core=True), peer(tensor=True)]
        + [peer(bit) for bit in far]
    )
    count = hid_src.shape[0]
    width = attn_w.shape[1]
    spreads = [
        Spread(links, gain_src, lambda low, core: 0, gains, gain_src.shape[0], 0, 128, far)
    ]
    for start, cols in cuts(0, width // 128, 3):
        spreads.append(
            Spread(
                links,
                pack_src,
                lambda low, core, start=start: core * width + start,
                attn_w,
                pack_src.shape[0],
                start,
                cols,
                far,
            )
        )
    ticks = Ticks(spreads, len(far) + 1)
    own_hid = links.copy(hid_src, hid.at[pl.ds(0, count)])
    own_cot = links.copy(cot_src, cot.at[pl.ds(0, count)])
    side = links.push(hid_src, hid.at[pl.ds(count, count)], peer(core=True))
    own_cot.wait()
    tokens = TokenSpread(links, cot, count)
    ticks.tick()
    tokens.begin()
    ticks.tick()
    ticks.tick()
    tokens.second()
    ticks.tick()
    ticks.tick()
    tokens.third()
    ticks.rest()
    tokens.wait()
    own_hid.wait()
    side.wait_recv()
    links.close()


def gather_attention(far, gain_pack, attn_pack, hidden, cotangent):
    units = 2 ** len(far)
    count, width = hidden.shape
    shapes = [
        jax.ShapeDtypeStruct((units * 4 * gain_pack.shape[0], 128), BF),
        jax.ShapeDtypeStruct((units * 4 * attn_pack.shape[0], attn_pack.shape[1] // 2), BF),
        jax.ShapeDtypeStruct((2 * count, width), BF),
        jax.ShapeDtypeStruct((4 * count, width), BF),
    ]
    return pl.pallas_call(
        functools.partial(gather_kernel, far),
        in_specs=[ANY] * 4,
        out_specs=[VMEM] * 4,
        out_shape=shapes,
        scratch_shapes=link_scratch(64, 16),
        compiler_params=pltpu.CompilerParams(
            collective_id=0, has_side_effects=True, vmem_limit_bytes=VMEM_LIMIT
        ),
        name="gather_attention",
    )(gain_pack, attn_pack, hidden, cotangent)


def silu_parts(gate, upward):
    sigmoid = 1.0 / (1.0 + jnp.exp(-gate))
    silu = gate * sigmoid
    return silu * upward, upward * sigmoid * (1.0 + gate * (1.0 - sigmoid)), silu


def ffn_forward_kernel(
    far,
    main,
    mixed,
    out_wt,
    hidden,
    gain,
    pack,
    middle,
    act,
    slope,
    n2_out,
    gu_out,
    down_out,
    gu_w,
    down_w,
    n2,
    part,
    land,
    summ,
    across,
    *sems,
):
    links = Links(*sems)
    greet(
        [peer(core=True), peer(LOW), peer(LOW, core=True), peer(tensor=True)]
        + [peer(bit) for bit in far]
    )
    height = pack.shape[0]
    count = hidden.shape[0]
    gu_cols, down_cols = gu_w.shape[1], down_w.shape[1]
    total = gu_cols + down_cols
    spreads = []
    for dst, base, parts in ((gu_w, 0, 4), (down_w, gu_cols, 2)):
        for start, cols in cuts(0, dst.shape[1] // 128, parts):
            spreads.append(
                Spread(
                    links,
                    pack,
                    lambda low, core, at=base + start: (low * 2 + core) * total + at,
                    dst,
                    height,
                    start,
                    cols,
                    far,
                )
            )
    ticks = Ticks(spreads, len(far) + 1)
    micro = 3
    rows = count // micro
    side = []
    for m in range(micro):
        span = pl.ds(m * rows, rows)
        part[span] = dot_last(mixed[pl.ds(count + m * rows, rows)], out_wt[...]).astype(BF)
        side.append(links.push(part.at[span], land.at[span], peer(core=True)))
    half = []
    for m in range(micro):
        span = pl.ds(m * rows, rows)
        own = dot_last(mixed[span], out_wt[...])
        side[m].wait_recv()
        summ[span] = (own + land[span].astype(F32)).astype(BF)
        half.append(links.push(summ.at[span], across.at[span], peer(tensor=True)))
    ticks.tick()

    def finish(start):
        span = pl.ds(start, 32)
        value = (
            hidden[span].astype(F32) + summ[span].astype(F32) + across[span].astype(F32)
        )
        middle[span] = value
        ratio = lax.rsqrt(jnp.mean(value * value, axis=-1, keepdims=True) + epsilon)
        n2[span] = (value * ratio * gain[...]).astype(BF)

    for m in range(micro):
        half[m].wait_recv()
        by_rows(m * rows, rows, 32, finish)
        if m < 2:
            ticks.tick()
    tokens = TokenSpread(links, n2, count)
    tokens.begin()
    ticks.tick()
    tokens.second()
    ticks.tick()
    tokens.third()
    ticks.tick()
    tokens.wait()
    outs = [links.copy(n2, n2_out), links.copy(gu_w, gu_out)]

    def gates(start):
        span = pl.ds(start, 256)
        raw = dot_plain(n2[span], gu_w[...])
        parts = silu_parts(raw[:, :main], raw[:, main : 2 * main])
        last = raw[:, 2 * main :]
        lane = lax.broadcasted_iota(jnp.int32, last.shape, 1)
        ends = silu_parts(last, pltpu.roll(last, 64, 1))
        for ref, base, body, end in (
            (act, 0, parts[0], ends[0]),
            (slope, 0, parts[1], ends[1]),
            (slope, main + 128, parts[2], ends[2]),
        ):
            ref[span, base : base + main] = body.astype(BF)
            ref[span, base + main : base + main + 128] = jnp.where(lane < 64, end, 0.0).astype(BF)

    by_rows(0, 2 * count, 256, gates)
    ticks.tick()
    by_rows(2 * count, 2 * count, 256, gates)
    ticks.rest()
    outs.append(links.copy(down_w, down_out))
    for copy in outs:
        copy.wait()
    links.close()


def ffn_forward(far, main, mixed, out_wt, hidden, gain, pack):
    units = 2 ** len(far)
    count, width = hidden.shape
    gu_cols, down_cols = 2 * main + 128, main + 128
    group = 4 * count
    shapes = [
        jax.ShapeDtypeStruct((count, width), F32),
        jax.ShapeDtypeStruct((group, down_cols), BF),
        jax.ShapeDtypeStruct((group, 2 * down_cols), BF),
        jax.ShapeDtypeStruct((group, width), BF),
        jax.ShapeDtypeStruct((width, gu_cols), BF),
        jax.ShapeDtypeStruct((width, down_cols), BF),
    ]
    return pl.pallas_call(
        functools.partial(ffn_forward_kernel, far, main),
        in_specs=[VMEM] * 4 + [ANY],
        out_specs=[VMEM] * 3 + [ANY] * 3,
        out_shape=shapes,
        scratch_shapes=[
            pltpu.VMEM((width, gu_cols), BF),
            pltpu.VMEM((width, down_cols), BF),
            pltpu.VMEM((group, width), BF),
            pltpu.VMEM((count, width), BF),
            pltpu.VMEM((count, width), BF),
            pltpu.VMEM((count, width), BF),
            pltpu.VMEM((count, width), BF),
        ]
        + link_scratch(64, 16),
        compiler_params=pltpu.CompilerParams(
            collective_id=1, has_side_effects=True, vmem_limit_bytes=VMEM_BIG
        ),
        name="ffn_forward",
    )(mixed, out_wt, hidden, gain, pack)


class Collect:
    TILE = 256

    def __init__(self, links, far, width, sent, came, held, came_far, total, more):
        self.links, self.far, self.half = links, far, width // 2
        self.sent, self.came, self.held, self.came_far = sent, came, held, came_far
        self.total, self.more = total, more
        self.tiles = self.half // self.TILE
        self.arrivals = {}

    def send_half(self, name, job, which=None):
        columns, left, right = job
        tiles, tile = self.tiles, self.TILE
        if which is None:
            which = [i for i in range(tiles // 2, tiles)] + [i for i in range(tiles // 2)]
        for i in which:
            rows = pl.ds(i * tile, tile)
            start = self.half + i * tile
            self.sent[rows, columns] = dot_first(left[:, start : start + tile], right[...]).astype(
                BF
            )
            self.arrivals[name, i] = self.links.push(
                self.sent.at[rows, columns], self.came.at[rows, columns], peer(self.far[-1])
            )

    def own_half(self, name, job, which):
        columns, left, right = job
        tiles, tile = self.tiles, self.TILE
        for i in which:
            rows = pl.ds(i * tile, tile)
            self.arrivals[name, i].wait_recv()
            term = dot_first(left[:, i * tile : (i + 1) * tile], right[...])
            term = term + self.came[rows, columns].astype(F32)
            if i >= tiles // 2:
                place = pl.ds((i - tiles // 2) * tile, tile)
                self.held[place, columns] = term.astype(BF)
                self.arrivals[name, "far", i - tiles // 2] = self.links.push(
                    self.held.at[place, columns],
                    self.came_far.at[place, columns],
                    peer(self.far[-2]),
                )
            else:
                self.total[rows, columns] = term

    def upper(self):
        return range(self.tiles // 2, self.tiles)

    def lower(self):
        return range(self.tiles // 2)

    def finish(self, name, job):
        columns = job[0]
        for i in self.lower():
            rows = pl.ds(i * self.TILE, self.TILE)
            self.arrivals[name, "far", i].wait_recv()
            self.total[rows, columns] = self.total[rows, columns] + self.came_far[
                rows, columns
            ].astype(F32)

    def finish_more(self):
        kept = self.half // 2
        for bit, (sent, came) in zip(self.far[-3::-1], self.more):
            kept //= 2
            sent[...] = self.total[pl.ds(kept, kept)].astype(BF)
            copy = self.links.push(sent, came, peer(bit))
            copy.wait_recv()
            self.total[pl.ds(0, kept)] = self.total[pl.ds(0, kept)] + came[...].astype(F32)


def collect_scratch(far, width, cols):
    shapes = [
        pltpu.VMEM((width // 2, cols), BF),
        pltpu.VMEM((width // 2, cols), BF),
        pltpu.VMEM((width // 4, cols), BF),
        pltpu.VMEM((width // 4, cols), BF),
    ]
    kept = width // 4
    for _ in far[2:]:
        kept //= 2
        shapes += [pltpu.VMEM((kept, cols), BF)] * 2
    return shapes


def paired(refs):
    return [(refs[i], refs[i + 1]) for i in range(0, len(refs), 2)]


def group_sum_parts(links, count, rows_of, part, land, low_part, land_low):
    step = 128
    flight = {}

    def outer(slot):
        def work(start):
            dst = pl.ds(pl.multiple_of(start - (slot // 2 + 1) * count, step), step)
            part[dst] = rows_of(start, step).astype(BF)

        by_rows(slot * count, count, step, work)
        rows = pl.ds((slot // 2) * count, count)
        flight[slot] = links.push(part.at[rows], land.at[rows], peer(core=True))

    def to_low():
        flight[3].wait_recv()

        def work(start):
            dst = pl.ds(pl.multiple_of(start - 2 * count, step), step)
            came = land[pl.ds(pl.multiple_of(start - count, step), step)].astype(F32)
            low_part[dst] = (rows_of(start, step) + came).astype(BF)

        by_rows(2 * count, count, step, work)
        flight["low"] = links.push(low_part, land_low, peer(LOW))

    def to_half(summ, across):
        flight["low"].wait_recv()
        flight[1].wait_recv()

        def work(start):
            span = pl.ds(start, step)
            value = rows_of(start, step) + land[span].astype(F32) + land_low[span].astype(F32)
            summ[span] = value.astype(BF)

        by_rows(0, count, step, work)
        flight["half"] = links.push(summ, across, peer(tensor=True))

    return outer, to_low, to_half, flight


def group_sum_scratch(count, width):
    return [
        pltpu.VMEM((2 * count, width), BF),
        pltpu.VMEM((2 * count, width), BF),
        pltpu.VMEM((count, width), BF),
        pltpu.VMEM((count, width), BF),
    ]


def ffn_backward_kernel(far, main, *refs):
    cot_in, act_in, down_in, slope_in, n2_in, gu_in = refs[:6]
    summ, across, total = refs[6:9]
    cot, act, down_w, slope, n2, gu_w = refs[9:15]
    part, land, low_part, land_low = refs[15:19]
    sent, came, held, came_far = refs[19:23]
    more = paired(refs[23:-3])
    links = Links(*refs[-3:])
    loads = [
        links.copy(src, dst)
        for src, dst in (
            (cot_in, cot),
            (act_in, act),
            (down_in, down_w),
            (slope_in, slope),
            (n2_in, n2),
            (gu_in, gu_w),
        )
    ]
    greet([peer(core=True), peer(LOW), peer(tensor=True)] + [peer(bit) for bit in far])
    group, width = cot.shape
    count = group // 4
    down_cols, gu_cols = down_w.shape[1], gu_w.shape[1]
    grads = slope.at[:, pl.ds(0, gu_cols)]
    down_job = (pl.ds(0, down_cols), cot, act)
    gu_job = (pl.ds(down_cols, gu_cols), n2, grads)
    collect = Collect(links, far, width, sent, came, held, came_far, total, more)

    loads[0].wait()
    loads[1].wait()
    collect.send_half("d", down_job)
    loads[2].wait()
    loads[3].wait()
    lane = lax.broadcasted_iota(jnp.int32, (128, 128), 1)

    def slopes(start):
        span = pl.ds(start, 128)
        grad_act = dot_plain(cot[span], down_w[...])
        gate = grad_act * slope[span, 0:down_cols].astype(F32)
        upward = grad_act * slope[span, down_cols : 2 * down_cols].astype(F32)
        slope[span, 0:main] = gate[:, :main].astype(BF)
        slope[span, main : 2 * main] = upward[:, :main].astype(BF)
        last = jnp.where(lane < 64, gate[:, main:], pltpu.roll(upward[:, main:], 64, 1))
        slope[span, 2 * main : 2 * main + 128] = last.astype(BF)

    by_rows(0, group, 128, slopes)
    loads[4].wait()
    collect.send_half("g", gu_job)

    loads[5].wait()

    def rows_of(start, size):
        return dot_last(slope[pl.ds(start, size), 0:gu_cols], gu_w[...])

    outer, to_low, to_half, flight = group_sum_parts(
        links, count, rows_of, part, land, low_part, land_low
    )
    outer(3)
    outer(1)
    to_low()
    collect.own_half("d", down_job, collect.upper())
    collect.own_half("d", down_job, collect.lower())
    to_half(summ, across)
    collect.own_half("g", gu_job, collect.upper())
    collect.own_half("g", gu_job, collect.lower())
    collect.finish("d", down_job)
    collect.finish("g", gu_job)
    collect.finish_more()
    flight["half"].wait_recv()
    links.close()


def ffn_backward(far, main, cot, act, down_w, slope, n2, gu_w):
    group, width = cot.shape
    count = group // 4
    cols = gu_w.shape[1] + down_w.shape[1]
    inputs = (cot, act, down_w, slope, n2, gu_w)
    return pl.pallas_call(
        functools.partial(ffn_backward_kernel, far, main),
        in_specs=[ANY] * 6,
        out_specs=[VMEM] * 3,
        out_shape=[
            jax.ShapeDtypeStruct((count, width), BF),
            jax.ShapeDtypeStruct((count, width), BF),
            jax.ShapeDtypeStruct((width // 4, cols), F32),
        ],
        scratch_shapes=[pltpu.VMEM(a.shape, BF) for a in inputs]
        + group_sum_scratch(count, width)
        + collect_scratch(far, width, cols)
        + link_scratch(64, 16),
        compiler_params=pltpu.CompilerParams(
            collective_id=2, has_side_effects=True, vmem_limit_bytes=VMEM_BIG
        ),
        name="ffn_backward",
    )(*inputs)


def attention_grads_kernel(far, *refs):
    n1, raw, gmid, mixed, qkv_w, act, down_w = refs[:7]
    summ, across, feed, feed_across, total = refs[7:12]
    side, land_side = refs[12:14]
    part, land, low_part, land_low = refs[14:18]
    sent, came, held, came_far = refs[18:22]
    more = paired(refs[22:-3])
    links = Links(*refs[-3:])
    greet([peer(core=True), peer(LOW), peer(tensor=True)] + [peer(bit) for bit in far])
    width = n1.shape[1]
    count = n1.shape[0] // 2
    qkv_cols, out_cols = raw.shape[1], mixed.shape[1]
    collect = Collect(links, far, width, sent, came, held, came_far, total, more)
    qkv_job = (pl.ds(0, qkv_cols), n1, raw)
    out_job = (pl.ds(qkv_cols, out_cols), gmid, mixed)
    for which in ([i for i in collect.upper()], [i for i in collect.lower()]):
        collect.send_half("o", out_job, which)
        collect.send_half("q", qkv_job, which)

    def side_rows(start):
        dst = pl.ds(pl.multiple_of(start - count, 128), 128)
        side[dst] = dot_last(raw[pl.ds(start, 128)], qkv_w[...]).astype(BF)

    by_rows(count, count, 128, side_rows)
    to_core = links.push(side, land_side, peer(core=True))

    def rows_of(start, size):
        return dot_last(act[pl.ds(start, size)], down_w[...])

    outer, to_low, to_half, flight = group_sum_parts(
        links, count, rows_of, part, land, low_part, land_low
    )
    outer(3)
    to_core.wait_recv()

    def own_rows(start):
        span = pl.ds(start, 128)
        value = dot_last(raw[span], qkv_w[...]) + land_side[span].astype(F32)
        summ[span] = value.astype(BF)

    by_rows(0, count, 128, own_rows)
    over = links.push(summ, across, peer(tensor=True))
    to_low()
    outer(1)
    for which in (collect.upper(), collect.lower()):
        collect.own_half("o", out_job, which)
        collect.own_half("q", qkv_job, which)
    to_half(feed, feed_across)
    collect.finish("o", out_job)
    collect.finish("q", qkv_job)
    collect.finish_more()
    over.wait_recv()
    flight["half"].wait_recv()
    links.close()


def attention_grads(far, n1, raw, gmid, mixed, qkv_w, act, down_w):
    both, width = n1.shape
    count = both // 2
    cols = raw.shape[1] + mixed.shape[1]
    rows = jax.ShapeDtypeStruct((count, width), BF)
    return pl.pallas_call(
        functools.partial(attention_grads_kernel, far),
        in_specs=[VMEM] * 7,
        out_specs=[VMEM] * 5,
        out_shape=[rows, rows, rows, rows, jax.ShapeDtypeStruct((width // 4, cols), F32)],
        scratch_shapes=[pltpu.VMEM((count, width), BF)] * 2
        + group_sum_scratch(count, width)
        + collect_scratch(far, width, cols)
        + link_scratch(64, 16),
        compiler_params=pltpu.CompilerParams(
            collective_id=3, has_side_effects=True, vmem_limit_bytes=VMEM_BIG
        ),
        name="attention_grads",
    )(n1, raw, gmid, mixed, qkv_w, act, down_w)


def body(
    tokens,
    doc_position,
    attn_gain,
    w_query,
    w_key,
    w_value,
    w_out,
    ffn_gain,
    w_gate,
    w_up,
    w_down,
    cotangent,
):
    size = lax.axis_size("dp")
    chips = size // 2
    far = [1 << place for place in range(chips.bit_length() - 1) if 1 << place != LOW][::-1]
    me = lax.axis_index("dp")
    core = me % 2
    chip = me // 2
    low = (chip // LOW) % 2
    micro, stretch, width = tokens.shape
    count = micro * stretch
    block = width // chips
    own_block = block // 2
    span_chips = SEQ_LEN // (2 * stretch)
    in_span = chip % span_chips

    keys = [0]
    for bit in far:
        keys = keys + [key | bit for key in keys]

    def rearranged(array):
        base = chip - LOW * low
        return jnp.concatenate(
            [
                lax.dynamic_slice_in_dim(
                    array, ((base ^ key) + LOW * side) * block, block, array.ndim - 1
                )
                for key in keys
                for side in range(2)
            ],
            axis=-1,
        )

    def restored(array):
        unit_of = jnp.array([keys.index(other & ~LOW) for other in range(chips)], jnp.int32)
        return jnp.concatenate(
            [
                lax.dynamic_slice_in_dim(
                    array,
                    (unit_of[chip ^ natural] * 2 + (natural // LOW) % 2) * block,
                    block,
                    array.ndim - 1,
                )
                for natural in range(chips)
            ],
            axis=-1,
        )

    def halves(array):
        n = array.shape[1] // 2
        return array[:, :n], array[:, n:]

    attn_pack = jnp.concatenate(
        [
            halves(w)[side]
            for side in range(2)
            for w in (w_query, w_key, w_value, w_out.T)
        ],
        axis=1,
    )
    hidden_units = w_gate.shape[1] // 4
    main = hidden_units // 128 * 128
    rest = hidden_units - main
    assert rest == 64

    def mains(array, place):
        return array[:, place * main : (place + 1) * main]

    def rests(array, place):
        return array[:, 4 * main + place * rest : 4 * main + (place + 1) * rest]

    w_down_t = w_down.T
    empty = jnp.zeros((own_block, 128 - rest), BF)
    ffn_pack = jnp.concatenate(
        [
            piece
            for place in range(4)
            for piece in (
                mains(w_gate, place),
                mains(w_up, place),
                rests(w_gate, place),
                rests(w_up, place),
                mains(w_down_t, place),
                rests(w_down_t, place),
                empty,
            )
        ],
        axis=1,
    )
    gain_pack = jnp.zeros((16, 128), BF).at[0, :own_block].set(attn_gain)
    gain_pack = gain_pack.at[1, :own_block].set(ffn_gain)
    hidden = rearranged(tokens.reshape(count, width))
    grad_final = rearranged(cotangent.reshape(count, width))

    gains, attn_w, hidden_both, grad_final_all = gather_attention(
        far, gain_pack, attn_pack, hidden, grad_final
    )
    gains = gains.reshape(2 ** len(far), 4, 16, 128)[:, :, :2, :own_block]
    gains = gains.transpose(2, 0, 1, 3).reshape(2, width).astype(F32)
    gain_one, gain_two = gains[0:1], gains[1:2]

    hidden_both_f = hidden_both.astype(F32)
    ratio_both = lax.rsqrt(
        jnp.mean(hidden_both_f * hidden_both_f, axis=-1, keepdims=True) + epsilon
    )
    normed = (hidden_both_f * ratio_both * gain_one).astype(BF)
    hidden_f = hidden.astype(F32)
    ratio_one = ratio_both[:count]
    position_both = jnp.stack([doc_position, swap_core(doc_position)])

    power = jnp.arange(HEAD_DIM // 2, dtype=F32) * (2.0 / HEAD_DIM)
    inverse = 10000.0 ** (-power)
    turned = position_both.reshape(2 * count).astype(F32)[:, None] * jnp.tile(inverse, 4)[None, :]
    cosine, sine = jnp.cos(turned), jnp.sin(turned)

    inner = jnp.arange(2 * stretch, dtype=jnp.int32) ^ (core * stretch)
    row_place = in_span * (2 * stretch) + inner
    kpos = jnp.concatenate(
        [(in_span ^ key) * (2 * stretch) + inner for key in range(span_chips)]
    ).reshape(-1, 1)
    row_position = position_both.transpose(1, 0, 2).reshape(micro, 2 * stretch)
    row_places = jnp.broadcast_to(row_place[None, :], row_position.shape)
    rowinfo = jnp.stack([row_places, row_places - row_position], axis=1)

    n_q = w_query.shape[1] // 2
    n_kv = w_key.shape[1] // 2
    n_qkv = n_q + 2 * n_kv
    qkv_w = attn_w[:, :n_qkv]
    out_wt = attn_w[:, n_qkv:]
    queries, kv_own = project(normed, qkv_w, cosine, sine)
    kv_shape = (2, micro, stretch, 2 * n_kv)
    kvs = [kv_own.reshape(kv_shape)] + [
        swap_chip(kv_own, key).reshape(kv_shape) for key in range(1, span_chips)
    ]
    queries = queries.reshape(2, micro, stretch, n_q)
    mixed, lse = attend(kpos, rowinfo, queries, kvs)
    mixed = mixed.reshape(2 * count, n_q)

    middle, activated, slopes, normed_two, gu_w, down_wt = ffn_forward(
        far, main, mixed, out_wt, hidden, gain_two, ffn_pack
    )
    grad_two, grad_two_across, ffn_grad = ffn_backward(
        far, main, grad_final_all, activated, down_wt, slopes, normed_two, gu_w
    )
    grad_normed_two = grad_two.astype(F32) + grad_two_across.astype(F32)
    ratio_two = lax.rsqrt(jnp.mean(middle * middle, axis=-1, keepdims=True) + epsilon)
    grad_mid_norm, grad_gain_two = norm_back(grad_normed_two, middle, ratio_two, gain_two)
    grad_middle = grad_final.astype(F32) + grad_mid_norm
    grad_middle_low = grad_middle.astype(BF)
    grad_middle_both = jnp.concatenate([grad_middle_low, swap_core(grad_middle_low)], axis=0)

    grad_mixed = dot_plain(grad_middle_both, out_wt).astype(BF)
    results = attend_back(
        kpos,
        rowinfo,
        cosine.reshape(2, micro, stretch, 128),
        sine.reshape(2, micro, stretch, 128),
        queries,
        grad_mixed.reshape(queries.shape),
        lse,
        kvs,
    )
    grad_query_raw = results[0].reshape(2 * count, n_q)
    grad_kv = results[1].reshape(2 * count, 2 * n_kv)
    for key in range(1, span_chips):
        grad_kv = grad_kv + swap_chip(results[1 + key].reshape(2 * count, 2 * n_kv), key).astype(
            F32
        )
    grad_k, grad_v = grad_kv[:, :n_kv], grad_kv[:, n_kv:]
    half_dim = HEAD_DIM // 2
    cos_h, sin_h = cosine[:, :half_dim], sine[:, :half_dim]
    first_half, second_half = grad_k[:, :half_dim], grad_k[:, half_dim:]
    grad_raw = jnp.concatenate(
        [
            grad_query_raw,
            (first_half * cos_h + second_half * sin_h).astype(BF),
            (second_half * cos_h - first_half * sin_h).astype(BF),
            grad_v.astype(BF),
        ],
        axis=1,
    )
    grad_one, grad_one_across, feed, feed_across, attn_grad = attention_grads(
        far, normed, grad_raw, grad_middle_both, mixed, qkv_w, activated, down_wt
    )
    output = restored((middle + (feed.astype(F32) + feed_across.astype(F32))).astype(BF))
    grad_normed = grad_one.astype(F32) + grad_one_across.astype(F32)
    grad_in_norm, grad_gain_one = norm_back(grad_normed, hidden_f, ratio_one, gain_one)
    grad_tokens = restored(grad_middle + grad_in_norm)

    grad_gains = restored(jnp.stack([grad_gain_one, grad_gain_two]))
    grad_gains = lax.psum_scatter(grad_gains, "dp", scatter_dimension=1, tiled=True)

    def picked(pair, side):
        return jnp.where(side == 0, pair[0], pair[1]), jnp.where(side == 0, pair[1], pair[0])

    attn_grad = attn_grad[: 2 * block].reshape(2, 2, own_block, -1)
    mine, other = picked(attn_grad, low)
    mine = mine + swap_chip(other.astype(BF), LOW).astype(F32)
    mine, other = picked(mine, core)
    came = swap_core(other)
    parts = picked((mine, came), core)

    def columns(start, stop):
        return jnp.concatenate([part[:, start:stop] for part in parts], axis=1)

    grad_w_query = columns(0, n_q)
    grad_w_key = columns(n_q, n_q + n_kv)
    grad_w_value = columns(n_q + n_kv, n_qkv)
    grad_w_out = columns(n_qkv, n_qkv + n_q).T

    ffn_grad = ffn_grad[: 2 * block].reshape(2, 2, own_block, -1)
    mine, other = picked(ffn_grad, low)
    came = swap_chip(other.astype(BF), LOW).astype(F32)
    by_low = jnp.stack(picked((mine, came), low))
    mine, other = picked((by_low[:, 0], by_low[:, 1]), core)
    came = swap_core(other)
    by_core = picked((mine, came), core)
    places = [by_core[place % 2][place // 2] for place in range(4)]
    down_cols = main + 128
    gu = down_cols

    def gathered(main_start, rest_start):
        return jnp.concatenate(
            [part[:, main_start : main_start + main] for part in places]
            + [part[:, rest_start : rest_start + rest] for part in places],
            axis=1,
        )

    grad_w_down = gathered(0, main).T
    grad_w_gate = gathered(gu, gu + 2 * main)
    grad_w_up = gathered(gu + main, gu + 2 * main + rest)
    return (
        output.reshape(tokens.shape),
        grad_tokens.reshape(tokens.shape),
        grad_gains[0],
        grad_w_query,
        grad_w_key,
        grad_w_value,
        grad_w_out,
        grad_gains[1],
        grad_w_gate,
        grad_w_up,
        grad_w_down,
    )


def solution(mesh):
    return jax.shard_map(
        body,
        mesh=mesh,
        in_specs=(
            P(None, "dp", None),
            P(None, "dp"),
            P("dp"),
            P("dp", "tensor"),
            P("dp", "tensor"),
            P("dp", "tensor"),
            P("tensor", "dp"),
            P("dp"),
            P("dp", "tensor"),
            P("dp", "tensor"),
            P("tensor", "dp"),
            P(None, "dp", None),
        ),
        out_specs=(
            P(None, "dp", None),
            P(None, "dp", None),
            P("dp"),
            P("dp", "tensor"),
            P("dp", "tensor"),
            P("dp", "tensor"),
            P("tensor", "dp"),
            P("dp"),
            P("dp", "tensor"),
            P("dp", "tensor"),
            P("tensor", "dp"),
        ),
        check_vma=False,
    )
```

```python
import functools

import jax
import jax.numpy as jnp
from jax import lax
from jax.experimental import pallas as pl
from jax.experimental.pallas import tpu as pltpu
from jax.sharding import PartitionSpec as P

HEAD_DIM = 64
SEQ_LEN = 1024
BF = jnp.bfloat16
F32 = jnp.float32
epsilon = 1e-05
VMEM_LIMIT = 48 * 1024 * 1024
VMEM_BIG = 62 * 1024 * 1024


LOW = 2


def swap_core(block):
    size = lax.axis_size("dp")
    return lax.ppermute(block, "dp", [(i, i ^ 1) for i in range(size)])


def swap_chip(block, distance):
    size = lax.axis_size("dp")
    return lax.ppermute(block, "dp", [(i, i ^ (2 * distance)) for i in range(size)])


def flipped(index, distance):
    return index + distance * (1 - 2 * ((index // distance) % 2))


def peer(distance=0, core=False, tensor=False):
    place = lax.axis_index("dp")
    bit = 1
    while bit <= distance:
        if distance & bit:
            place = flipped(place, 2 * bit)
        bit *= 2
    if core:
        place = flipped(place, 1)
    half = lax.axis_index("tensor")
    if tensor:
        half = 1 - half
    return (place, half)


def greet(peers):
    barrier = pltpu.get_barrier_semaphore()
    for name in sorted(set(peers)):
        pl.semaphore_signal(
            barrier, inc=1, device_id=peer(*name), device_id_type=pl.DeviceIdType.MESH
        )
    pl.semaphore_wait(barrier, len(set(peers)))


CORE = (0, True, False)
TENSOR = (0, False, True)


def chips_apart(*distances):
    return [(distance, False, False) for distance in distances]


class Links:
    def __init__(self, send, recv, local):
        self.send, self.recv, self.local = send, recv, local
        self.used = 0
        self.used_local = 0
        self.sent = []

    def push(self, src, dst, device):
        copy = pltpu.make_async_remote_copy(
            src_ref=src,
            dst_ref=dst,
            send_sem=self.send.at[self.used],
            recv_sem=self.recv.at[self.used],
            device_id=device,
            device_id_type=pl.DeviceIdType.MESH,
        )
        self.used += 1
        copy.start()
        self.sent.append(copy)
        return copy

    def copy(self, src, dst):
        copy = pltpu.make_async_copy(src, dst, self.local.at[self.used_local])
        self.used_local += 1
        copy.start()
        return copy

    def settle(self, copies):
        for copy in copies:
            copy.wait_send()
            self.sent = [other for other in self.sent if other is not copy]

    def close(self):
        for copy in self.sent:
            copy.wait_send()


def link_scratch(copies, locals_):
    return [
        pltpu.SemaphoreType.DMA((copies,)),
        pltpu.SemaphoreType.DMA((copies,)),
        pltpu.SemaphoreType.DMA((locals_,)),
    ]


def low_bit():
    return (lax.axis_index("dp") // (2 * LOW)) % 2


def core_bit():
    return lax.axis_index("dp") % 2


def group_rows(height, low, core):
    return pl.ds(pl.multiple_of((low * 2 + core) * height, height), height)


class Spread:
    def __init__(self, links, src, column, dst, height, start, cols, far):
        self.links, self.src, self.column, self.dst = links, src, column, dst
        self.height, self.start, self.cols, self.far = height, start, cols, far
        self.level = 0

    def begin(self):
        low, core = low_bit(), core_bit()
        mine = self.dst.at[group_rows(self.height, low, core), pl.ds(self.start, self.cols)]

        def part(low, core):
            return self.src.at[:, pl.ds(pl.multiple_of(self.column(low, core), 128), self.cols)]

        self.local = self.links.copy(part(low, core), mine)
        self.stage = [
            self.links.push(part(1 - low, core), mine, peer(LOW)),
            self.links.push(part(1 - low, 1 - core), mine, peer(LOW, core=True)),
            self.links.push(part(low, 1 - core), mine, peer(core=True)),
        ]

    def unit(self, index):
        size = 4 * self.height
        return self.dst.at[pl.ds(index * size, size), pl.ds(self.start, self.cols)]

    def pass_on(self, index, first):
        for level in range(first, len(self.far)):
            reached = index + 2**level
            self.arrivals[reached] = self.links.push(
                self.unit(index), self.unit(reached), peer(self.far[level])
            )

    def launch(self):
        for copy in self.stage:
            copy.wait_recv()
        self.local.wait()
        self.arrivals = {}
        self.pass_on(0, 0)

    def forward(self):
        for index in range(1, 2 ** (len(self.far) - 1)):
            self.arrivals.pop(index).wait_recv()
            self.pass_on(index, index.bit_length())

    def finish(self):
        for copy in self.arrivals.values():
            copy.wait_recv()
        self.arrivals = {}


class TokenSpread:
    def __init__(self, links, own, others):
        self.links, self.own, self.others = links, own, others
        self.count = own.shape[0]

    def rows(self, slot, half=None):
        ref = self.others if slot else self.own
        base = (slot - 1) * self.count if slot else 0
        if half is None:
            return ref.at[pl.ds(base, self.count)]
        size = self.count // 2
        return ref.at[pl.ds(pl.multiple_of(base + half * size, size), size)]

    def begin(self):
        half = lax.axis_index("tensor")
        self.side = self.links.push(self.rows(0), self.rows(1), peer(core=True))
        self.low = self.links.push(self.rows(0, half), self.rows(2, half), peer(LOW))

    def second(self):
        half = lax.axis_index("tensor")
        self.low.wait_recv()
        self.across = self.links.push(self.rows(2, half), self.rows(2, half), peer(tensor=True))
        self.first = self.links.push(self.rows(2, half), self.rows(3, half), peer(core=True))

    def third(self):
        other = 1 - lax.axis_index("tensor")
        self.across.wait_recv()
        self.last = self.links.push(self.rows(2, other), self.rows(3, other), peer(core=True))

    def wait(self):
        self.side.wait_recv()
        self.first.wait_recv()
        self.last.wait_recv()


def cuts(start, tiles, parts):
    edges = [start + tiles * part // parts * 128 for part in range(parts + 1)]
    return [(edges[i], edges[i + 1] - edges[i]) for i in range(parts)]


def by_rows(start, total, step, work):
    def go(i, carry):
        work(pl.multiple_of(start + i * step, step))
        return carry

    lax.fori_loop(0, total // step, go, 0)


ANY = pl.BlockSpec(memory_space=pl.ANY)
VMEM = pl.BlockSpec(memory_space=pltpu.VMEM)


def dot_plain(left, right):
    return jnp.dot(left, right, preferred_element_type=F32)


def dot_first(left, right):
    return lax.dot_general(left, right, (((0,), (0,)), ((), ())), preferred_element_type=F32)


def dot_last(left, right):
    return lax.dot_general(left, right, (((1,), (1,)), ((), ())), preferred_element_type=F32)


def norm_back(grad, value, ratio, gain):
    scaled = grad * gain
    inner = jnp.mean(scaled * value, axis=-1, keepdims=True)
    return ratio * scaled - value * ratio**3 * inner


def turn(value, cosine, sine, back):
    tiles = []
    lane = lax.broadcasted_iota(jnp.int32, (value.shape[0], 128), 1)
    first = (lane % 64) < 32
    for start in range(0, value.shape[1], 128):
        tile = value[:, start : start + 128]
        up = pltpu.roll(tile, 96, 1)
        down = pltpu.roll(tile, 32, 1)
        if back:
            other = jnp.where(first, up, -down)
        else:
            other = jnp.where(first, -up, down)
        tiles.append(tile * cosine + other * sine)
    return tiles[0] if len(tiles) == 1 else jnp.concatenate(tiles, axis=1)


def mask_bias(kpos, row):
    place, floor = row[0:1, :], row[1:2, :]
    allowed = (kpos <= place) & (kpos >= floor)
    return jnp.where(allowed, 0.0, -1e30).astype(F32)


def attend(bias_ref, queries, kv):
    keys = kv[:, :HEAD_DIM]
    values_t = kv.T[HEAD_DIM:, :]
    parts = []
    sums = []
    for head in range(queries.shape[1] // HEAD_DIM):
        q_head = queries[:, head * HEAD_DIM : (head + 1) * HEAD_DIM]
        scores = dot_last(keys, q_head) + bias_ref[...]
        peak = jnp.max(scores, axis=0, keepdims=True)
        expon = jnp.exp(scores - peak)
        total = jnp.sum(expon, axis=0, keepdims=True)
        parts.append(dot_plain(values_t, expon.astype(BF)) * (1.0 / total))
        sums.append(peak + jnp.log(total))
    return jnp.concatenate(parts, axis=0), jnp.concatenate(sums, axis=0)


def attend_back(bias_ref, queries, grads, lse, kv, dk_ref, dv_ref):
    keys = kv[:, :HEAD_DIM]
    values = kv[:, HEAD_DIM:]
    keys_t = kv.T[:HEAD_DIM, :]
    parts = []
    for head in range(queries.shape[1] // HEAD_DIM):
        q_head = queries[:, head * HEAD_DIM : (head + 1) * HEAD_DIM]
        g_head = grads[:, head * HEAD_DIM : (head + 1) * HEAD_DIM]
        scores = dot_last(keys, q_head) + bias_ref[...]
        probs = jnp.exp(scores - lse[head : head + 1, :])
        grad_probs = dot_last(values, g_head)
        inner = jnp.sum(probs * grad_probs, axis=0, keepdims=True)
        grad_scores = (probs * (grad_probs - inner)).astype(BF)
        grad_values = dot_plain(probs.astype(BF), g_head)
        grad_keys = dot_plain(grad_scores, q_head)
        if head == 0:
            dv_ref[...] = grad_values
            dk_ref[...] = grad_keys
        else:
            dv_ref[...] += grad_values
            dk_ref[...] += grad_keys
        parts.append(dot_plain(keys_t, grad_scores))
    return jnp.concatenate(parts, axis=0).T * HEAD_DIM ** (-0.5)


def silu_parts(gate, upward):
    sigmoid = 1.0 / (1.0 + jnp.exp(-gate))
    silu = gate * sigmoid
    return silu * upward, upward * sigmoid * (1.0 + gate * (1.0 - sigmoid)), silu


def forward_kernel(far, main, micro, *refs):
    gain_src, attn_src, ffn_src, hid_src, cot_src, cosine, sine, kpos, rowinfo = refs[:9]
    (
        gain_rows,
        lse,
        middle,
        act,
        slope,
        mixed,
        queries,
        kvs,
        n1_out,
        attn_out,
        n2_out,
        gu_out,
        down_out,
        cot_out,
    ) = refs[9:23]
    gains, attn_w, gu_w, down_w, hid, n1, n2, bias, ratios, part, land, summ, across = refs[23:36]
    links = Links(*refs[36:])
    count = hid_src.shape[0]
    rows = count // micro
    span_chips = kvs.shape[0]
    greet(
        [CORE, TENSOR, (LOW, True, False)] + chips_apart(LOW, *far) + chips_apart(*range(1, span_chips))
    )
    attn_cols, gu_cols, down_cols = attn_w.shape[1], gu_w.shape[1], down_w.shape[1]
    total = gu_cols + down_cols
    height = attn_src.shape[0]

    def core_column(start):
        return lambda low, core: core * attn_cols + start

    def group_column(start):
        return lambda low, core: (low * 2 + core) * total + start

    spreads = [
        Spread(links, gain_src, lambda low, core: 0, gains, gain_src.shape[0], 0, 128, far)
    ]
    n_q = queries.shape[1]
    n_qkv = n_q + 128
    for base, tiles, parts in ((0, n_qkv // 128, 2), (n_qkv, n_q // 128, 2)):
        for start, cols in cuts(base, tiles, parts):
            spreads.append(
                Spread(links, attn_src, core_column(start), attn_w, height, start, cols, far)
            )
        if base == 0:
            qkv_spreads = len(spreads)
    attn_spreads = len(spreads)
    for start, cols in cuts(0, gu_cols // 128, 4):
        spreads.append(Spread(links, ffn_src, group_column(start), gu_w, height, start, cols, far))
    gu_spreads = len(spreads)
    for start, cols in cuts(0, down_cols // 128, 2):
        spreads.append(
            Spread(links, ffn_src, group_column(gu_cols + start), down_w, height, start, cols, far)
        )
    attn = spreads[:attn_spreads]
    gu = spreads[attn_spreads:gu_spreads]
    down = spreads[gu_spreads:]
    for spread in attn:
        spread.begin()
    own_hid = links.copy(hid_src, hid.at[pl.ds(0, count)])
    side_hid = links.push(hid_src, hid.at[pl.ds(count, count)], peer(core=True))
    tokens = TokenSpread(links, cot_src, cot_out)
    own_hid.wait()
    side_hid.wait_recv()

    def first_ratio(start):
        span = pl.ds(start, 64)
        value = hid[span].astype(F32)
        ratio = lax.rsqrt(jnp.mean(value * value, axis=-1, keepdims=True) + epsilon)
        ratios[span] = jnp.broadcast_to(ratio, (64, 128))

    by_rows(0, 2 * count, 64, first_ratio)
    for spread in attn:
        spread.launch()
    for spread in gu[:2]:
        spread.begin()
    tokens.begin()
    spreads[0].forward()

    spreads[0].finish()
    n_units = 2 ** len(far)
    own_block = gain_rows.shape[1] // (4 * n_units)
    both_gains = gains[...].astype(F32)
    for place in range(4 * n_units):
        gain_rows[0:2, place * own_block : (place + 1) * own_block] = both_gains[
            place * 16 : place * 16 + 2, :own_block
        ]

    def first_norm(start):
        span = pl.ds(start, 64)
        n1[span] = (hid[span].astype(F32) * ratios[span, 0:1] * gain_rows[0:1]).astype(BF)

    by_rows(0, 2 * count, 64, first_norm)
    outs = [links.copy(n1, n1_out)]
    for spread in spreads[1:qkv_spreads]:
        spread.forward()
    for spread in spreads[1:qkv_spreads]:
        spread.finish()

    def project(start):
        span = pl.ds(start, 256)
        raw = dot_plain(n1[span], attn_w[:, 0:n_qkv])
        cos, sin = cosine[span], sine[span]
        queries[span] = (turn(raw[:, :n_q], cos, sin, False) * HEAD_DIM ** (-0.5)).astype(BF)
        pair = raw[:, n_q:]
        lane = lax.broadcasted_iota(jnp.int32, pair.shape, 1)
        kvs[0, span] = jnp.where(lane < HEAD_DIM, turn(pair, cos, sin, False), pair).astype(BF)

    by_rows(0, 2 * count, 256, project)
    came = [
        links.push(kvs.at[0], kvs.at[key], peer(key)) for key in range(1, span_chips)
    ]
    for spread in gu[2:] + down:
        spread.begin()
    gu[0].launch()
    spreads[qkv_spreads].forward()
    gu[1].launch()
    for copy in came:
        copy.wait_recv()

    tokens.second()
    half = []
    for m in range(micro):
        own, other = pl.ds(m * rows, rows), pl.ds(count + m * rows, rows)
        bias[...] = mask_bias(kpos[...], rowinfo[m])
        kv = jnp.concatenate(
            [kvs[key, span] for key in range(span_chips) for span in (own, other)], axis=0
        )
        q_both = jnp.concatenate([queries[own], queries[other]], axis=0)
        mixed_t, sums = attend(bias, q_both, kv)
        lse[m] = sums
        value = mixed_t.T.astype(BF)
        mixed[own] = value[:rows]
        mixed[other] = value[rows:]
        if m == 0:
            for spread in spreads[qkv_spreads + 1 : attn_spreads]:
                spread.forward()
            for spread in spreads[qkv_spreads:attn_spreads]:
                spread.finish()
            outs.append(links.copy(attn_w, attn_out))
        out_w = attn_w.at[:, pl.ds(n_qkv, n_q)]
        term = dot_last(value, out_w[...])
        part[own] = term[rows:].astype(BF)
        side = links.push(part.at[own], land.at[own], peer(core=True))
        side.wait_recv()
        summ[own] = (term[:rows] + land[own].astype(F32)).astype(BF)
        half.append(links.push(summ.at[own], across.at[own], peer(tensor=True)))
        if m == 0:
            for spread in gu[2:]:
                spread.launch()
        if m == 1:
            gu[0].forward()
    for spread in down:
        spread.launch()
    gu[1].forward()
    tokens.third()

    def finish(start):
        span = pl.ds(start, 32)
        value = hid[span].astype(F32) + summ[span].astype(F32) + across[span].astype(F32)
        middle[span] = value
        ratio = lax.rsqrt(jnp.mean(value * value, axis=-1, keepdims=True) + epsilon)
        n2[span] = (value * ratio * gain_rows[1:2]).astype(BF)

    low = []
    for m in range(micro):
        half[m].wait_recv()
        by_rows(m * rows, rows, 32, finish)
        low.append(
            links.push(
                n2.at[pl.ds(m * rows, rows)], n2.at[pl.ds(2 * count + m * rows, rows)], peer(LOW)
            )
        )
    own_n2 = links.push(n2.at[pl.ds(0, count)], n2.at[pl.ds(count, count)], peer(core=True))
    gu[2].forward()
    gu[3].forward()
    for spread in spreads[attn_spreads:gu_spreads]:
        spread.finish()

    def gates(start):
        span = pl.ds(start, 256)
        raw = dot_plain(n2[span], gu_w[...])
        parts = silu_parts(raw[:, :main], raw[:, main : 2 * main])
        last = raw[:, 2 * main :]
        lane = lax.broadcasted_iota(jnp.int32, last.shape, 1)
        ends = silu_parts(last, pltpu.roll(last, 64, 1))
        for ref, base, body, end in (
            (act, 0, parts[0], ends[0]),
            (slope, 0, parts[1], ends[1]),
            (slope, main + 128, parts[2], ends[2]),
        ):
            ref[span, base : base + main] = body.astype(BF)
            ref[span, base + main : base + main + 128] = jnp.where(lane < 64, end, 0.0).astype(BF)

    own_n2.wait_recv()
    by_rows(0, 2 * count, 256, gates)
    for copy in low:
        copy.wait_recv()
    both = links.push(
        n2.at[pl.ds(2 * count, count)], n2.at[pl.ds(3 * count, count)], peer(core=True)
    )
    down[0].forward()
    outs.append(links.copy(gu_w, gu_out))
    both.wait_recv()
    outs.append(links.copy(n2, n2_out))
    by_rows(2 * count, 2 * count, 256, gates)
    down[1].forward()
    for spread in spreads[gu_spreads:]:
        spread.finish()
    outs.append(links.copy(down_w, down_out))
    tokens.wait()
    for copy in outs:
        copy.wait()
    links.close()


def forward(far, main, micro, span_chips, sources, tables):
    gain_pack, attn_pack, ffn_pack, hidden, cotangent = sources
    count, width = hidden.shape
    attn_cols = attn_pack.shape[1] // 2
    gu_cols, down_cols = 2 * main + 128, main + 128
    n_q = (attn_cols - 128) // 2
    group = 4 * count
    heads = n_q // HEAD_DIM
    span, tokens = tables[2].shape[0], tables[3].shape[2]

    def low(*shape):
        return jax.ShapeDtypeStruct(shape, BF)

    shapes = [
        jax.ShapeDtypeStruct((8, width), F32),
        jax.ShapeDtypeStruct((micro, heads, tokens), F32),
        jax.ShapeDtypeStruct((count, width), F32),
        low(group, down_cols),
        low(group, 2 * down_cols),
        low(2 * count, n_q),
        low(2 * count, n_q),
        low(span_chips, 2 * count, 128),
        low(2 * count, width),
        low(width, attn_cols),
        low(group, width),
        low(width, gu_cols),
        low(width, down_cols),
        low(3 * count, width),
    ]
    return pl.pallas_call(
        functools.partial(forward_kernel, far, main, micro),
        in_specs=[ANY] * 5 + [VMEM] * 4,
        out_specs=[VMEM] * 8 + [ANY] * 6,
        out_shape=shapes,
        scratch_shapes=[
            pltpu.VMEM((2 ** len(far) * 4 * gain_pack.shape[0], 128), BF),
            pltpu.VMEM((width, attn_cols), BF),
            pltpu.VMEM((width, gu_cols), BF),
            pltpu.VMEM((width, down_cols), BF),
            pltpu.VMEM((2 * count, width), BF),
            pltpu.VMEM((2 * count, width), BF),
            pltpu.VMEM((group, width), BF),
            pltpu.VMEM((span, tokens), F32),
            pltpu.VMEM((2 * count, 128), F32),
        ]
        + [pltpu.VMEM((count, width), BF)] * 4
        + link_scratch(256, 32),
        compiler_params=pltpu.CompilerParams(
            collective_id=0, has_side_effects=True, vmem_limit_bytes=VMEM_BIG
        ),
        name="forward",
    )(*sources, *tables)


class Collect:
    TILE = 256

    def __init__(self, links, far, width, sent, came, held, came_far, total, more):
        self.links, self.far, self.half = links, far, width // 2
        self.sent, self.came, self.held, self.came_far = sent, came, held, came_far
        self.total, self.more = total, more
        self.tiles = self.half // self.TILE
        self.arrivals = {}

    def send_half(self, name, job, which=None):
        columns, left, right = job
        tiles, tile = self.tiles, self.TILE
        if which is None:
            which = [i for i in range(tiles // 2, tiles)] + [i for i in range(tiles // 2)]
        for i in which:
            rows = pl.ds(i * tile, tile)
            start = self.half + i * tile
            self.sent[rows, columns] = dot_first(left[:, start : start + tile], right[...]).astype(
                BF
            )
            self.arrivals[name, i] = self.links.push(
                self.sent.at[rows, columns], self.came.at[rows, columns], peer(self.far[-1])
            )

    def own_half(self, name, job, which):
        columns, left, right = job
        tiles, tile = self.tiles, self.TILE
        for i in which:
            rows = pl.ds(i * tile, tile)
            self.arrivals[name, i].wait_recv()
            term = dot_first(left[:, i * tile : (i + 1) * tile], right[...])
            term = term + self.came[rows, columns].astype(F32)
            if i >= tiles // 2:
                place = pl.ds((i - tiles // 2) * tile, tile)
                self.held[place, columns] = term.astype(BF)
                self.arrivals[name, "far", i - tiles // 2] = self.links.push(
                    self.held.at[place, columns],
                    self.came_far.at[place, columns],
                    peer(self.far[-2]),
                )
            else:
                self.total[rows, columns] = term

    def upper(self):
        return range(self.tiles // 2, self.tiles)

    def lower(self):
        return range(self.tiles // 2)

    def finish(self, name, job):
        columns = job[0]
        for i in self.lower():
            rows = pl.ds(i * self.TILE, self.TILE)
            self.arrivals[name, "far", i].wait_recv()
            self.total[rows, columns] = self.total[rows, columns] + self.came_far[
                rows, columns
            ].astype(F32)

    def finish_more(self):
        kept = self.half // 2
        for bit, (sent, came) in zip(self.far[-3::-1], self.more):
            kept //= 2
            sent[...] = self.total[pl.ds(kept, kept)].astype(BF)
            copy = self.links.push(sent, came, peer(bit))
            copy.wait_recv()
            self.total[pl.ds(0, kept)] = self.total[pl.ds(0, kept)] + came[...].astype(F32)


def collect_scratch(far, width, cols):
    shapes = [
        pltpu.VMEM((width // 2, cols), BF),
        pltpu.VMEM((width // 2, cols), BF),
        pltpu.VMEM((width // 4, cols), BF),
        pltpu.VMEM((width // 4, cols), BF),
    ]
    kept = width // 4
    for _ in far[2:]:
        kept //= 2
        shapes += [pltpu.VMEM((kept, cols), BF)] * 2
    return shapes


def paired(refs):
    return [(refs[i], refs[i + 1]) for i in range(0, len(refs), 2)]


class GroupSum:
    def __init__(self, links, count, width, chunks, term, part, land, low_part, land_low, summ, across):
        self.links, self.count, self.term = links, count, term
        self.part, self.land, self.low_part, self.land_low = part, land, low_part, land_low
        self.summ, self.across = summ, across
        size = width // chunks
        self.spans = [pl.ds(i * size, size) for i in range(chunks)]
        self.flight = {}

    def outer(self, slot):
        rows = pl.ds((slot // 2) * self.count, self.count)
        own = pl.ds(0, self.count)
        if slot == 1:
            self.links.settle([self.flight[3, i] for i in range(len(self.spans))])
        for i, span in enumerate(self.spans):
            self.part[own, span] = self.term(slot, span).astype(BF)
            self.flight[slot, i] = self.links.push(
                self.part.at[own, span], self.land.at[rows, span], peer(core=True)
            )

    def to_low(self):
        for i, span in enumerate(self.spans):
            value = self.term(2, span)
            self.flight[3, i].wait_recv()
            value = value + self.land[pl.ds(self.count, self.count), span].astype(F32)
            self.low_part[:, span] = value.astype(BF)
            self.flight["low", i] = self.links.push(
                self.low_part.at[:, span], self.land_low.at[:, span], peer(LOW)
            )

    def to_half(self, which=None):
        for i, span in enumerate(self.spans):
            if which is not None and i not in which:
                continue
            value = self.term(0, span)
            self.flight["low", i].wait_recv()
            self.flight[1, i].wait_recv()
            value = value + self.land[pl.ds(0, self.count), span].astype(F32)
            value = value + self.land_low[:, span].astype(F32)
            self.summ[:, span] = value.astype(BF)
            self.flight["half", i] = self.links.push(
                self.summ.at[:, span], self.across.at[:, span], peer(tensor=True)
            )

    def wait(self):
        for i in range(len(self.spans)):
            self.flight["half", i].wait_recv()


def group_sum_scratch(count, width):
    return [
        pltpu.VMEM((count, width), BF),
        pltpu.VMEM((2 * count, width), BF),
        pltpu.VMEM((count, width), BF),
        pltpu.VMEM((count, width), BF),
    ]


def ffn_backward_kernel(far, main, *refs):
    own_in, cot_in, act_in, down_in, slope_in, n2_in, gu_in = refs[:7]
    summ, across, own_out, other_out = refs[7:11]
    cot, act, down_w, slope, n2, gu_w = refs[11:17]
    part, land, low_part, land_low = refs[17:21]
    total, sent, came, held, came_far = refs[21:26]
    more = paired(refs[26:-3])
    links = Links(*refs[-3:])
    loads = [
        links.copy(src, dst)
        for src, dst in (
            (cot_in, cot.at[pl.ds(own_in.shape[0], cot_in.shape[0])]),
            (act_in, act),
            (down_in, down_w),
            (slope_in, slope),
            (n2_in, n2),
            (gu_in, gu_w),
        )
    ]
    own_load = links.copy(own_in, cot.at[pl.ds(0, own_in.shape[0])])
    greet([CORE, TENSOR] + chips_apart(LOW, *far))
    group, width = cot.shape
    count = group // 4
    down_cols, gu_cols = down_w.shape[1], gu_w.shape[1]
    grads = slope.at[:, pl.ds(0, gu_cols)]
    down_job = (pl.ds(0, down_cols), cot, act)
    gu_job = (pl.ds(down_cols, gu_cols), n2, grads)
    collect = Collect(links, far, width, sent, came, held, came_far, total, more)

    own_load.wait()
    loads[0].wait()
    loads[1].wait()
    upper, lower = list(collect.upper()), list(collect.lower())
    collect.send_half("d", down_job, upper)
    loads[2].wait()
    loads[3].wait()
    lane = lax.broadcasted_iota(jnp.int32, (256, 128), 1)

    def slopes(start):
        span = pl.ds(start, 256)
        grad_act = dot_plain(cot[span], down_w[...])
        gate = grad_act * slope[span, 0:down_cols].astype(F32)
        upward = grad_act * slope[span, down_cols : 2 * down_cols].astype(F32)
        slope[span, 0:main] = gate[:, :main].astype(BF)
        slope[span, main : 2 * main] = upward[:, :main].astype(BF)
        last = jnp.where(lane < 64, gate[:, main:], pltpu.roll(upward[:, main:], 64, 1))
        slope[span, 2 * main : 2 * main + 128] = last.astype(BF)

    by_rows(0, group, 256, slopes)
    loads[4].wait()
    collect.send_half("g", gu_job, upper)

    loads[5].wait()

    def term(slot, span):
        return dot_last(slope[pl.ds(slot * count, count), 0:gu_cols], gu_w[span])

    sums = GroupSum(
        links, count, width, 4, term, part, land, low_part, land_low, summ, across
    )
    sums.outer(3)
    collect.own_half("d", down_job, upper)
    sums.to_low()
    sums.outer(1)
    collect.send_half("d", down_job, lower)
    collect.send_half("g", gu_job, lower)
    collect.own_half("g", gu_job, upper[:1])
    sums.to_half([0, 1])
    collect.own_half("g", gu_job, upper[1:])
    sums.to_half([2, 3])
    collect.own_half("d", down_job, lower)
    collect.own_half("g", gu_job, lower)
    collect.finish("d", down_job)
    collect.finish("g", gu_job)
    collect.finish_more()
    half_unit = own_out.shape[0]
    low = low_bit()
    own_out[...] = total[pl.ds(pl.multiple_of(low * half_unit, half_unit), half_unit)]
    other_out[...] = total[
        pl.ds(pl.multiple_of((1 - low) * half_unit, half_unit), half_unit)
    ].astype(BF)
    sums.wait()
    links.close()


def ffn_backward(far, main, own, cot, act, down_w, slope, n2, gu_w):
    group, width = n2.shape
    count = group // 4
    cols = gu_w.shape[1] + down_w.shape[1]
    inputs = (own, cot, act, down_w, slope, n2, gu_w)
    return pl.pallas_call(
        functools.partial(ffn_backward_kernel, far, main),
        in_specs=[ANY] * 7,
        out_specs=[VMEM] * 4,
        out_shape=[
            jax.ShapeDtypeStruct((count, width), BF),
            jax.ShapeDtypeStruct((count, width), BF),
            jax.ShapeDtypeStruct((width // 2 ** (len(far) + 1), cols), F32),
            jax.ShapeDtypeStruct((width // 2 ** (len(far) + 1), cols), BF),
        ],
        scratch_shapes=[pltpu.VMEM((group, width), BF)]
        + [pltpu.VMEM(a.shape, BF) for a in inputs[2:]]
        + group_sum_scratch(count, width)
        + [pltpu.VMEM((width // 4, cols), F32)]
        + collect_scratch(far, width, cols)
        + link_scratch(128, 32),
        compiler_params=pltpu.CompilerParams(
            collective_id=2, has_side_effects=True, vmem_limit_bytes=VMEM_BIG
        ),
        name="ffn_backward",
    )(*inputs)


def finale_kernel(far, micro, *refs):
    (
        gain_rows,
        middle_in,
        cot_in,
        grad_two_in,
        across_two_in,
        hid_in,
        cos_in,
        sin_in,
        kpos,
        rowinfo,
        queries_in,
        lse,
        kvs_in,
        attn_in,
        n1_in,
        mixed_in,
        act_in,
        down_in,
        ffn_own,
        ffn_other,
    ) = refs[:20]
    (
        grad_middle,
        summ,
        across,
        feed,
        feed_across,
        attn_mine,
        attn_came,
        gains,
        ffn_core,
        ffn_low,
        ffn_low_core,
    ) = refs[20:31]
    attn_w, n1, mixed, gmid, raw = refs[31:36]
    dkv_own, dkv_sent, dkv_land, side, land_side = refs[36:41]
    low_sent, low_land = refs[41:43]
    near_gains, far_gains, low_gains, core_gains = refs[43:47]
    part, land, land_low = refs[47:50]
    total, sent, came, held, came_far = refs[50:55]
    queries, kvs, cosine, sine, bias, dk, dv, act, down_w = refs[55:64]
    more = paired(refs[64:-3])
    go = raw.at[:, pl.ds(0, mixed.shape[1])]
    links = Links(*refs[-3:])
    loads = [
        links.copy(src, dst)
        for src, dst in (
            (middle_in, grad_middle),
            (cot_in, summ),
            (grad_two_in, feed),
            (across_two_in, part),
            (attn_in, attn_w),
            (mixed_in, mixed),
            (n1_in, n1),
        )
    ]
    span_chips = kvs_in.shape[0]
    greet([CORE, TENSOR] + chips_apart(LOW, *far) + chips_apart(*range(1, span_chips)))
    count, width = grad_middle.shape
    rows = count // micro
    n_q = queries_in.shape[1]
    n_qkv = n_q + 128
    low, core = low_bit(), core_bit()
    block = ffn_own.shape[0] // 2

    def core_rows(which):
        return pl.ds(pl.multiple_of(which * block, block), block)

    ffn_flight = [
        links.push(ffn_other, ffn_low, peer(LOW)),
        links.push(ffn_own.at[core_rows(1 - core)], ffn_core, peer(core=True)),
    ]

    for load in loads[:4]:
        load.wait()
    near_gains[...] = jnp.zeros_like(near_gains)

    def second_norm(start):
        span = pl.ds(start, 64)
        grad = feed[span].astype(F32) + part[span].astype(F32)
        value = grad_middle[span]
        ratio = lax.rsqrt(jnp.mean(value * value, axis=-1, keepdims=True) + epsilon)
        turned = value * ratio
        near_gains[1:2] += jnp.sum(grad * turned, axis=0, keepdims=True)
        scaled = grad * gain_rows[1:2]
        inner = jnp.mean(scaled * turned, axis=-1, keepdims=True)
        result = summ[span].astype(F32) + ratio * (scaled - turned * inner)
        grad_middle[span] = result
        gmid[span] = result.astype(BF)

    by_rows(0, count, 64, second_norm)
    own = links.push(gmid.at[pl.ds(0, count)], gmid.at[pl.ds(count, count)], peer(core=True))
    collect = Collect(links, far, width, sent, came, held, came_far, total, more)
    out_job = (pl.ds(n_qkv, n_q), gmid, mixed)
    qkv_job = (pl.ds(0, n_qkv), n1, raw)
    upper, lower = list(collect.upper()), list(collect.lower())
    loads[4].wait()
    loads[5].wait()

    def mixed_back(start):
        span = pl.ds(start, 128)
        go[span] = dot_plain(gmid[span], attn_w[:, n_qkv : n_qkv + n_q]).astype(BF)

    by_rows(0, count, 128, mixed_back)
    own.wait_recv()
    by_rows(count, count, 128, mixed_back)
    collect.send_half("o", out_job, upper)
    collect.send_half("o", out_job, lower)

    def attention():
        scoped = [
            links.copy(src, dst)
            for src, dst in (
                (queries_in, queries),
                (kvs_in, kvs),
                (cos_in, cosine),
                (sin_in, sine),
            )
        ]
        for load in scoped:
            load.wait()
        for m in range(micro):
            mine, other = pl.ds(m * rows, rows), pl.ds(count + m * rows, rows)
            bias[...] = mask_bias(kpos[...], rowinfo[m])

            def both(ref):
                return jnp.concatenate([ref[mine], ref[other]], axis=0)

            kv = jnp.concatenate(
                [kvs[key, span] for key in range(span_chips) for span in (mine, other)], axis=0
            )
            grad_q = attend_back(bias, both(queries), both(go), lse[m], kv, dk, dv)
            grad_q = turn(grad_q, both(cosine), both(sine), True).astype(BF)
            raw[mine, 0:n_q] = grad_q[:rows]
            raw[other, 0:n_q] = grad_q[rows:]
            for key in range(span_chips):
                for place, span in ((0, mine), (rows, other)):
                    at = pl.ds(key * 2 * rows + place, rows)
                    pair = jnp.concatenate([dk[at], dv[at]], axis=1)
                    if key == 0:
                        dkv_own[span] = pair
                    else:
                        dkv_sent[key - 1, span] = pair.astype(BF)
        flight = [
            links.push(dkv_sent.at[key - 1], dkv_land.at[key - 1], peer(key))
            for key in range(1, span_chips)
        ]
        collect.own_half("o", out_job, upper)
        for copy in flight:
            copy.wait_recv()

        def key_values(start):
            span = pl.ds(start, 256)
            pair = dkv_own[span]
            for key in range(span_chips - 1):
                pair = pair + dkv_land[key, span].astype(F32)
            lane = lax.broadcasted_iota(jnp.int32, pair.shape, 1)
            turned = turn(pair, cosine[span], sine[span], True)
            raw[span, n_q:n_qkv] = jnp.where(lane < HEAD_DIM, turned, pair).astype(BF)

        by_rows(0, 2 * count, 256, key_values)

    attention()

    loads[6].wait()
    collect.send_half("q", qkv_job, upper)
    collect.send_half("q", qkv_job, lower)
    spans = [pl.ds(i * (width // 4), width // 4) for i in range(4)]
    to_core = []
    for span in spans:
        side[:, span] = dot_last(raw[pl.ds(count, count)], attn_w[span, 0:n_qkv]).astype(BF)
        to_core.append(links.push(side.at[:, span], land_side.at[:, span], peer(core=True)))
    over = []
    for i, span in enumerate(spans):
        value = dot_last(raw[pl.ds(0, count)], attn_w[span, 0:n_qkv])
        to_core[i].wait_recv()
        summ[:, span] = (value + land_side[:, span].astype(F32)).astype(BF)
        over.append(links.push(summ.at[:, span], across.at[:, span], peer(tensor=True)))
    load_hid = links.copy(hid_in, land_side)

    def feed_sums():
        scoped = [links.copy(act_in, act), links.copy(down_in, down_w)]
        collect.own_half("q", qkv_job, upper)
        collect.own_half("o", out_job, lower)
        for load in scoped:
            load.wait()

        def term(slot, span):
            return dot_last(act[pl.ds(slot * count, count)], down_w[span])

        sums = GroupSum(
            links, count, width, 4, term, part, land, side, land_low, feed, feed_across
        )
        links.settle(to_core)
        sums.outer(3)
        sums.to_low()
        sums.outer(1)
        collect.own_half("q", qkv_job, lower)
        sums.to_half()
        return sums

    sums = feed_sums()
    collect.finish("o", out_job)
    collect.finish("q", qkv_job)
    collect.finish_more()

    half_unit = attn_mine.shape[0] * 2

    def low_rows(which):
        return pl.ds(pl.multiple_of(which * half_unit, half_unit), half_unit)

    low_sent[...] = total[low_rows(1 - low)].astype(BF)
    low_flight = links.push(low_sent, low_land, peer(LOW))

    for copy in over:
        copy.wait_recv()
    load_hid.wait()

    def first_norm(start):
        span = pl.ds(start, 64)
        value = land_side[span].astype(F32)
        ratio = lax.rsqrt(jnp.mean(value * value, axis=-1, keepdims=True) + epsilon)
        grad = summ[span].astype(F32) + across[span].astype(F32)
        near_gains[0:1] += jnp.sum(grad * value * ratio, axis=0, keepdims=True)

    by_rows(0, count, 64, first_norm)
    kept, base = width, 0
    for bit in far[::-1]:
        kept //= 2
        landed = far_gains.at[:, pl.ds(base, kept)]
        copy = links.push(near_gains.at[:, pl.ds(kept, kept)], landed, peer(bit))
        copy.wait_recv()
        near_gains[:, 0:kept] = near_gains[:, 0:kept] + landed[...]
        base += kept
    copy = links.push(near_gains.at[:, pl.ds(0, kept)], low_gains, peer(LOW))
    ffn_flight[0].wait_recv()
    ffn_flight.append(
        links.push(ffn_low.at[core_rows(1 - core)], ffn_low_core, peer(core=True))
    )
    copy.wait_recv()
    gains[...] = near_gains[:, 0:kept] + low_gains[...]
    copy = links.push(gains, core_gains, peer(core=True))

    low_flight.wait_recv()
    own_unit = total[low_rows(low)] + low_land[...].astype(F32)
    total[0:half_unit] = own_unit
    core_flight = links.push(total.at[core_rows(1 - core)], attn_came, peer(core=True))
    attn_mine[...] = total[core_rows(core)]
    copy.wait_recv()
    core_flight.wait_recv()
    for flight in ffn_flight[1:]:
        flight.wait_recv()
    sums.wait()
    links.close()
    gains[...] = gains[...] + core_gains[...]


def finale(far, micro, inputs):
    (
        gain_rows,
        middle,
        cot,
        grad_two,
        across_two,
        hid,
        cosine,
        sine,
        kpos,
        rowinfo,
        queries,
        lse,
        kvs,
        attn_w,
        n1,
        mixed,
        act,
        down_w,
        ffn_own,
        ffn_other,
    ) = inputs
    count, width = middle.shape
    n_q = mixed.shape[1]
    attn_cols, ffn_cols = attn_w.shape[1], ffn_own.shape[1]
    unit = width // 2 ** len(far)
    block = unit // 4
    span_chips = kvs.shape[0]

    def shape(dtype, *dims):
        return jax.ShapeDtypeStruct(dims, dtype)

    rows = shape(BF, count, width)
    any_or_vmem = [VMEM] + [ANY] * 7 + [VMEM] * 2 + [ANY] + [VMEM] + [ANY] * 8
    return pl.pallas_call(
        functools.partial(finale_kernel, far, micro),
        in_specs=any_or_vmem,
        out_specs=[VMEM] * 6 + [ANY, VMEM] + [ANY] * 3,
        out_shape=[
            shape(F32, count, width),
            rows,
            rows,
            rows,
            rows,
            shape(F32, block, attn_cols),
            shape(F32, block, attn_cols),
            shape(F32, 8, unit),
            shape(F32, block, ffn_cols),
            shape(BF, 2 * block, ffn_cols),
            shape(BF, block, ffn_cols),
        ],
        scratch_shapes=[
            pltpu.VMEM((width, attn_cols), BF),
            pltpu.VMEM((2 * count, width), BF),
            pltpu.VMEM((2 * count, n_q), BF),
            pltpu.VMEM((2 * count, width), BF),
            pltpu.VMEM((2 * count, n_q + 128), BF),
            pltpu.VMEM((2 * count, 128), F32),
            pltpu.VMEM((span_chips - 1, 2 * count, 128), BF),
            pltpu.VMEM((span_chips - 1, 2 * count, 128), BF),
            pltpu.VMEM((count, width), BF),
            pltpu.VMEM((count, width), BF),
            pltpu.VMEM((2 * block, attn_cols), BF),
            pltpu.VMEM((2 * block, attn_cols), BF),
            pltpu.VMEM((8, width), F32),
            pltpu.VMEM((8, width), F32),
            pltpu.VMEM((8, unit), F32),
            pltpu.VMEM((8, unit), F32),
        ]
        + group_sum_scratch(count, width)[:3]
        + [pltpu.VMEM((width // 4, attn_cols), F32)]
        + collect_scratch(far, width, attn_cols)[:4]
        + [
            pltpu.VMEM(queries.shape, BF),
            pltpu.VMEM(kvs.shape, BF),
            pltpu.VMEM(cosine.shape, F32),
            pltpu.VMEM(sine.shape, F32),
            pltpu.VMEM((kpos.shape[0], rowinfo.shape[2]), F32),
            pltpu.VMEM((kpos.shape[0], HEAD_DIM), F32),
            pltpu.VMEM((kpos.shape[0], HEAD_DIM), F32),
            pltpu.VMEM(act.shape, BF),
            pltpu.VMEM(down_w.shape, BF),
        ]
        + collect_scratch(far, width, attn_cols)[4:]
        + link_scratch(192, 32),
        compiler_params=pltpu.CompilerParams(
            collective_id=3, has_side_effects=True, vmem_limit_bytes=VMEM_BIG
        ),
        name="finale",
    )(*inputs)


def body(
    tokens,
    doc_position,
    attn_gain,
    w_query,
    w_key,
    w_value,
    w_out,
    ffn_gain,
    w_gate,
    w_up,
    w_down,
    cotangent,
):
    size = lax.axis_size("dp")
    chips = size // 2
    far = [1 << place for place in range(chips.bit_length() - 1) if 1 << place != LOW][::-1]
    me = lax.axis_index("dp")
    core = me % 2
    chip = me // 2
    low = (chip // LOW) % 2
    micro, stretch, width = tokens.shape
    count = micro * stretch
    block = width // chips
    own_block = block // 2
    span_chips = SEQ_LEN // (2 * stretch)
    in_span = chip % span_chips

    keys = [0]
    for bit in far:
        keys = keys + [key | bit for key in keys]

    def rearranged(array):
        base = chip - LOW * low
        return jnp.concatenate(
            [
                lax.dynamic_slice_in_dim(
                    array, ((base ^ key) + LOW * side) * block, block, array.ndim - 1
                )
                for key in keys
                for side in range(2)
            ],
            axis=-1,
        )

    def restored(array):
        unit_of = jnp.array([keys.index(other & ~LOW) for other in range(chips)], jnp.int32)
        return jnp.concatenate(
            [
                lax.dynamic_slice_in_dim(
                    array,
                    (unit_of[chip ^ natural] * 2 + (natural // LOW) % 2) * block,
                    block,
                    array.ndim - 1,
                )
                for natural in range(chips)
            ],
            axis=-1,
        )

    def halves(array):
        n = array.shape[1] // 2
        return array[:, :n], array[:, n:]

    attn_pack = jnp.concatenate(
        [
            halves(w)[side]
            for side in range(2)
            for w in (w_query, w_key, w_value, w_out.T)
        ],
        axis=1,
    )
    hidden_units = w_gate.shape[1] // 4
    main = hidden_units // 128 * 128
    rest = hidden_units - main
    assert rest == 64

    def mains(array, place):
        return array[:, place * main : (place + 1) * main]

    def rests(array, place):
        return array[:, 4 * main + place * rest : 4 * main + (place + 1) * rest]

    w_down_t = w_down.T
    empty = jnp.zeros((own_block, 128 - rest), BF)
    ffn_pack = jnp.concatenate(
        [
            piece
            for place in range(4)
            for piece in (
                mains(w_gate, place),
                mains(w_up, place),
                rests(w_gate, place),
                rests(w_up, place),
                mains(w_down_t, place),
                rests(w_down_t, place),
                empty,
            )
        ],
        axis=1,
    )
    gain_pack = jnp.zeros((16, 128), BF).at[0, :own_block].set(attn_gain)
    gain_pack = gain_pack.at[1, :own_block].set(ffn_gain)
    hidden = rearranged(tokens.reshape(count, width))
    grad_final = rearranged(cotangent.reshape(count, width))

    hidden_f = hidden.astype(F32)
    position_both = jnp.stack([doc_position, swap_core(doc_position)])

    power = jnp.arange(HEAD_DIM // 2, dtype=F32) * (2.0 / HEAD_DIM)
    inverse = 10000.0 ** (-power)
    turned = position_both.reshape(2 * count).astype(F32)[:, None] * jnp.tile(inverse, 4)[None, :]
    cosine, sine = jnp.cos(turned), jnp.sin(turned)

    inner = jnp.arange(2 * stretch, dtype=jnp.int32) ^ (core * stretch)
    row_place = in_span * (2 * stretch) + inner
    kpos = jnp.concatenate(
        [(in_span ^ key) * (2 * stretch) + inner for key in range(span_chips)]
    ).reshape(-1, 1)
    row_position = position_both.transpose(1, 0, 2).reshape(micro, 2 * stretch)
    row_places = jnp.broadcast_to(row_place[None, :], row_position.shape)
    rowinfo = jnp.stack([row_places, row_places - row_position], axis=1)

    n_q = w_query.shape[1] // 2
    n_kv = w_key.shape[1] // 2
    n_qkv = n_q + 2 * n_kv
    (
        gain_rows,
        lse,
        middle,
        activated,
        slopes,
        mixed,
        queries,
        kvs,
        normed,
        attn_w,
        normed_two,
        gu_w,
        down_wt,
        grad_final_others,
    ) = forward(
        far,
        main,
        micro,
        span_chips,
        (gain_pack, attn_pack, ffn_pack, hidden, grad_final),
        (cosine, sine, kpos, rowinfo),
    )
    gain_one, gain_two = gain_rows[0:1], gain_rows[1:2]
    grad_two, grad_two_across, ffn_own, ffn_other = ffn_backward(
        far, main, grad_final, grad_final_others, activated, down_wt, slopes, normed_two, gu_w
    )
    (
        grad_middle,
        grad_one,
        grad_one_across,
        feed,
        feed_across,
        attn_mine,
        attn_came,
        grad_gains,
        ffn_core,
        ffn_low,
        ffn_low_core,
    ) = finale(
        far,
        micro,
        (
            gain_rows,
            middle,
            grad_final,
            grad_two,
            grad_two_across,
            hidden,
            cosine,
            sine,
            kpos,
            rowinfo,
            queries,
            lse,
            kvs,
            attn_w,
            normed,
            mixed,
            activated,
            down_wt,
            ffn_own,
            ffn_other,
        ),
    )
    output = restored((middle + (feed.astype(F32) + feed_across.astype(F32))).astype(BF))
    grad_normed = grad_one.astype(F32) + grad_one_across.astype(F32)
    ratio_one = lax.rsqrt(jnp.mean(hidden_f * hidden_f, axis=-1, keepdims=True) + epsilon)
    grad_in_norm = norm_back(grad_normed, hidden_f, ratio_one, gain_rows[0:1])
    grad_tokens = restored(grad_middle + grad_in_norm)
    grad_gains = lax.dynamic_slice_in_dim(grad_gains, (2 * low + core) * own_block, own_block, 1)

    def picked(pair, side):
        return jnp.where(side == 0, pair[0], pair[1]), jnp.where(side == 0, pair[1], pair[0])

    parts = picked((attn_mine, attn_came), core)

    def columns(start, stop):
        return jnp.concatenate([part[:, start:stop] for part in parts], axis=1)

    grad_w_query = columns(0, n_q)
    grad_w_key = columns(n_q, n_q + n_kv)
    grad_w_value = columns(n_q + n_kv, n_qkv)
    grad_w_out = columns(n_qkv, n_qkv + n_q).T

    def own_rows(array):
        return lax.dynamic_slice_in_dim(array, core * own_block, own_block, 0)

    mine_low = picked((own_rows(ffn_own), ffn_core), core)
    other_low = picked((own_rows(ffn_low).astype(F32), ffn_low_core.astype(F32)), core)
    by_low = [
        picked((mine_low[side], other_low[side]), low) for side in range(2)
    ]
    places = [by_low[place % 2][place // 2] for place in range(4)]
    down_cols = main + 128
    gu = down_cols

    def gathered(main_start, rest_start):
        return jnp.concatenate(
            [part[:, main_start : main_start + main] for part in places]
            + [part[:, rest_start : rest_start + rest] for part in places],
            axis=1,
        )

    grad_w_down = gathered(0, main).T
    grad_w_gate = gathered(gu, gu + 2 * main)
    grad_w_up = gathered(gu + main, gu + 2 * main + rest)
    return (
        output.reshape(tokens.shape),
        grad_tokens.reshape(tokens.shape),
        grad_gains[0],
        grad_w_query,
        grad_w_key,
        grad_w_value,
        grad_w_out,
        grad_gains[1],
        grad_w_gate,
        grad_w_up,
        grad_w_down,
    )


def solution(mesh):
    return jax.shard_map(
        body,
        mesh=mesh,
        in_specs=(
            P(None, "dp", None),
            P(None, "dp"),
            P("dp"),
            P("dp", "tensor"),
            P("dp", "tensor"),
            P("dp", "tensor"),
            P("tensor", "dp"),
            P("dp"),
            P("dp", "tensor"),
            P("dp", "tensor"),
            P("tensor", "dp"),
            P(None, "dp", None),
        ),
        out_specs=(
            P(None, "dp", None),
            P(None, "dp", None),
            P("dp"),
            P("dp", "tensor"),
            P("dp", "tensor"),
            P("dp", "tensor"),
            P("tensor", "dp"),
            P("dp"),
            P("dp", "tensor"),
            P("dp", "tensor"),
            P("tensor", "dp"),
        ),
        check_vma=False,
    )
```

```python
import functools

import jax
import jax.numpy as jnp
from jax import lax
from jax.experimental import pallas as pl
from jax.experimental.pallas import tpu as pltpu
from jax.sharding import PartitionSpec as P

HEAD_DIM = 64
SEQ_LEN = 1024
BF = jnp.bfloat16
F32 = jnp.float32
epsilon = 1e-05
VMEM_LIMIT = 48 * 1024 * 1024
VMEM_BIG = 62 * 1024 * 1024


LOW = 2


def swap_core(block):
    size = lax.axis_size("dp")
    return lax.ppermute(block, "dp", [(i, i ^ 1) for i in range(size)])


def swap_chip(block, distance):
    size = lax.axis_size("dp")
    return lax.ppermute(block, "dp", [(i, i ^ (2 * distance)) for i in range(size)])


def flipped(index, distance):
    return index + distance * (1 - 2 * ((index // distance) % 2))


def peer(distance=0, core=False, tensor=False):
    place = lax.axis_index("dp")
    bit = 1
    while bit <= distance:
        if distance & bit:
            place = flipped(place, 2 * bit)
        bit *= 2
    if core:
        place = flipped(place, 1)
    half = lax.axis_index("tensor")
    if tensor:
        half = 1 - half
    return (place, half)


def greet(peers):
    barrier = pltpu.get_barrier_semaphore()
    for name in sorted(set(peers)):
        pl.semaphore_signal(
            barrier, inc=1, device_id=peer(*name), device_id_type=pl.DeviceIdType.MESH
        )
    pl.semaphore_wait(barrier, len(set(peers)))


CORE = (0, True, False)
TENSOR = (0, False, True)


def chips_apart(*distances):
    return [(distance, False, False) for distance in distances]


class Links:
    def __init__(self, send, recv, local):
        self.send, self.recv, self.local = send, recv, local
        self.used = 0
        self.used_local = 0
        self.sent = []

    def push(self, src, dst, device):
        copy = pltpu.make_async_remote_copy(
            src_ref=src,
            dst_ref=dst,
            send_sem=self.send.at[self.used],
            recv_sem=self.recv.at[self.used],
            device_id=device,
            device_id_type=pl.DeviceIdType.MESH,
        )
        self.used += 1
        copy.start()
        self.sent.append(copy)
        return copy

    def copy(self, src, dst):
        copy = pltpu.make_async_copy(src, dst, self.local.at[self.used_local])
        self.used_local += 1
        copy.start()
        return copy

    def settle(self, copies):
        for copy in copies:
            copy.wait_send()
            self.sent = [other for other in self.sent if other is not copy]

    def close(self):
        for copy in self.sent:
            copy.wait_send()


def link_scratch(copies, locals_):
    return [
        pltpu.SemaphoreType.DMA((copies,)),
        pltpu.SemaphoreType.DMA((copies,)),
        pltpu.SemaphoreType.DMA((locals_,)),
    ]


class Joint:
    def __init__(self, copies):
        self.copies = copies

    def wait(self):
        for copy in self.copies:
            copy.wait()


def block_start(far, unit, side, block):
    place = lax.axis_index("dp") // 2
    place = place - LOW * ((place // LOW) % 2) + LOW * side
    for level, bit in enumerate(far):
        if (unit // 2**level) % 2:
            place = flipped(place, bit)
    return pl.multiple_of(place * block, block)


def load_rearranged(links, far, src, dst):
    units = 2 ** len(far)
    block = src.shape[1] // (2 * units)
    if block % 128:
        return links.copy(src, dst)
    copies = []
    for unit in range(units):
        for side in range(2):
            start = block_start(far, unit, side, block)
            copies.append(
                links.copy(
                    src.at[:, pl.ds(start, block)],
                    dst.at[:, pl.ds((2 * unit + side) * block, block)],
                )
            )
    return Joint(copies)


def low_bit():
    return (lax.axis_index("dp") // (2 * LOW)) % 2


def core_bit():
    return lax.axis_index("dp") % 2


def group_rows(height, low, core):
    return pl.ds(pl.multiple_of((low * 2 + core) * height, height), height)


class Spread:
    def __init__(self, links, src, column, dst, height, start, cols, far):
        self.links, self.src, self.column, self.dst = links, src, column, dst
        self.height, self.start, self.cols, self.far = height, start, cols, far
        self.level = 0

    def begin(self):
        low, core = low_bit(), core_bit()
        mine = self.dst.at[group_rows(self.height, low, core), pl.ds(self.start, self.cols)]

        def part(low, core):
            return self.src.at[:, pl.ds(pl.multiple_of(self.column(low, core), 128), self.cols)]

        self.local = self.links.copy(part(low, core), mine)
        self.stage = [
            self.links.push(part(1 - low, core), mine, peer(LOW)),
            self.links.push(part(1 - low, 1 - core), mine, peer(LOW, core=True)),
            self.links.push(part(low, 1 - core), mine, peer(core=True)),
        ]

    def unit(self, index):
        size = 4 * self.height
        return self.dst.at[pl.ds(index * size, size), pl.ds(self.start, self.cols)]

    def pass_on(self, index, first):
        for level in range(first, len(self.far)):
            reached = index + 2**level
            self.arrivals[reached] = self.links.push(
                self.unit(index), self.unit(reached), peer(self.far[level])
            )

    def launch(self):
        for copy in self.stage:
            copy.wait_recv()
        self.local.wait()
        self.arrivals = {}
        self.pass_on(0, 0)

    def forward(self):
        for index in range(1, 2 ** (len(self.far) - 1)):
            self.arrivals.pop(index).wait_recv()
            self.pass_on(index, index.bit_length())

    def finish(self):
        for copy in self.arrivals.values():
            copy.wait_recv()
        self.arrivals = {}


class TokenSpread:
    def __init__(self, links, own, others):
        self.links, self.own, self.others = links, own, others
        self.count = own.shape[0]

    def rows(self, slot, half=None):
        ref = self.others if slot else self.own
        base = (slot - 1) * self.count if slot else 0
        if half is None:
            return ref.at[pl.ds(base, self.count)]
        size = self.count // 2
        return ref.at[pl.ds(pl.multiple_of(base + half * size, size), size)]

    def begin(self):
        half = lax.axis_index("tensor")
        self.side = self.links.push(self.rows(0), self.rows(1), peer(core=True))
        self.low = self.links.push(self.rows(0, half), self.rows(2, half), peer(LOW))

    def second(self):
        half = lax.axis_index("tensor")
        self.low.wait_recv()
        self.across = self.links.push(self.rows(2, half), self.rows(2, half), peer(tensor=True))
        self.first = self.links.push(self.rows(2, half), self.rows(3, half), peer(core=True))

    def third(self):
        other = 1 - lax.axis_index("tensor")
        self.across.wait_recv()
        self.last = self.links.push(self.rows(2, other), self.rows(3, other), peer(core=True))

    def wait(self):
        self.side.wait_recv()
        self.first.wait_recv()
        self.last.wait_recv()


def cuts(start, tiles, parts):
    edges = [start + tiles * part // parts * 128 for part in range(parts + 1)]
    return [(edges[i], edges[i + 1] - edges[i]) for i in range(parts)]


def by_rows(start, total, step, work):
    def go(i, carry):
        work(pl.multiple_of(start + i * step, step))
        return carry

    lax.fori_loop(0, total // step, go, 0)


ANY = pl.BlockSpec(memory_space=pl.ANY)
VMEM = pl.BlockSpec(memory_space=pltpu.VMEM)


def dot_plain(left, right):
    return jnp.dot(left, right, preferred_element_type=F32)


def dot_first(left, right):
    return lax.dot_general(left, right, (((0,), (0,)), ((), ())), preferred_element_type=F32)


def dot_last(left, right):
    return lax.dot_general(left, right, (((1,), (1,)), ((), ())), preferred_element_type=F32)


def turn(value, cosine, sine, back):
    tiles = []
    lane = lax.broadcasted_iota(jnp.int32, (value.shape[0], 128), 1)
    first = (lane % 64) < 32
    for start in range(0, value.shape[1], 128):
        tile = value[:, start : start + 128]
        up = pltpu.roll(tile, 96, 1)
        down = pltpu.roll(tile, 32, 1)
        if back:
            other = jnp.where(first, up, -down)
        else:
            other = jnp.where(first, -up, down)
        tiles.append(tile * cosine + other * sine)
    return tiles[0] if len(tiles) == 1 else jnp.concatenate(tiles, axis=1)


def mask_bias(kpos, row):
    place, floor = row[0:1, :], row[1:2, :]
    allowed = (kpos <= place) & (kpos >= floor)
    return jnp.where(allowed, 0.0, -1e30).astype(F32)


def attend(bias_ref, queries, kv):
    keys = kv[:, :HEAD_DIM]
    values_t = kv.T[HEAD_DIM:, :]
    parts = []
    sums = []
    for head in range(queries.shape[1] // HEAD_DIM):
        q_head = queries[:, head * HEAD_DIM : (head + 1) * HEAD_DIM]
        scores = dot_last(keys, q_head) + bias_ref[...]
        peak = jnp.max(scores, axis=0, keepdims=True)
        expon = jnp.exp(scores - peak)
        total = jnp.sum(expon, axis=0, keepdims=True)
        parts.append(dot_plain(values_t, expon.astype(BF)) * (1.0 / total))
        sums.append(peak + jnp.log(total))
    return jnp.concatenate(parts, axis=0), jnp.concatenate(sums, axis=0)


def attend_back(bias_ref, queries, grads, lse, kv, dk_ref, dv_ref):
    keys = kv[:, :HEAD_DIM]
    values = kv[:, HEAD_DIM:]
    keys_t = kv.T[:HEAD_DIM, :]
    parts = []
    for head in range(queries.shape[1] // HEAD_DIM):
        q_head = queries[:, head * HEAD_DIM : (head + 1) * HEAD_DIM]
        g_head = grads[:, head * HEAD_DIM : (head + 1) * HEAD_DIM]
        scores = dot_last(keys, q_head) + bias_ref[...]
        probs = jnp.exp(scores - lse[head : head + 1, :])
        grad_probs = dot_last(values, g_head)
        inner = jnp.sum(probs * grad_probs, axis=0, keepdims=True)
        grad_scores = (probs * (grad_probs - inner)).astype(BF)
        grad_values = dot_plain(probs.astype(BF), g_head)
        grad_keys = dot_plain(grad_scores, q_head)
        if head == 0:
            dv_ref[...] = grad_values
            dk_ref[...] = grad_keys
        else:
            dv_ref[...] += grad_values
            dk_ref[...] += grad_keys
        parts.append(dot_plain(keys_t, grad_scores))
    return jnp.concatenate(parts, axis=0).T * HEAD_DIM ** (-0.5)


def silu_parts(gate, upward):
    sigmoid = 1.0 / (1.0 + jnp.exp(-gate))
    silu = gate * sigmoid
    return silu * upward, upward * sigmoid * (1.0 + gate * (1.0 - sigmoid)), silu


def forward_kernel(far, main, micro, *refs):
    gain_src, attn_src, ffn_src, hid_src, cot_src, cosine, sine, kpos, rowinfo = refs[:9]
    (
        gain_rows,
        lse,
        middle,
        act,
        slope,
        mixed,
        queries,
        kvs,
        n1_out,
        attn_out,
        n2_out,
        gu_out,
        down_out,
        cot_out,
    ) = refs[9:23]
    gains, attn_w, gu_w, down_w, hid, n1, n2, bias, ratios, part, land, summ, across = refs[23:36]
    links = Links(*refs[36:])
    count = hid_src.shape[0]
    rows = count // micro
    span_chips = kvs.shape[0]
    greet(
        [CORE, TENSOR, (LOW, True, False)] + chips_apart(LOW, *far) + chips_apart(*range(1, span_chips))
    )
    attn_cols, gu_cols, down_cols = attn_w.shape[1], gu_w.shape[1], down_w.shape[1]
    total = gu_cols + down_cols
    height = attn_src.shape[0]

    def core_column(start):
        return lambda low, core: core * attn_cols + start

    def group_column(start):
        return lambda low, core: (low * 2 + core) * total + start

    spreads = [
        Spread(links, gain_src, lambda low, core: 0, gains, gain_src.shape[0], 0, 128, far)
    ]
    n_q = queries.shape[1]
    n_qkv = n_q + 128
    for base, tiles, parts in ((0, n_qkv // 128, 2), (n_qkv, n_q // 128, 2)):
        for start, cols in cuts(base, tiles, parts):
            spreads.append(
                Spread(links, attn_src, core_column(start), attn_w, height, start, cols, far)
            )
        if base == 0:
            qkv_spreads = len(spreads)
    attn_spreads = len(spreads)
    for start, cols in cuts(0, gu_cols // 128, 4):
        spreads.append(Spread(links, ffn_src, group_column(start), gu_w, height, start, cols, far))
    gu_spreads = len(spreads)
    for start, cols in cuts(0, down_cols // 128, 2):
        spreads.append(
            Spread(links, ffn_src, group_column(gu_cols + start), down_w, height, start, cols, far)
        )
    attn = spreads[:attn_spreads]
    gu = spreads[attn_spreads:gu_spreads]
    down = spreads[gu_spreads:]
    for spread in attn:
        spread.begin()
    own_hid = load_rearranged(links, far, hid_src, hid.at[pl.ds(0, count)])
    tokens = TokenSpread(links, cot_src, cot_out)
    own_hid.wait()
    side_hid = links.push(
        hid.at[pl.ds(0, count)], hid.at[pl.ds(count, count)], peer(core=True)
    )
    side_hid.wait_recv()

    def first_ratio(start):
        span = pl.ds(start, 64)
        value = hid[span].astype(F32)
        ratio = lax.rsqrt(jnp.mean(value * value, axis=-1, keepdims=True) + epsilon)
        ratios[span] = jnp.broadcast_to(ratio, (64, 128))

    by_rows(0, 2 * count, 64, first_ratio)
    for spread in attn:
        spread.launch()
    for spread in gu[:2]:
        spread.begin()
    tokens.begin()
    spreads[0].forward()

    spreads[0].finish()
    n_units = 2 ** len(far)
    own_block = gain_rows.shape[1] // (4 * n_units)
    both_gains = gains[...].astype(F32)
    for place in range(4 * n_units):
        gain_rows[0:2, place * own_block : (place + 1) * own_block] = both_gains[
            place * 16 : place * 16 + 2, :own_block
        ]

    def first_norm(start):
        span = pl.ds(start, 64)
        n1[span] = (hid[span].astype(F32) * ratios[span, 0:1] * gain_rows[0:1]).astype(BF)

    by_rows(0, 2 * count, 64, first_norm)
    outs = [links.copy(n1, n1_out)]
    for spread in spreads[1:qkv_spreads]:
        spread.forward()
    for spread in spreads[1:qkv_spreads]:
        spread.finish()

    def project(start):
        span = pl.ds(start, 256)
        raw = dot_plain(n1[span], attn_w[:, 0:n_qkv])
        cos, sin = cosine[span], sine[span]
        queries[span] = (turn(raw[:, :n_q], cos, sin, False) * HEAD_DIM ** (-0.5)).astype(BF)
        pair = raw[:, n_q:]
        lane = lax.broadcasted_iota(jnp.int32, pair.shape, 1)
        kvs[0, span] = jnp.where(lane < HEAD_DIM, turn(pair, cos, sin, False), pair).astype(BF)

    by_rows(0, 2 * count, 256, project)
    came = [
        links.push(kvs.at[0], kvs.at[key], peer(key)) for key in range(1, span_chips)
    ]
    for spread in gu[2:] + down:
        spread.begin()
    gu[0].launch()
    spreads[qkv_spreads].forward()
    gu[1].launch()
    for copy in came:
        copy.wait_recv()

    tokens.second()
    half = []
    for m in range(micro):
        own, other = pl.ds(m * rows, rows), pl.ds(count + m * rows, rows)
        bias[...] = mask_bias(kpos[...], rowinfo[m])
        kv = jnp.concatenate(
            [kvs[key, span] for key in range(span_chips) for span in (own, other)], axis=0
        )
        q_both = jnp.concatenate([queries[own], queries[other]], axis=0)
        mixed_t, sums = attend(bias, q_both, kv)
        lse[m] = sums
        value = mixed_t.T.astype(BF)
        mixed[own] = value[:rows]
        mixed[other] = value[rows:]
        if m == 0:
            for spread in spreads[qkv_spreads + 1 : attn_spreads]:
                spread.forward()
            for spread in spreads[qkv_spreads:attn_spreads]:
                spread.finish()
            outs.append(links.copy(attn_w, attn_out))
        out_w = attn_w.at[:, pl.ds(n_qkv, n_q)]
        term = dot_last(value, out_w[...])
        part[own] = term[rows:].astype(BF)
        side = links.push(part.at[own], land.at[own], peer(core=True))
        side.wait_recv()
        summ[own] = (term[:rows] + land[own].astype(F32)).astype(BF)
        half.append(links.push(summ.at[own], across.at[own], peer(tensor=True)))
        if m == 0:
            for spread in gu[2:]:
                spread.launch()
        if m == 1:
            gu[0].forward()
    for spread in down:
        spread.launch()
    gu[1].forward()
    tokens.third()

    def finish(start):
        span = pl.ds(start, 32)
        value = hid[span].astype(F32) + summ[span].astype(F32) + across[span].astype(F32)
        middle[span] = value
        ratio = lax.rsqrt(jnp.mean(value * value, axis=-1, keepdims=True) + epsilon)
        n2[span] = (value * ratio * gain_rows[1:2]).astype(BF)

    low = []
    for m in range(micro):
        half[m].wait_recv()
        by_rows(m * rows, rows, 32, finish)
        low.append(
            links.push(
                n2.at[pl.ds(m * rows, rows)], n2.at[pl.ds(2 * count + m * rows, rows)], peer(LOW)
            )
        )
    own_n2 = links.push(n2.at[pl.ds(0, count)], n2.at[pl.ds(count, count)], peer(core=True))
    gu[2].forward()
    gu[3].forward()
    for spread in spreads[attn_spreads:gu_spreads]:
        spread.finish()

    def gates(start):
        span = pl.ds(start, 256)
        raw = dot_plain(n2[span], gu_w[...])
        parts = silu_parts(raw[:, :main], raw[:, main : 2 * main])
        last = raw[:, 2 * main :]
        lane = lax.broadcasted_iota(jnp.int32, last.shape, 1)
        ends = silu_parts(last, pltpu.roll(last, 64, 1))
        for ref, base, body, end in (
            (act, 0, parts[0], ends[0]),
            (slope, 0, parts[1], ends[1]),
            (slope, main + 128, parts[2], ends[2]),
        ):
            ref[span, base : base + main] = body.astype(BF)
            ref[span, base + main : base + main + 128] = jnp.where(lane < 64, end, 0.0).astype(BF)

    own_n2.wait_recv()
    by_rows(0, 2 * count, 256, gates)
    for copy in low:
        copy.wait_recv()
    both = links.push(
        n2.at[pl.ds(2 * count, count)], n2.at[pl.ds(3 * count, count)], peer(core=True)
    )
    down[0].forward()
    outs.append(links.copy(gu_w, gu_out))
    both.wait_recv()
    outs.append(links.copy(n2, n2_out))
    by_rows(2 * count, 2 * count, 256, gates)
    down[1].forward()
    for spread in spreads[gu_spreads:]:
        spread.finish()
    outs.append(links.copy(down_w, down_out))
    tokens.wait()
    for copy in outs:
        copy.wait()
    links.close()


def forward(far, main, micro, span_chips, sources, tables):
    gain_pack, attn_pack, ffn_pack, hidden, cotangent = sources
    count, width = hidden.shape
    attn_cols = attn_pack.shape[1] // 2
    gu_cols, down_cols = 2 * main + 128, main + 128
    n_q = (attn_cols - 128) // 2
    group = 4 * count
    heads = n_q // HEAD_DIM
    span, tokens = tables[2].shape[0], tables[3].shape[2]

    def low(*shape):
        return jax.ShapeDtypeStruct(shape, BF)

    shapes = [
        jax.ShapeDtypeStruct((8, width), F32),
        jax.ShapeDtypeStruct((micro, heads, tokens), F32),
        jax.ShapeDtypeStruct((count, width), F32),
        low(group, down_cols),
        low(group, 2 * down_cols),
        low(2 * count, n_q),
        low(2 * count, n_q),
        low(span_chips, 2 * count, 128),
        low(2 * count, width),
        low(width, attn_cols),
        low(group, width),
        low(width, gu_cols),
        low(width, down_cols),
        low(3 * count, width),
    ]
    return pl.pallas_call(
        functools.partial(forward_kernel, far, main, micro),
        in_specs=[ANY] * 5 + [VMEM] * 4,
        out_specs=[VMEM] * 8 + [ANY] * 6,
        out_shape=shapes,
        scratch_shapes=[
            pltpu.VMEM((2 ** len(far) * 4 * gain_pack.shape[0], 128), BF),
            pltpu.VMEM((width, attn_cols), BF),
            pltpu.VMEM((width, gu_cols), BF),
            pltpu.VMEM((width, down_cols), BF),
            pltpu.VMEM((2 * count, width), BF),
            pltpu.VMEM((2 * count, width), BF),
            pltpu.VMEM((group, width), BF),
            pltpu.VMEM((span, tokens), F32),
            pltpu.VMEM((2 * count, 128), F32),
        ]
        + [pltpu.VMEM((count, width), BF)] * 4
        + link_scratch(256, 64),
        compiler_params=pltpu.CompilerParams(
            collective_id=0, has_side_effects=True, vmem_limit_bytes=VMEM_BIG
        ),
        name="forward",
    )(*sources, *tables)


class Collect:
    TILE = 256

    def __init__(self, links, far, width, sent, came, held, came_far, total, more):
        self.links, self.far, self.half = links, far, width // 2
        self.sent, self.came, self.held, self.came_far = sent, came, held, came_far
        self.total, self.more = total, more
        self.tiles = self.half // self.TILE
        self.arrivals = {}

    def send_half(self, name, job, which=None):
        columns, left, right = job
        tiles, tile = self.tiles, self.TILE
        if which is None:
            which = [i for i in range(tiles // 2, tiles)] + [i for i in range(tiles // 2)]
        for i in which:
            rows = pl.ds(i * tile, tile)
            start = self.half + i * tile
            self.sent[rows, columns] = dot_first(left[:, start : start + tile], right[...]).astype(
                BF
            )
            self.arrivals[name, i] = self.links.push(
                self.sent.at[rows, columns], self.came.at[rows, columns], peer(self.far[-1])
            )

    def own_half(self, name, job, which):
        columns, left, right = job
        tiles, tile = self.tiles, self.TILE
        for i in which:
            rows = pl.ds(i * tile, tile)
            self.arrivals[name, i].wait_recv()
            term = dot_first(left[:, i * tile : (i + 1) * tile], right[...])
            term = term + self.came[rows, columns].astype(F32)
            if i >= tiles // 2:
                place = pl.ds((i - tiles // 2) * tile, tile)
                self.held[place, columns] = term.astype(BF)
                self.arrivals[name, "far", i - tiles // 2] = self.links.push(
                    self.held.at[place, columns],
                    self.came_far.at[place, columns],
                    peer(self.far[-2]),
                )
            else:
                self.total[rows, columns] = term

    def upper(self):
        return range(self.tiles // 2, self.tiles)

    def lower(self):
        return range(self.tiles // 2)

    def finish(self, name, job):
        columns = job[0]
        for i in self.lower():
            rows = pl.ds(i * self.TILE, self.TILE)
            self.arrivals[name, "far", i].wait_recv()
            self.total[rows, columns] = self.total[rows, columns] + self.came_far[
                rows, columns
            ].astype(F32)

    def finish_more(self):
        kept = self.half // 2
        for bit, (sent, came) in zip(self.far[-3::-1], self.more):
            kept //= 2
            sent[...] = self.total[pl.ds(kept, kept)].astype(BF)
            copy = self.links.push(sent, came, peer(bit))
            copy.wait_recv()
            self.total[pl.ds(0, kept)] = self.total[pl.ds(0, kept)] + came[...].astype(F32)


def collect_scratch(far, width, cols):
    shapes = [
        pltpu.VMEM((width // 2, cols), BF),
        pltpu.VMEM((width // 2, cols), BF),
        pltpu.VMEM((width // 4, cols), BF),
        pltpu.VMEM((width // 4, cols), BF),
    ]
    kept = width // 4
    for _ in far[2:]:
        kept //= 2
        shapes += [pltpu.VMEM((kept, cols), BF)] * 2
    return shapes


def paired(refs):
    return [(refs[i], refs[i + 1]) for i in range(0, len(refs), 2)]


class GroupSum:
    def __init__(self, links, count, width, chunks, term, part, land, low_part, land_low, summ, across):
        self.links, self.count, self.term = links, count, term
        self.part, self.land, self.low_part, self.land_low = part, land, low_part, land_low
        self.summ, self.across = summ, across
        size = width // chunks
        self.spans = [pl.ds(i * size, size) for i in range(chunks)]
        self.flight = {}

    def outer(self, slot):
        rows = pl.ds((slot // 2) * self.count, self.count)
        own = pl.ds(0, self.count)
        if slot == 1:
            self.links.settle([self.flight[3, i] for i in range(len(self.spans))])
        for i, span in enumerate(self.spans):
            self.part[own, span] = self.term(slot, span).astype(BF)
            self.flight[slot, i] = self.links.push(
                self.part.at[own, span], self.land.at[rows, span], peer(core=True)
            )

    def to_low(self, which=None):
        for i, span in enumerate(self.spans):
            if which is not None and i not in which:
                continue
            value = self.term(2, span)
            self.flight[3, i].wait_recv()
            value = value + self.land[pl.ds(self.count, self.count), span].astype(F32)
            self.low_part[:, span] = value.astype(BF)
            self.flight["low", i] = self.links.push(
                self.low_part.at[:, span], self.land_low.at[:, span], peer(LOW)
            )

    def to_half(self, which=None):
        for i, span in enumerate(self.spans):
            if which is not None and i not in which:
                continue
            value = self.term(0, span)
            self.flight["low", i].wait_recv()
            self.flight[1, i].wait_recv()
            value = value + self.land[pl.ds(0, self.count), span].astype(F32)
            value = value + self.land_low[:, span].astype(F32)
            self.summ[:, span] = value.astype(BF)
            self.flight["half", i] = self.links.push(
                self.summ.at[:, span], self.across.at[:, span], peer(tensor=True)
            )

    def wait(self):
        for i in range(len(self.spans)):
            self.flight["half", i].wait_recv()


def group_sum_scratch(count, width):
    return [
        pltpu.VMEM((count, width), BF),
        pltpu.VMEM((2 * count, width), BF),
        pltpu.VMEM((count, width), BF),
        pltpu.VMEM((count, width), BF),
    ]


def ffn_backward_kernel(far, main, *refs):
    own_in, cot_in, act_in, down_in, slope_in, n2_in, gu_in = refs[:7]
    summ, across, own_out, other_out = refs[7:11]
    cot, act, down_w, slope, n2, gu_w = refs[11:17]
    part, land, low_part, land_low = refs[17:21]
    total, sent, came, held, came_far = refs[21:26]
    more = paired(refs[26:-3])
    links = Links(*refs[-3:])
    n_own = own_in.shape[0]
    cot_load = Joint(
        [load_rearranged(links, far, own_in, cot.at[pl.ds(0, n_own)])]
        + [
            load_rearranged(
                links, far, cot_in.at[pl.ds(i * n_own, n_own)], cot.at[pl.ds((i + 1) * n_own, n_own)]
            )
            for i in range(3)
        ]
    )
    loads = [
        links.copy(src, dst)
        for src, dst in (
            (act_in, act),
            (down_in, down_w),
            (slope_in, slope),
            (n2_in, n2),
            (gu_in, gu_w),
        )
    ]
    greet([CORE, TENSOR] + chips_apart(LOW, *far))
    group, width = cot.shape
    count = group // 4
    down_cols, gu_cols = down_w.shape[1], gu_w.shape[1]
    grads = slope.at[:, pl.ds(0, gu_cols)]
    down_job = (pl.ds(0, down_cols), cot, act)
    gu_job = (pl.ds(down_cols, gu_cols), n2, grads)
    collect = Collect(links, far, width, sent, came, held, came_far, total, more)

    cot_load.wait()
    loads[0].wait()
    upper, lower = list(collect.upper()), list(collect.lower())
    collect.send_half("d", down_job, upper)
    loads[1].wait()
    loads[2].wait()
    lane = lax.broadcasted_iota(jnp.int32, (256, 128), 1)

    def slopes(start):
        span = pl.ds(start, 256)
        grad_act = dot_plain(cot[span], down_w[...])
        gate = grad_act * slope[span, 0:down_cols].astype(F32)
        upward = grad_act * slope[span, down_cols : 2 * down_cols].astype(F32)
        slope[span, 0:main] = gate[:, :main].astype(BF)
        slope[span, main : 2 * main] = upward[:, :main].astype(BF)
        last = jnp.where(lane < 64, gate[:, main:], pltpu.roll(upward[:, main:], 64, 1))
        slope[span, 2 * main : 2 * main + 128] = last.astype(BF)

    by_rows(0, group, 256, slopes)
    loads[3].wait()
    collect.send_half("g", gu_job, upper)

    loads[4].wait()

    def term(slot, span):
        return dot_last(slope[pl.ds(slot * count, count), 0:gu_cols], gu_w[span])

    sums = GroupSum(
        links, count, width, 4, term, part, land, low_part, land_low, summ, across
    )
    sums.outer(3)
    collect.own_half("d", down_job, upper)
    sums.to_low()
    sums.outer(1)
    collect.send_half("d", down_job, lower)
    collect.send_half("g", gu_job, lower)
    collect.own_half("g", gu_job, upper)
    sums.to_half()
    collect.own_half("d", down_job, lower)
    collect.own_half("g", gu_job, lower)
    collect.finish("d", down_job)
    collect.finish("g", gu_job)
    collect.finish_more()
    half_unit = own_out.shape[0]
    low = low_bit()
    own_out[...] = total[pl.ds(pl.multiple_of(low * half_unit, half_unit), half_unit)]
    other_out[...] = total[
        pl.ds(pl.multiple_of((1 - low) * half_unit, half_unit), half_unit)
    ].astype(BF)
    sums.wait()
    links.close()


def ffn_backward(far, main, own, cot, act, down_w, slope, n2, gu_w):
    group, width = n2.shape
    count = group // 4
    cols = gu_w.shape[1] + down_w.shape[1]
    inputs = (own, cot, act, down_w, slope, n2, gu_w)
    return pl.pallas_call(
        functools.partial(ffn_backward_kernel, far, main),
        in_specs=[ANY] * 7,
        out_specs=[VMEM] * 4,
        out_shape=[
            jax.ShapeDtypeStruct((count, width), BF),
            jax.ShapeDtypeStruct((count, width), BF),
            jax.ShapeDtypeStruct((width // 2 ** (len(far) + 1), cols), F32),
            jax.ShapeDtypeStruct((width // 2 ** (len(far) + 1), cols), BF),
        ],
        scratch_shapes=[pltpu.VMEM((group, width), BF)]
        + [pltpu.VMEM(a.shape, BF) for a in inputs[2:]]
        + group_sum_scratch(count, width)
        + [pltpu.VMEM((width // 4, cols), F32)]
        + collect_scratch(far, width, cols)
        + link_scratch(128, 64),
        compiler_params=pltpu.CompilerParams(
            collective_id=2, has_side_effects=True, vmem_limit_bytes=VMEM_BIG
        ),
        name="ffn_backward",
    )(*inputs)


def finale_kernel(far, micro, *refs):
    (
        gain_rows,
        middle_in,
        cot_in,
        grad_two_in,
        across_two_in,
        hid_in,
        cos_in,
        sin_in,
        kpos,
        rowinfo,
        queries_in,
        lse,
        kvs_in,
        attn_in,
        n1_in,
        mixed_in,
        act_in,
        down_in,
        ffn_own,
        ffn_other,
    ) = refs[:20]
    (
        grad_middle,
        summ,
        across,
        feed,
        feed_across,
        attn_mine,
        attn_came,
        gains,
        ffn_core,
        ffn_low,
        ffn_low_core,
    ) = refs[20:31]
    attn_w, n1, mixed, gmid, raw = refs[31:36]
    dkv_own, dkv_sent, dkv_land, side, land_side = refs[36:41]
    low_sent, low_land = refs[41:43]
    near_gains, far_gains, low_gains, core_gains = refs[43:47]
    part, land, land_low = refs[47:50]
    total, sent, came, held, came_far = refs[50:55]
    queries, kvs, cosine, sine, bias, dk, dv, act, down_w = refs[55:64]
    more = paired(refs[64:-3])
    go = raw.at[:, pl.ds(0, mixed.shape[1])]
    links = Links(*refs[-3:])
    loads = [
        links.copy(src, dst)
        for src, dst in (
            (middle_in, grad_middle),
            (grad_two_in, feed),
            (across_two_in, part),
            (attn_in, attn_w),
            (mixed_in, mixed),
            (n1_in, n1),
        )
    ]
    loads.insert(1, load_rearranged(links, far, cot_in, summ))
    span_chips = kvs_in.shape[0]
    greet([CORE, TENSOR] + chips_apart(LOW, *far) + chips_apart(*range(1, span_chips)))
    count, width = grad_middle.shape
    rows = count // micro
    n_q = queries_in.shape[1]
    n_qkv = n_q + 128
    low, core = low_bit(), core_bit()
    block = ffn_own.shape[0] // 2

    def core_rows(which):
        return pl.ds(pl.multiple_of(which * block, block), block)

    ffn_flight = [
        links.push(ffn_other, ffn_low, peer(LOW)),
        links.push(ffn_own.at[core_rows(1 - core)], ffn_core, peer(core=True)),
    ]

    feed_loads = [links.copy(act_in, act), links.copy(down_in, down_w)]

    for load in loads[:4]:
        load.wait()
    near_gains[...] = jnp.zeros_like(near_gains)

    def second_norm(start):
        span = pl.ds(start, 64)
        grad = feed[span].astype(F32) + part[span].astype(F32)
        value = grad_middle[span]
        ratio = lax.rsqrt(jnp.mean(value * value, axis=-1, keepdims=True) + epsilon)
        turned = value * ratio
        near_gains[1:2] += jnp.sum(grad * turned, axis=0, keepdims=True)
        scaled = grad * gain_rows[1:2]
        inner = jnp.mean(scaled * turned, axis=-1, keepdims=True)
        result = summ[span].astype(F32) + ratio * (scaled - turned * inner)
        grad_middle[span] = result
        gmid[span] = result.astype(BF)

    by_rows(0, count, 64, second_norm)
    own = links.push(gmid.at[pl.ds(0, count)], gmid.at[pl.ds(count, count)], peer(core=True))
    collect = Collect(links, far, width, sent, came, held, came_far, total, more)
    out_job = (pl.ds(n_qkv, n_q), gmid, mixed)
    q_job = (pl.ds(0, n_q), n1, go)
    kv_job = (pl.ds(n_q, 128), n1, raw.at[:, pl.ds(n_q, 128)])
    jobs = (("o", out_job), ("q", q_job), ("v", kv_job))
    upper, lower = list(collect.upper()), list(collect.lower())
    loads[4].wait()
    loads[5].wait()

    def mixed_back(start):
        span = pl.ds(start, 128)
        go[span] = dot_plain(gmid[span], attn_w[:, n_qkv : n_qkv + n_q]).astype(BF)

    by_rows(0, count, 128, mixed_back)
    own.wait_recv()
    by_rows(count, count, 128, mixed_back)
    collect.send_half("o", out_job, upper)
    collect.send_half("o", out_job, lower)

    def term(slot, span):
        return dot_last(act[pl.ds(slot * count, count)], down_w[span])

    sums = GroupSum(
        links, count, width, 4, term, part, land, side, land_low, feed, feed_across
    )
    for load in feed_loads:
        load.wait()
    sums.outer(3)
    sums.to_low([0, 1])
    sums.outer(1)

    def attention():
        scoped = [
            links.copy(src, dst)
            for src, dst in (
                (queries_in, queries),
                (kvs_in, kvs),
                (cos_in, cosine),
                (sin_in, sine),
            )
        ]
        for load in scoped:
            load.wait()
        def one(m, carry):
            mine = pl.ds(pl.multiple_of(m * rows, rows), rows)
            other = pl.ds(pl.multiple_of(count + m * rows, rows), rows)
            bias[...] = mask_bias(kpos[...], rowinfo[m])

            def both(ref):
                return jnp.concatenate([ref[mine], ref[other]], axis=0)

            kv = jnp.concatenate(
                [kvs[key, span] for key in range(span_chips) for span in (mine, other)], axis=0
            )
            grad_q = attend_back(bias, both(queries), both(go), lse[m], kv, dk, dv)
            grad_q = turn(grad_q, both(cosine), both(sine), True).astype(BF)
            raw[mine, 0:n_q] = grad_q[:rows]
            raw[other, 0:n_q] = grad_q[rows:]
            for key in range(span_chips):
                for place, span in ((0, mine), (rows, other)):
                    at = pl.ds(key * 2 * rows + place, rows)
                    pair = jnp.concatenate([dk[at], dv[at]], axis=1)
                    if key == 0:
                        dkv_own[span] = pair
                    else:
                        dkv_sent[key - 1, span] = pair.astype(BF)
            return carry

        lax.fori_loop(0, micro, one, 0)
        flight = [
            links.push(dkv_sent.at[key - 1], dkv_land.at[key - 1], peer(key))
            for key in range(1, span_chips)
        ]
        for load in loads[6:]:
            load.wait()
        collect.send_half("q", q_job, upper)
        collect.own_half("o", out_job, upper)
        collect.send_half("q", q_job, lower)
        sums.to_half([0, 1])
        for copy in flight:
            copy.wait_recv()

        def key_values(start):
            span = pl.ds(start, 256)
            pair = dkv_own[span]
            for key in range(span_chips - 1):
                pair = pair + dkv_land[key, span].astype(F32)
            lane = lax.broadcasted_iota(jnp.int32, pair.shape, 1)
            turned = turn(pair, cosine[span], sine[span], True)
            raw[span, n_q:n_qkv] = jnp.where(lane < HEAD_DIM, turned, pair).astype(BF)

        by_rows(0, 2 * count, 256, key_values)

    attention()

    collect.send_half("v", kv_job, upper)
    collect.send_half("v", kv_job, lower)
    links.settle([sums.flight["low", i] for i in range(2)])
    spans = [pl.ds(i * (width // 4), width // 4) for i in range(4)]
    to_core = []
    for span in spans:
        side[:, span] = dot_last(raw[pl.ds(count, count)], attn_w[span, 0:n_qkv]).astype(BF)
        to_core.append(links.push(side.at[:, span], land_side.at[:, span], peer(core=True)))
    over = []
    for i, span in enumerate(spans):
        value = dot_last(raw[pl.ds(0, count)], attn_w[span, 0:n_qkv])
        to_core[i].wait_recv()
        summ[:, span] = (value + land_side[:, span].astype(F32)).astype(BF)
        over.append(links.push(summ.at[:, span], across.at[:, span], peer(tensor=True)))
    load_hid = load_rearranged(links, far, hid_in, land_side)

    for name, job in jobs[1:]:
        collect.own_half(name, job, upper)
    links.settle(to_core)
    sums.to_low([2, 3])
    half_unit = attn_mine.shape[0] * 2

    def low_rows(which):
        return pl.ds(pl.multiple_of(which * half_unit, half_unit), half_unit)

    low_flight = {}

    def to_low(name, job):
        columns = job[0]
        low_sent[:, columns] = total[low_rows(1 - low), columns].astype(BF)
        low_flight[name] = links.push(low_sent.at[:, columns], low_land.at[:, columns], peer(LOW))

    collect.own_half("o", out_job, lower)
    collect.finish("o", out_job)
    if not collect.more:
        to_low("o", out_job)
    for name, job in jobs[1:]:
        collect.own_half(name, job, lower)
    for name, job in jobs[1:]:
        collect.finish(name, job)
        if not collect.more:
            to_low(name, job)
    if collect.more:
        collect.finish_more()
        for name, job in jobs:
            to_low(name, job)

    for copy in over:
        copy.wait_recv()
    load_hid.wait()

    def first_norm(start):
        span = pl.ds(start, 64)
        value = land_side[span].astype(F32)
        ratio = lax.rsqrt(jnp.mean(value * value, axis=-1, keepdims=True) + epsilon)
        grad = summ[span].astype(F32) + across[span].astype(F32)
        turned = value * ratio
        near_gains[0:1] += jnp.sum(grad * turned, axis=0, keepdims=True)
        scaled = grad * gain_rows[0:1]
        inner = jnp.mean(scaled * turned, axis=-1, keepdims=True)
        grad_middle[span] = grad_middle[span] + ratio * (scaled - turned * inner)

    by_rows(0, count, 64, first_norm)
    kept, base = width, 0
    for bit in far[::-1]:
        kept //= 2
        landed = far_gains.at[:, pl.ds(base, kept)]
        copy = links.push(near_gains.at[:, pl.ds(kept, kept)], landed, peer(bit))
        if base == 0:
            sums.to_half([2, 3])
        copy.wait_recv()
        near_gains[:, 0:kept] = near_gains[:, 0:kept] + landed[...]
        base += kept
    copy = links.push(near_gains.at[:, pl.ds(0, kept)], low_gains, peer(LOW))
    ffn_flight[0].wait_recv()
    ffn_flight.append(
        links.push(ffn_low.at[core_rows(1 - core)], ffn_low_core, peer(core=True))
    )
    copy.wait_recv()
    gains[...] = near_gains[:, 0:kept] + low_gains[...]
    copy = links.push(gains, core_gains, peer(core=True))

    core_flight = []
    for name, job in jobs:
        columns = job[0]
        low_flight[name].wait_recv()
        total[0:half_unit, columns] = total[low_rows(low), columns] + low_land[:, columns].astype(
            F32
        )
        core_flight.append(
            links.push(
                total.at[core_rows(1 - core), columns], attn_came.at[:, columns], peer(core=True)
            )
        )
        attn_mine[:, columns] = total[core_rows(core), columns]
    copy.wait_recv()
    for flight in core_flight:
        flight.wait_recv()
    for flight in ffn_flight[1:]:
        flight.wait_recv()
    sums.wait()
    links.close()
    gains[...] = gains[...] + core_gains[...]


def finale(far, micro, inputs):
    (
        gain_rows,
        middle,
        cot,
        grad_two,
        across_two,
        hid,
        cosine,
        sine,
        kpos,
        rowinfo,
        queries,
        lse,
        kvs,
        attn_w,
        n1,
        mixed,
        act,
        down_w,
        ffn_own,
        ffn_other,
    ) = inputs
    count, width = middle.shape
    n_q = mixed.shape[1]
    attn_cols, ffn_cols = attn_w.shape[1], ffn_own.shape[1]
    unit = width // 2 ** len(far)
    block = unit // 4
    span_chips = kvs.shape[0]

    def shape(dtype, *dims):
        return jax.ShapeDtypeStruct(dims, dtype)

    rows = shape(BF, count, width)
    any_or_vmem = [VMEM] + [ANY] * 7 + [VMEM] * 2 + [ANY] + [VMEM] + [ANY] * 8
    return pl.pallas_call(
        functools.partial(finale_kernel, far, micro),
        in_specs=any_or_vmem,
        out_specs=[VMEM] * 6 + [ANY, VMEM] + [ANY] * 3,
        out_shape=[
            shape(F32, count, width),
            rows,
            rows,
            rows,
            rows,
            shape(F32, block, attn_cols),
            shape(F32, block, attn_cols),
            shape(F32, 8, unit),
            shape(F32, block, ffn_cols),
            shape(BF, 2 * block, ffn_cols),
            shape(BF, block, ffn_cols),
        ],
        scratch_shapes=[
            pltpu.VMEM((width, attn_cols), BF),
            pltpu.VMEM((2 * count, width), BF),
            pltpu.VMEM((2 * count, n_q), BF),
            pltpu.VMEM((2 * count, width), BF),
            pltpu.VMEM((2 * count, n_q + 128), BF),
            pltpu.VMEM((2 * count, 128), F32),
            pltpu.VMEM((span_chips - 1, 2 * count, 128), BF),
            pltpu.VMEM((span_chips - 1, 2 * count, 128), BF),
            pltpu.VMEM((count, width), BF),
            pltpu.VMEM((count, width), BF),
            pltpu.VMEM((2 * block, attn_cols), BF),
            pltpu.VMEM((2 * block, attn_cols), BF),
            pltpu.VMEM((8, width), F32),
            pltpu.VMEM((8, width), F32),
            pltpu.VMEM((8, unit), F32),
            pltpu.VMEM((8, unit), F32),
        ]
        + group_sum_scratch(count, width)[:3]
        + [pltpu.VMEM((width // 4, attn_cols), F32)]
        + collect_scratch(far, width, attn_cols)[:4]
        + [
            pltpu.VMEM(queries.shape, BF),
            pltpu.VMEM(kvs.shape, BF),
            pltpu.VMEM(cosine.shape, F32),
            pltpu.VMEM(sine.shape, F32),
            pltpu.VMEM((kpos.shape[0], rowinfo.shape[2]), F32),
            pltpu.VMEM((kpos.shape[0], HEAD_DIM), F32),
            pltpu.VMEM((kpos.shape[0], HEAD_DIM), F32),
            pltpu.VMEM(act.shape, BF),
            pltpu.VMEM(down_w.shape, BF),
        ]
        + collect_scratch(far, width, attn_cols)[4:]
        + link_scratch(192, 64),
        compiler_params=pltpu.CompilerParams(
            collective_id=3, has_side_effects=True, vmem_limit_bytes=VMEM_BIG
        ),
        name="finale",
    )(*inputs)


def restore_kernel(places, middle, feed, feed_across, grad, output, grad_out):
    value = middle[...] + (feed[...].astype(F32) + feed_across[...].astype(F32))
    output[...] = value.astype(BF)
    grad_out[...] = grad[...]


def restore(places, block, middle, feed, feed_across, grad):
    count, width = middle.shape
    moved = pl.BlockSpec((count, block), lambda i, places: (0, places[i]))
    kept = pl.BlockSpec((count, block), lambda i, places: (0, i))
    return pl.pallas_call(
        restore_kernel,
        grid_spec=pltpu.PrefetchScalarGridSpec(
            num_scalar_prefetch=1,
            grid=(width // block,),
            in_specs=[moved] * 4,
            out_specs=[kept] * 2,
        ),
        out_shape=[
            jax.ShapeDtypeStruct((count, width), BF),
            jax.ShapeDtypeStruct((count, width), F32),
        ],
        compiler_params=pltpu.CompilerParams(vmem_limit_bytes=VMEM_LIMIT),
        name="restore",
    )(places, middle, feed, feed_across, grad)


def body(
    tokens,
    doc_position,
    attn_gain,
    w_query,
    w_key,
    w_value,
    w_out,
    ffn_gain,
    w_gate,
    w_up,
    w_down,
    cotangent,
):
    size = lax.axis_size("dp")
    chips = size // 2
    far = [1 << place for place in range(chips.bit_length() - 1) if 1 << place != LOW][::-1]
    me = lax.axis_index("dp")
    core = me % 2
    chip = me // 2
    low = (chip // LOW) % 2
    micro, stretch, width = tokens.shape
    count = micro * stretch
    block = width // chips
    own_block = block // 2
    span_chips = SEQ_LEN // (2 * stretch)
    in_span = chip % span_chips

    keys = [0]
    for bit in far:
        keys = keys + [key | bit for key in keys]

    def rearranged(array):
        base = chip - LOW * low
        return jnp.concatenate(
            [
                lax.dynamic_slice_in_dim(
                    array, ((base ^ key) + LOW * side) * block, block, array.ndim - 1
                )
                for key in keys
                for side in range(2)
            ],
            axis=-1,
        )

    unit_of = jnp.array([keys.index(other & ~LOW) for other in range(chips)], jnp.int32)
    naturals = jnp.arange(chips, dtype=jnp.int32)
    places = unit_of[chip ^ naturals] * 2 + (naturals // LOW) % 2

    def restored(array):
        return jnp.concatenate(
            [
                lax.dynamic_slice_in_dim(array, places[natural] * block, block, array.ndim - 1)
                for natural in range(chips)
            ],
            axis=-1,
        )

    def halves(array):
        n = array.shape[1] // 2
        return array[:, :n], array[:, n:]

    attn_pack = jnp.concatenate(
        [
            halves(w)[side]
            for side in range(2)
            for w in (w_query, w_key, w_value, w_out.T)
        ],
        axis=1,
    )
    hidden_units = w_gate.shape[1] // 4
    main = hidden_units // 128 * 128
    rest = hidden_units - main
    assert rest == 64

    def mains(array, place):
        return array[:, place * main : (place + 1) * main]

    def rests(array, place):
        return array[:, 4 * main + place * rest : 4 * main + (place + 1) * rest]

    w_down_t = w_down.T
    empty = jnp.zeros((own_block, 128 - rest), BF)
    ffn_pack = jnp.concatenate(
        [
            piece
            for place in range(4)
            for piece in (
                mains(w_gate, place),
                mains(w_up, place),
                rests(w_gate, place),
                rests(w_up, place),
                mains(w_down_t, place),
                rests(w_down_t, place),
                empty,
            )
        ],
        axis=1,
    )
    gain_pack = jnp.zeros((16, 128), BF).at[0, :own_block].set(attn_gain)
    gain_pack = gain_pack.at[1, :own_block].set(ffn_gain)
    hidden = tokens.reshape(count, width)
    grad_final = cotangent.reshape(count, width)
    if block % 128:
        hidden, grad_final = rearranged(hidden), rearranged(grad_final)

    position_both = jnp.stack([doc_position, swap_core(doc_position)])

    power = jnp.arange(HEAD_DIM // 2, dtype=F32) * (2.0 / HEAD_DIM)
    inverse = 10000.0 ** (-power)
    turned = position_both.reshape(2 * count).astype(F32)[:, None] * jnp.tile(inverse, 4)[None, :]
    cosine, sine = jnp.cos(turned), jnp.sin(turned)

    inner = jnp.arange(2 * stretch, dtype=jnp.int32) ^ (core * stretch)
    row_place = in_span * (2 * stretch) + inner
    kpos = jnp.concatenate(
        [(in_span ^ key) * (2 * stretch) + inner for key in range(span_chips)]
    ).reshape(-1, 1)
    row_position = position_both.transpose(1, 0, 2).reshape(micro, 2 * stretch)
    row_places = jnp.broadcast_to(row_place[None, :], row_position.shape)
    rowinfo = jnp.stack([row_places, row_places - row_position], axis=1)

    n_q = w_query.shape[1] // 2
    n_kv = w_key.shape[1] // 2
    n_qkv = n_q + 2 * n_kv
    (
        gain_rows,
        lse,
        middle,
        activated,
        slopes,
        mixed,
        queries,
        kvs,
        normed,
        attn_w,
        normed_two,
        gu_w,
        down_wt,
        grad_final_others,
    ) = forward(
        far,
        main,
        micro,
        span_chips,
        (gain_pack, attn_pack, ffn_pack, hidden, grad_final),
        (cosine, sine, kpos, rowinfo),
    )
    gain_one, gain_two = gain_rows[0:1], gain_rows[1:2]
    grad_two, grad_two_across, ffn_own, ffn_other = ffn_backward(
        far, main, grad_final, grad_final_others, activated, down_wt, slopes, normed_two, gu_w
    )
    (
        grad_hidden,
        _,
        _,
        feed,
        feed_across,
        attn_mine,
        attn_came,
        grad_gains,
        ffn_core,
        ffn_low,
        ffn_low_core,
    ) = finale(
        far,
        micro,
        (
            gain_rows,
            middle,
            grad_final,
            grad_two,
            grad_two_across,
            hidden,
            cosine,
            sine,
            kpos,
            rowinfo,
            queries,
            lse,
            kvs,
            attn_w,
            normed,
            mixed,
            activated,
            down_wt,
            ffn_own,
            ffn_other,
        ),
    )
    if block % 128:
        output = restored((middle + (feed.astype(F32) + feed_across.astype(F32))).astype(BF))
        grad_tokens = restored(grad_hidden)
    else:
        output, grad_tokens = restore(places, block, middle, feed, feed_across, grad_hidden)
    grad_gains = lax.dynamic_slice_in_dim(grad_gains, (2 * low + core) * own_block, own_block, 1)

    def picked(pair, side):
        return jnp.where(side == 0, pair[0], pair[1]), jnp.where(side == 0, pair[1], pair[0])

    parts = picked((attn_mine, attn_came), core)

    def columns(start, stop):
        return jnp.concatenate([part[:, start:stop] for part in parts], axis=1)

    grad_w_query = columns(0, n_q)
    grad_w_key = columns(n_q, n_q + n_kv)
    grad_w_value = columns(n_q + n_kv, n_qkv)
    grad_w_out = columns(n_qkv, n_qkv + n_q).T

    def own_rows(array):
        return lax.dynamic_slice_in_dim(array, core * own_block, own_block, 0)

    mine_low = picked((own_rows(ffn_own), ffn_core), core)
    other_low = picked((own_rows(ffn_low).astype(F32), ffn_low_core.astype(F32)), core)
    by_low = [
        picked((mine_low[side], other_low[side]), low) for side in range(2)
    ]
    places = [by_low[place % 2][place // 2] for place in range(4)]
    down_cols = main + 128
    gu = down_cols

    def gathered(main_start, rest_start):
        return jnp.concatenate(
            [part[:, main_start : main_start + main] for part in places]
            + [part[:, rest_start : rest_start + rest] for part in places],
            axis=1,
        )

    grad_w_down = gathered(0, main).T
    grad_w_gate = gathered(gu, gu + 2 * main)
    grad_w_up = gathered(gu + main, gu + 2 * main + rest)
    return (
        output.reshape(tokens.shape),
        grad_tokens.reshape(tokens.shape),
        grad_gains[0],
        grad_w_query,
        grad_w_key,
        grad_w_value,
        grad_w_out,
        grad_gains[1],
        grad_w_gate,
        grad_w_up,
        grad_w_down,
    )


def solution(mesh):
    return jax.shard_map(
        body,
        mesh=mesh,
        in_specs=(
            P(None, "dp", None),
            P(None, "dp"),
            P("dp"),
            P("dp", "tensor"),
            P("dp", "tensor"),
            P("dp", "tensor"),
            P("tensor", "dp"),
            P("dp"),
            P("dp", "tensor"),
            P("dp", "tensor"),
            P("tensor", "dp"),
            P(None, "dp", None),
        ),
        out_specs=(
            P(None, "dp", None),
            P(None, "dp", None),
            P("dp"),
            P("dp", "tensor"),
            P("dp", "tensor"),
            P("dp", "tensor"),
            P("tensor", "dp"),
            P("dp"),
            P("dp", "tensor"),
            P("dp", "tensor"),
            P("tensor", "dp"),
        ),
        check_vma=False,
    )
```

```python
import functools

import jax
import jax.numpy as jnp
from jax import lax
from jax.experimental import pallas as pl
from jax.experimental.pallas import tpu as pltpu
from jax.sharding import PartitionSpec as P

HEAD_DIM = 64
SEQ_LEN = 1024
BF = jnp.bfloat16
F32 = jnp.float32
epsilon = 1e-05
VMEM_LIMIT = 48 * 1024 * 1024
VMEM_BIG = 62 * 1024 * 1024


LOW = 2


def swap_core(block):
    size = lax.axis_size("dp")
    return lax.ppermute(block, "dp", [(i, i ^ 1) for i in range(size)])


def swap_chip(block, distance):
    size = lax.axis_size("dp")
    return lax.ppermute(block, "dp", [(i, i ^ (2 * distance)) for i in range(size)])


def flipped(index, distance):
    return index + distance * (1 - 2 * ((index // distance) % 2))


def peer(distance=0, core=False, tensor=False):
    place = lax.axis_index("dp")
    bit = 1
    while bit <= distance:
        if distance & bit:
            place = flipped(place, 2 * bit)
        bit *= 2
    if core:
        place = flipped(place, 1)
    half = lax.axis_index("tensor")
    if tensor:
        half = 1 - half
    return (place, half)


def greet(peers):
    barrier = pltpu.get_barrier_semaphore()
    for name in sorted(set(peers)):
        pl.semaphore_signal(
            barrier, inc=1, device_id=peer(*name), device_id_type=pl.DeviceIdType.MESH
        )
    pl.semaphore_wait(barrier, len(set(peers)))


CORE = (0, True, False)
TENSOR = (0, False, True)


def chips_apart(*distances):
    return [(distance, False, False) for distance in distances]


class Links:
    def __init__(self, send, recv, local):
        self.send, self.recv, self.local = send, recv, local
        self.used = 0
        self.used_local = 0
        self.sent = []

    def push(self, src, dst, device):
        copy = pltpu.make_async_remote_copy(
            src_ref=src,
            dst_ref=dst,
            send_sem=self.send.at[self.used],
            recv_sem=self.recv.at[self.used],
            device_id=device,
            device_id_type=pl.DeviceIdType.MESH,
        )
        self.used += 1
        copy.start()
        self.sent.append(copy)
        return copy

    def copy(self, src, dst):
        copy = pltpu.make_async_copy(src, dst, self.local.at[self.used_local])
        self.used_local += 1
        copy.start()
        return copy

    def settle(self, copies):
        for copy in copies:
            copy.wait_send()
            self.sent = [other for other in self.sent if other is not copy]

    def close(self):
        for copy in self.sent:
            copy.wait_send()


def link_scratch(copies, locals_):
    return [
        pltpu.SemaphoreType.DMA((copies,)),
        pltpu.SemaphoreType.DMA((copies,)),
        pltpu.SemaphoreType.DMA((locals_,)),
    ]


class Joint:
    def __init__(self, copies):
        self.copies = copies

    def wait(self):
        for copy in self.copies:
            copy.wait()


def block_start(far, unit, side, block):
    place = lax.axis_index("dp") // 2
    place = place - LOW * ((place // LOW) % 2) + LOW * side
    for level, bit in enumerate(far):
        if (unit // 2**level) % 2:
            place = flipped(place, bit)
    return pl.multiple_of(place * block, block)


def load_rearranged(links, far, src, dst):
    units = 2 ** len(far)
    block = src.shape[1] // (2 * units)
    if block % 128:
        return links.copy(src, dst)
    copies = []
    for unit in range(units):
        for side in range(2):
            start = block_start(far, unit, side, block)
            copies.append(
                links.copy(
                    src.at[:, pl.ds(start, block)],
                    dst.at[:, pl.ds((2 * unit + side) * block, block)],
                )
            )
    return Joint(copies)


def low_bit():
    return (lax.axis_index("dp") // (2 * LOW)) % 2


def core_bit():
    return lax.axis_index("dp") % 2


def group_rows(height, low, core):
    return pl.ds(pl.multiple_of((low * 2 + core) * height, height), height)


class Spread:
    def __init__(self, links, pieces, dst, height, start, far):
        self.links, self.pieces, self.dst = links, pieces, dst
        self.height, self.start, self.far = height, start, far
        self.cols = sum(cols for _, _, cols in pieces)

    def begin(self):
        low, core = low_bit(), core_bit()
        rows = group_rows(self.height, low, core)
        start = self.start
        self.local, self.stage = [], []
        for src, column, cols in self.pieces:
            mine = self.dst.at[rows, pl.ds(start, cols)]

            def part(low, core, src=src, column=column, cols=cols):
                return src.at[:, pl.ds(pl.multiple_of(column(low, core), 128), cols)]

            self.local.append(self.links.copy(part(low, core), mine))
            self.stage += [
                self.links.push(part(1 - low, core), mine, peer(LOW)),
                self.links.push(part(1 - low, 1 - core), mine, peer(LOW, core=True)),
                self.links.push(part(low, 1 - core), mine, peer(core=True)),
            ]
            start += cols

    def unit(self, index):
        size = 4 * self.height
        return self.dst.at[pl.ds(index * size, size), pl.ds(self.start, self.cols)]

    def pass_on(self, index, first):
        for level in range(first, len(self.far)):
            reached = index + 2**level
            self.arrivals[reached] = self.links.push(
                self.unit(index), self.unit(reached), peer(self.far[level])
            )

    def launch(self):
        for copy in self.stage:
            copy.wait_recv()
        for copy in self.local:
            copy.wait()
        self.arrivals = {}
        self.pass_on(0, 0)

    def forward(self):
        for index in range(1, 2 ** (len(self.far) - 1)):
            self.arrivals.pop(index).wait_recv()
            self.pass_on(index, index.bit_length())

    def finish(self):
        for copy in self.arrivals.values():
            copy.wait_recv()
        self.arrivals = {}


class TokenSpread:
    def __init__(self, links, own, others):
        self.links, self.own, self.others = links, own, others
        self.count = own.shape[0]

    def rows(self, slot, half=None):
        ref = self.others if slot else self.own
        base = (slot - 1) * self.count if slot else 0
        if half is None:
            return ref.at[pl.ds(base, self.count)]
        size = self.count // 2
        return ref.at[pl.ds(pl.multiple_of(base + half * size, size), size)]

    def begin(self):
        half = lax.axis_index("tensor")
        self.side = self.links.push(self.rows(0), self.rows(1), peer(core=True))
        self.low = self.links.push(self.rows(0, half), self.rows(2, half), peer(LOW))

    def second(self):
        half = lax.axis_index("tensor")
        self.low.wait_recv()
        self.across = self.links.push(self.rows(2, half), self.rows(2, half), peer(tensor=True))
        self.first = self.links.push(self.rows(2, half), self.rows(3, half), peer(core=True))

    def third(self):
        other = 1 - lax.axis_index("tensor")
        self.across.wait_recv()
        self.last = self.links.push(self.rows(2, other), self.rows(3, other), peer(core=True))

    def wait(self):
        self.side.wait_recv()
        self.first.wait_recv()
        self.last.wait_recv()


def cuts(start, tiles, parts):
    edges = [start + tiles * part // parts * 128 for part in range(parts + 1)]
    return [(edges[i], edges[i + 1] - edges[i]) for i in range(parts)]


def by_rows(start, total, step, work):
    def go(i, carry):
        work(pl.multiple_of(start + i * step, step))
        return carry

    lax.fori_loop(0, total // step, go, 0)


ANY = pl.BlockSpec(memory_space=pl.ANY)
VMEM = pl.BlockSpec(memory_space=pltpu.VMEM)


def dot_plain(left, right):
    return jnp.dot(left, right, preferred_element_type=F32)


def dot_first(left, right):
    return lax.dot_general(left, right, (((0,), (0,)), ((), ())), preferred_element_type=F32)


def dot_last(left, right):
    return lax.dot_general(left, right, (((1,), (1,)), ((), ())), preferred_element_type=F32)


def turn(value, cosine, sine, back):
    tiles = []
    lane = lax.broadcasted_iota(jnp.int32, (value.shape[0], 128), 1)
    first = (lane % 64) < 32
    for start in range(0, value.shape[1], 128):
        tile = value[:, start : start + 128]
        up = pltpu.roll(tile, 96, 1)
        down = pltpu.roll(tile, 32, 1)
        if back:
            other = jnp.where(first, up, -down)
        else:
            other = jnp.where(first, -up, down)
        tiles.append(tile * cosine + other * sine)
    return tiles[0] if len(tiles) == 1 else jnp.concatenate(tiles, axis=1)


def mask_bias(kpos, row):
    place, floor = row[0:1, :], row[1:2, :]
    allowed = (kpos <= place) & (kpos >= floor)
    return jnp.where(allowed, 0.0, -1e30).astype(F32)


def attend(bias_ref, queries, kv):
    keys = kv[:, :HEAD_DIM]
    values_t = kv.T[HEAD_DIM:, :]
    parts = []
    sums = []
    for head in range(queries.shape[1] // HEAD_DIM):
        q_head = queries[:, head * HEAD_DIM : (head + 1) * HEAD_DIM]
        scores = dot_last(keys, q_head) + bias_ref[...]
        peak = jnp.max(scores, axis=0, keepdims=True)
        expon = jnp.exp(scores - peak)
        total = jnp.sum(expon, axis=0, keepdims=True)
        parts.append(dot_plain(values_t, expon.astype(BF)) * (1.0 / total))
        sums.append(peak + jnp.log(total))
    return jnp.concatenate(parts, axis=0), jnp.concatenate(sums, axis=0)


def attend_back(bias_ref, queries, grads, lse, kv, dk_ref, dv_ref):
    keys = kv[:, :HEAD_DIM]
    values = kv[:, HEAD_DIM:]
    keys_t = kv.T[:HEAD_DIM, :]
    parts = []
    for head in range(queries.shape[1] // HEAD_DIM):
        q_head = queries[:, head * HEAD_DIM : (head + 1) * HEAD_DIM]
        g_head = grads[:, head * HEAD_DIM : (head + 1) * HEAD_DIM]
        scores = dot_last(keys, q_head) + bias_ref[...]
        probs = jnp.exp(scores - lse[head : head + 1, :])
        grad_probs = dot_last(values, g_head)
        inner = jnp.sum(probs * grad_probs, axis=0, keepdims=True)
        grad_scores = (probs * (grad_probs - inner)).astype(BF)
        grad_values = dot_plain(probs.astype(BF), g_head)
        grad_keys = dot_plain(grad_scores, q_head)
        if head == 0:
            dv_ref[...] = grad_values
            dk_ref[...] = grad_keys
        else:
            dv_ref[...] += grad_values
            dk_ref[...] += grad_keys
        parts.append(dot_plain(keys_t, grad_scores))
    return jnp.concatenate(parts, axis=0).T * HEAD_DIM ** (-0.5)


def silu_parts(gate, upward):
    sigmoid = 1.0 / (1.0 + jnp.exp(-gate))
    silu = gate * sigmoid
    return silu * upward, upward * sigmoid * (1.0 + gate * (1.0 - sigmoid)), silu


def forward_kernel(far, main, micro, *refs):
    gain_src, attn_src, gate_src, up_src, down_src, ends_src, hid_src, cot_src = refs[:8]
    cosine, sine, kpos, rowinfo = refs[8:12]
    (
        gain_rows,
        lse,
        middle,
        act,
        slope,
        mixed,
        queries,
        kvs,
        n1_out,
        attn_out,
        n2_out,
        gu_out,
        down_out,
        cot_out,
    ) = refs[12:26]
    gains, attn_w, gu_w, down_w, hid, n1, n2, bias, ratios, part, land, summ, across = refs[26:39]
    links = Links(*refs[39:])
    count = hid_src.shape[0]
    rows = count // micro
    span_chips = kvs.shape[0]
    greet(
        [CORE, TENSOR, (LOW, True, False)] + chips_apart(LOW, *far) + chips_apart(*range(1, span_chips))
    )
    attn_cols, gu_cols, down_cols = attn_w.shape[1], gu_w.shape[1], down_w.shape[1]
    total = gu_cols + down_cols
    height = attn_src.shape[0]

    def core_column(start):
        return lambda low, core: core * attn_cols + start

    def group_column(width, start):
        return lambda low, core: (low * 2 + core) * width + start

    spreads = [
        Spread(links, [(gain_src, lambda low, core: 0, 128)], gains, gain_src.shape[0], 0, far)
    ]
    n_q = queries.shape[1]
    n_qkv = n_q + 128
    for base, tiles, parts in ((0, n_qkv // 128, 2), (n_qkv, n_q // 128, 2)):
        for start, cols in cuts(base, tiles, parts):
            spreads.append(
                Spread(links, [(attn_src, core_column(start), cols)], attn_w, height, start, far)
            )
        if base == 0:
            qkv_spreads = len(spreads)
    attn_spreads = len(spreads)
    first, second = cuts(0, main // 128, 2)
    ends = (ends_src, group_column(256, 0), 128)
    for src, base in ((gate_src, 0), (up_src, main)):
        for start, cols in (first, second):
            pieces = [(src, group_column(main, start), cols)]
            if base and start:
                pieces.append(ends)
            spreads.append(Spread(links, pieces, gu_w, height, base + start, far))
    gu_spreads = len(spreads)
    ends = (ends_src, group_column(256, 128), 128)
    for start, cols in (first, second):
        pieces = [(down_src, group_column(main, start), cols)]
        if start:
            pieces.append(ends)
        spreads.append(Spread(links, pieces, down_w, height, start, far))
    attn = spreads[:attn_spreads]
    gu = spreads[attn_spreads:gu_spreads]
    down = spreads[gu_spreads:]
    for spread in attn:
        spread.begin()
    own_hid = load_rearranged(links, far, hid_src, hid.at[pl.ds(0, count)])
    tokens = TokenSpread(links, cot_src, cot_out)
    own_hid.wait()
    side_hid = links.push(
        hid.at[pl.ds(0, count)], hid.at[pl.ds(count, count)], peer(core=True)
    )
    side_hid.wait_recv()

    def first_ratio(start):
        span = pl.ds(start, 64)
        value = hid[span].astype(F32)
        ratio = lax.rsqrt(jnp.mean(value * value, axis=-1, keepdims=True) + epsilon)
        ratios[span] = jnp.broadcast_to(ratio, (64, 128))

    by_rows(0, 2 * count, 64, first_ratio)
    for spread in attn:
        spread.launch()
    for spread in gu[:2]:
        spread.begin()
    tokens.begin()
    spreads[0].forward()

    spreads[0].finish()
    n_units = 2 ** len(far)
    own_block = gain_rows.shape[1] // (4 * n_units)
    both_gains = gains[...].astype(F32)
    for place in range(4 * n_units):
        gain_rows[0:2, place * own_block : (place + 1) * own_block] = both_gains[
            place * 16 : place * 16 + 2, :own_block
        ]

    def first_norm(start):
        span = pl.ds(start, 64)
        n1[span] = (hid[span].astype(F32) * ratios[span, 0:1] * gain_rows[0:1]).astype(BF)

    by_rows(0, 2 * count, 64, first_norm)
    outs = [links.copy(n1, n1_out)]
    for spread in spreads[1:qkv_spreads]:
        spread.forward()
    for spread in spreads[1:qkv_spreads]:
        spread.finish()

    def project(start):
        span = pl.ds(start, 256)
        raw = dot_plain(n1[span], attn_w[:, 0:n_qkv])
        cos, sin = cosine[span], sine[span]
        queries[span] = (turn(raw[:, :n_q], cos, sin, False) * HEAD_DIM ** (-0.5)).astype(BF)
        pair = raw[:, n_q:]
        lane = lax.broadcasted_iota(jnp.int32, pair.shape, 1)
        kvs[0, span] = jnp.where(lane < HEAD_DIM, turn(pair, cos, sin, False), pair).astype(BF)

    by_rows(0, 2 * count, 256, project)
    came = [
        links.push(kvs.at[0], kvs.at[key], peer(key)) for key in range(1, span_chips)
    ]
    for spread in gu[2:] + down:
        spread.begin()
    gu[0].launch()
    spreads[qkv_spreads].forward()
    gu[1].launch()
    for copy in came:
        copy.wait_recv()

    tokens.second()
    half = []
    for m in range(micro):
        own, other = pl.ds(m * rows, rows), pl.ds(count + m * rows, rows)
        bias[...] = mask_bias(kpos[...], rowinfo[m])
        kv = jnp.concatenate(
            [kvs[key, span] for key in range(span_chips) for span in (own, other)], axis=0
        )
        q_both = jnp.concatenate([queries[own], queries[other]], axis=0)
        mixed_t, sums = attend(bias, q_both, kv)
        lse[m] = sums
        value = mixed_t.T.astype(BF)
        mixed[own] = value[:rows]
        mixed[other] = value[rows:]
        if m == 0:
            for spread in spreads[qkv_spreads + 1 : attn_spreads]:
                spread.forward()
            for spread in spreads[qkv_spreads:attn_spreads]:
                spread.finish()
            outs.append(links.copy(attn_w, attn_out))
        out_w = attn_w.at[:, pl.ds(n_qkv, n_q)]
        term = dot_last(value, out_w[...])
        part[own] = term[rows:].astype(BF)
        side = links.push(part.at[own], land.at[own], peer(core=True))
        side.wait_recv()
        summ[own] = (term[:rows] + land[own].astype(F32)).astype(BF)
        half.append(links.push(summ.at[own], across.at[own], peer(tensor=True)))
        if m == 0:
            for spread in gu[2:]:
                spread.launch()
        if m == 1:
            gu[0].forward()
    for spread in down:
        spread.launch()
    gu[1].forward()
    tokens.third()

    def finish(start):
        span = pl.ds(start, 32)
        value = hid[span].astype(F32) + summ[span].astype(F32) + across[span].astype(F32)
        middle[span] = value
        ratio = lax.rsqrt(jnp.mean(value * value, axis=-1, keepdims=True) + epsilon)
        n2[span] = (value * ratio * gain_rows[1:2]).astype(BF)

    low = []
    for m in range(micro):
        half[m].wait_recv()
        by_rows(m * rows, rows, 32, finish)
        low.append(
            links.push(
                n2.at[pl.ds(m * rows, rows)], n2.at[pl.ds(2 * count + m * rows, rows)], peer(LOW)
            )
        )
    own_n2 = links.push(n2.at[pl.ds(0, count)], n2.at[pl.ds(count, count)], peer(core=True))
    gu[2].forward()
    gu[3].forward()
    for spread in spreads[attn_spreads:gu_spreads]:
        spread.finish()

    def gates(start):
        span = pl.ds(start, 256)
        raw = dot_plain(n2[span], gu_w[...])
        parts = silu_parts(raw[:, :main], raw[:, main : 2 * main])
        last = raw[:, 2 * main :]
        lane = lax.broadcasted_iota(jnp.int32, last.shape, 1)
        ends = silu_parts(last, pltpu.roll(last, 64, 1))
        for ref, base, body, end in (
            (act, 0, parts[0], ends[0]),
            (slope, 0, parts[1], ends[1]),
            (slope, main + 128, parts[2], ends[2]),
        ):
            ref[span, base : base + main] = body.astype(BF)
            ref[span, base + main : base + main + 128] = jnp.where(lane < 64, end, 0.0).astype(BF)

    own_n2.wait_recv()
    by_rows(0, 2 * count, 256, gates)
    for copy in low:
        copy.wait_recv()
    both = links.push(
        n2.at[pl.ds(2 * count, count)], n2.at[pl.ds(3 * count, count)], peer(core=True)
    )
    down[0].forward()
    outs.append(links.copy(gu_w, gu_out))
    both.wait_recv()
    outs.append(links.copy(n2, n2_out))
    by_rows(2 * count, 2 * count, 256, gates)
    down[1].forward()
    for spread in spreads[gu_spreads:]:
        spread.finish()
    outs.append(links.copy(down_w, down_out))
    tokens.wait()
    for copy in outs:
        copy.wait()
    links.close()


def forward(far, main, micro, span_chips, sources, tables):
    gain_pack, attn_pack, _, _, _, _, hidden, _ = sources
    count, width = hidden.shape
    attn_cols = attn_pack.shape[1] // 2
    gu_cols, down_cols = 2 * main + 128, main + 128
    n_q = (attn_cols - 128) // 2
    group = 4 * count
    heads = n_q // HEAD_DIM
    span, tokens = tables[2].shape[0], tables[3].shape[2]

    def low(*shape):
        return jax.ShapeDtypeStruct(shape, BF)

    shapes = [
        jax.ShapeDtypeStruct((8, width), F32),
        jax.ShapeDtypeStruct((micro, heads, tokens), F32),
        jax.ShapeDtypeStruct((count, width), F32),
        low(group, down_cols),
        low(group, 2 * down_cols),
        low(2 * count, n_q),
        low(2 * count, n_q),
        low(span_chips, 2 * count, 128),
        low(2 * count, width),
        low(width, attn_cols),
        low(group, width),
        low(width, gu_cols),
        low(width, down_cols),
        low(3 * count, width),
    ]
    return pl.pallas_call(
        functools.partial(forward_kernel, far, main, micro),
        in_specs=[ANY] * 8 + [VMEM] * 4,
        out_specs=[VMEM] * 8 + [ANY] * 6,
        out_shape=shapes,
        scratch_shapes=[
            pltpu.VMEM((2 ** len(far) * 4 * gain_pack.shape[0], 128), BF),
            pltpu.VMEM((width, attn_cols), BF),
            pltpu.VMEM((width, gu_cols), BF),
            pltpu.VMEM((width, down_cols), BF),
            pltpu.VMEM((2 * count, width), BF),
            pltpu.VMEM((2 * count, width), BF),
            pltpu.VMEM((group, width), BF),
            pltpu.VMEM((span, tokens), F32),
            pltpu.VMEM((2 * count, 128), F32),
        ]
        + [pltpu.VMEM((count, width), BF)] * 4
        + link_scratch(256, 64),
        compiler_params=pltpu.CompilerParams(
            collective_id=0, has_side_effects=True, vmem_limit_bytes=VMEM_BIG
        ),
        name="forward",
    )(*sources, *tables)


class Collect:
    TILE = 256

    def __init__(self, links, far, width, sent, came, held, came_far, total, more):
        self.links, self.far, self.half = links, far, width // 2
        self.sent, self.came, self.held, self.came_far = sent, came, held, came_far
        self.total, self.more = total, more
        self.tiles = self.half // self.TILE
        self.arrivals = {}

    def send_half(self, name, job, which=None):
        columns, left, right = job
        tiles, tile = self.tiles, self.TILE
        if which is None:
            which = [i for i in range(tiles // 2, tiles)] + [i for i in range(tiles // 2)]
        for i in which:
            rows = pl.ds(i * tile, tile)
            start = self.half + i * tile
            self.sent[rows, columns] = dot_first(left[:, start : start + tile], right[...]).astype(
                BF
            )
            self.arrivals[name, i] = self.links.push(
                self.sent.at[rows, columns], self.came.at[rows, columns], peer(self.far[-1])
            )

    def own_half(self, name, job, which):
        columns, left, right = job
        tiles, tile = self.tiles, self.TILE
        for i in which:
            rows = pl.ds(i * tile, tile)
            self.arrivals[name, i].wait_recv()
            term = dot_first(left[:, i * tile : (i + 1) * tile], right[...])
            term = term + self.came[rows, columns].astype(F32)
            if i >= tiles // 2:
                place = pl.ds((i - tiles // 2) * tile, tile)
                self.held[place, columns] = term.astype(BF)
                self.arrivals[name, "far", i - tiles // 2] = self.links.push(
                    self.held.at[place, columns],
                    self.came_far.at[place, columns],
                    peer(self.far[-2]),
                )
            else:
                self.total[rows, columns] = term

    def upper(self):
        return range(self.tiles // 2, self.tiles)

    def lower(self):
        return range(self.tiles // 2)

    def finish(self, name, job):
        columns = job[0]
        for i in self.lower():
            rows = pl.ds(i * self.TILE, self.TILE)
            self.arrivals[name, "far", i].wait_recv()
            self.total[rows, columns] = self.total[rows, columns] + self.came_far[
                rows, columns
            ].astype(F32)

    def finish_more(self):
        kept = self.half // 2
        for bit, (sent, came) in zip(self.far[-3::-1], self.more):
            kept //= 2
            sent[...] = self.total[pl.ds(kept, kept)].astype(BF)
            copy = self.links.push(sent, came, peer(bit))
            copy.wait_recv()
            self.total[pl.ds(0, kept)] = self.total[pl.ds(0, kept)] + came[...].astype(F32)


def collect_scratch(far, width, cols):
    shapes = [
        pltpu.VMEM((width // 2, cols), BF),
        pltpu.VMEM((width // 2, cols), BF),
        pltpu.VMEM((width // 4, cols), BF),
        pltpu.VMEM((width // 4, cols), BF),
    ]
    kept = width // 4
    for _ in far[2:]:
        kept //= 2
        shapes += [pltpu.VMEM((kept, cols), BF)] * 2
    return shapes


def paired(refs):
    return [(refs[i], refs[i + 1]) for i in range(0, len(refs), 2)]


class GroupSum:
    def __init__(self, links, count, width, chunks, term, part, land, low_part, land_low, summ, across):
        self.links, self.count, self.term = links, count, term
        self.part, self.land, self.low_part, self.land_low = part, land, low_part, land_low
        self.summ, self.across = summ, across
        size = width // chunks
        self.spans = [pl.ds(i * size, size) for i in range(chunks)]
        self.flight = {}

    def outer(self, slot):
        rows = pl.ds((slot // 2) * self.count, self.count)
        own = pl.ds(0, self.count)
        if slot == 1:
            self.links.settle([self.flight[3, i] for i in range(len(self.spans))])
        for i, span in enumerate(self.spans):
            self.part[own, span] = self.term(slot, span).astype(BF)
            self.flight[slot, i] = self.links.push(
                self.part.at[own, span], self.land.at[rows, span], peer(core=True)
            )

    def to_low(self, which=None):
        for i, span in enumerate(self.spans):
            if which is not None and i not in which:
                continue
            value = self.term(2, span)
            self.flight[3, i].wait_recv()
            value = value + self.land[pl.ds(self.count, self.count), span].astype(F32)
            self.low_part[:, span] = value.astype(BF)
            self.flight["low", i] = self.links.push(
                self.low_part.at[:, span], self.land_low.at[:, span], peer(LOW)
            )

    def to_half(self, which=None):
        for i, span in enumerate(self.spans):
            if which is not None and i not in which:
                continue
            value = self.term(0, span)
            self.flight["low", i].wait_recv()
            self.flight[1, i].wait_recv()
            value = value + self.land[pl.ds(0, self.count), span].astype(F32)
            value = value + self.land_low[:, span].astype(F32)
            self.summ[:, span] = value.astype(BF)
            self.flight["half", i] = self.links.push(
                self.summ.at[:, span], self.across.at[:, span], peer(tensor=True)
            )

    def wait(self):
        for i in range(len(self.spans)):
            self.flight["half", i].wait_recv()


def group_sum_scratch(count, width):
    return [
        pltpu.VMEM((count, width), BF),
        pltpu.VMEM((2 * count, width), BF),
        pltpu.VMEM((count, width), BF),
        pltpu.VMEM((count, width), BF),
    ]


def ffn_backward_kernel(far, main, *refs):
    own_in, cot_in, act_in, down_in, slope_in, n2_in, gu_in = refs[:7]
    summ, across, own_out, other_out = refs[7:11]
    cot, act, down_w, slope, n2, gu_w = refs[11:17]
    part, land, low_part, land_low = refs[17:21]
    total, sent, came, held, came_far = refs[21:26]
    more = paired(refs[26:-3])
    links = Links(*refs[-3:])
    n_own = own_in.shape[0]
    cot_load = Joint(
        [load_rearranged(links, far, own_in, cot.at[pl.ds(0, n_own)])]
        + [
            load_rearranged(
                links, far, cot_in.at[pl.ds(i * n_own, n_own)], cot.at[pl.ds((i + 1) * n_own, n_own)]
            )
            for i in range(3)
        ]
    )
    loads = [
        links.copy(src, dst)
        for src, dst in (
            (act_in, act),
            (down_in, down_w),
            (slope_in, slope),
            (n2_in, n2),
            (gu_in, gu_w),
        )
    ]
    greet([CORE, TENSOR] + chips_apart(LOW, *far))
    group, width = cot.shape
    count = group // 4
    down_cols, gu_cols = down_w.shape[1], gu_w.shape[1]
    grads = slope.at[:, pl.ds(0, gu_cols)]
    down_job = (pl.ds(0, down_cols), cot, act)
    gu_job = (pl.ds(down_cols, gu_cols), n2, grads)
    collect = Collect(links, far, width, sent, came, held, came_far, total, more)

    cot_load.wait()
    loads[0].wait()
    upper, lower = list(collect.upper()), list(collect.lower())
    collect.send_half("d", down_job, upper)
    loads[1].wait()
    loads[2].wait()
    lane = lax.broadcasted_iota(jnp.int32, (256, 128), 1)

    def slopes(start):
        span = pl.ds(start, 256)
        grad_act = dot_plain(cot[span], down_w[...])
        gate = grad_act * slope[span, 0:down_cols].astype(F32)
        upward = grad_act * slope[span, down_cols : 2 * down_cols].astype(F32)
        slope[span, 0:main] = gate[:, :main].astype(BF)
        slope[span, main : 2 * main] = upward[:, :main].astype(BF)
        last = jnp.where(lane < 64, gate[:, main:], pltpu.roll(upward[:, main:], 64, 1))
        slope[span, 2 * main : 2 * main + 128] = last.astype(BF)

    by_rows(0, group, 256, slopes)
    loads[3].wait()
    collect.send_half("g", gu_job, upper)

    loads[4].wait()

    def term(slot, span):
        return dot_last(slope[pl.ds(slot * count, count), 0:gu_cols], gu_w[span])

    sums = GroupSum(
        links, count, width, 4, term, part, land, low_part, land_low, summ, across
    )
    sums.outer(3)
    collect.own_half("d", down_job, upper)
    sums.to_low()
    sums.outer(1)
    collect.send_half("d", down_job, lower)
    collect.send_half("g", gu_job, lower)
    collect.own_half("g", gu_job, upper)
    sums.to_half()
    collect.own_half("d", down_job, lower)
    collect.own_half("g", gu_job, lower)
    collect.finish("d", down_job)
    collect.finish("g", gu_job)
    collect.finish_more()
    half_unit = own_out.shape[0]
    low = low_bit()
    own_out[...] = total[pl.ds(pl.multiple_of(low * half_unit, half_unit), half_unit)]
    other_out[...] = total[
        pl.ds(pl.multiple_of((1 - low) * half_unit, half_unit), half_unit)
    ].astype(BF)
    sums.wait()
    links.close()


def ffn_backward(far, main, own, cot, act, down_w, slope, n2, gu_w):
    group, width = n2.shape
    count = group // 4
    cols = gu_w.shape[1] + down_w.shape[1]
    inputs = (own, cot, act, down_w, slope, n2, gu_w)
    return pl.pallas_call(
        functools.partial(ffn_backward_kernel, far, main),
        in_specs=[ANY] * 7,
        out_specs=[VMEM] * 4,
        out_shape=[
            jax.ShapeDtypeStruct((count, width), BF),
            jax.ShapeDtypeStruct((count, width), BF),
            jax.ShapeDtypeStruct((width // 2 ** (len(far) + 1), cols), F32),
            jax.ShapeDtypeStruct((width // 2 ** (len(far) + 1), cols), BF),
        ],
        scratch_shapes=[pltpu.VMEM((group, width), BF)]
        + [pltpu.VMEM(a.shape, BF) for a in inputs[2:]]
        + group_sum_scratch(count, width)
        + [pltpu.VMEM((width // 4, cols), F32)]
        + collect_scratch(far, width, cols)
        + link_scratch(128, 64),
        compiler_params=pltpu.CompilerParams(
            collective_id=2, has_side_effects=True, vmem_limit_bytes=VMEM_BIG
        ),
        name="ffn_backward",
    )(*inputs)


def finale_kernel(far, micro, *refs):
    (
        gain_rows,
        middle_in,
        cot_in,
        grad_two_in,
        across_two_in,
        hid_in,
        cos_in,
        sin_in,
        kpos,
        rowinfo,
        queries_in,
        lse,
        kvs_in,
        attn_in,
        n1_in,
        mixed_in,
        act_in,
        down_in,
        ffn_own,
        ffn_other,
    ) = refs[:20]
    (
        grad_middle,
        summ,
        across,
        feed,
        feed_across,
        attn_mine,
        attn_came,
        gains,
        ffn_core,
        ffn_low,
        ffn_low_core,
    ) = refs[20:31]
    attn_w, n1, mixed, gmid, raw = refs[31:36]
    dkv_own, dkv_sent, dkv_land, side, land_side = refs[36:41]
    low_sent, low_land = refs[41:43]
    near_gains, far_gains, low_gains, core_gains = refs[43:47]
    part, land, land_low = refs[47:50]
    total, sent, came, held, came_far = refs[50:55]
    queries, kvs, cosine, sine, bias, dk, dv, act, down_w = refs[55:64]
    more = paired(refs[64:-3])
    go = raw.at[:, pl.ds(0, mixed.shape[1])]
    links = Links(*refs[-3:])
    loads = [
        links.copy(src, dst)
        for src, dst in (
            (middle_in, grad_middle),
            (grad_two_in, feed),
            (across_two_in, part),
            (attn_in, attn_w),
            (mixed_in, mixed),
            (n1_in, n1),
        )
    ]
    loads.insert(1, load_rearranged(links, far, cot_in, summ))
    span_chips = kvs_in.shape[0]
    greet([CORE, TENSOR] + chips_apart(LOW, *far) + chips_apart(*range(1, span_chips)))
    count, width = grad_middle.shape
    rows = count // micro
    n_q = queries_in.shape[1]
    n_qkv = n_q + 128
    low, core = low_bit(), core_bit()
    block = ffn_own.shape[0] // 2

    def core_rows(which):
        return pl.ds(pl.multiple_of(which * block, block), block)

    ffn_flight = [
        links.push(ffn_other, ffn_low, peer(LOW)),
        links.push(ffn_own.at[core_rows(1 - core)], ffn_core, peer(core=True)),
    ]

    feed_loads = [links.copy(act_in, act), links.copy(down_in, down_w)]

    for load in loads[:4]:
        load.wait()
    near_gains[...] = jnp.zeros_like(near_gains)

    def second_norm(start):
        span = pl.ds(start, 64)
        grad = feed[span].astype(F32) + part[span].astype(F32)
        value = grad_middle[span]
        ratio = lax.rsqrt(jnp.mean(value * value, axis=-1, keepdims=True) + epsilon)
        turned = value * ratio
        near_gains[1:2] += jnp.sum(grad * turned, axis=0, keepdims=True)
        scaled = grad * gain_rows[1:2]
        inner = jnp.mean(scaled * turned, axis=-1, keepdims=True)
        result = summ[span].astype(F32) + ratio * (scaled - turned * inner)
        grad_middle[span] = result
        gmid[span] = result.astype(BF)

    by_rows(0, count, 64, second_norm)
    own = links.push(gmid.at[pl.ds(0, count)], gmid.at[pl.ds(count, count)], peer(core=True))
    collect = Collect(links, far, width, sent, came, held, came_far, total, more)
    out_job = (pl.ds(n_qkv, n_q), gmid, mixed)
    q_job = (pl.ds(0, n_q), n1, go)
    kv_job = (pl.ds(n_q, 128), n1, raw.at[:, pl.ds(n_q, 128)])
    jobs = (("o", out_job), ("q", q_job), ("v", kv_job))
    upper, lower = list(collect.upper()), list(collect.lower())
    loads[4].wait()
    loads[5].wait()

    def mixed_back(start):
        span = pl.ds(start, 128)
        go[span] = dot_plain(gmid[span], attn_w[:, n_qkv : n_qkv + n_q]).astype(BF)

    by_rows(0, count, 128, mixed_back)
    own.wait_recv()
    by_rows(count, count, 128, mixed_back)
    collect.send_half("o", out_job, upper)
    collect.send_half("o", out_job, lower)

    def term(slot, span):
        return dot_last(act[pl.ds(slot * count, count)], down_w[span])

    sums = GroupSum(
        links, count, width, 4, term, part, land, side, land_low, feed, feed_across
    )
    for load in feed_loads:
        load.wait()
    sums.outer(3)
    sums.to_low([0, 1])
    sums.outer(1)

    def attention():
        scoped = [
            links.copy(src, dst)
            for src, dst in (
                (queries_in, queries),
                (kvs_in, kvs),
                (cos_in, cosine),
                (sin_in, sine),
            )
        ]
        for load in scoped:
            load.wait()
        def one(m, carry):
            mine = pl.ds(pl.multiple_of(m * rows, rows), rows)
            other = pl.ds(pl.multiple_of(count + m * rows, rows), rows)
            bias[...] = mask_bias(kpos[...], rowinfo[m])

            def both(ref):
                return jnp.concatenate([ref[mine], ref[other]], axis=0)

            kv = jnp.concatenate(
                [kvs[key, span] for key in range(span_chips) for span in (mine, other)], axis=0
            )
            grad_q = attend_back(bias, both(queries), both(go), lse[m], kv, dk, dv)
            grad_q = turn(grad_q, both(cosine), both(sine), True).astype(BF)
            raw[mine, 0:n_q] = grad_q[:rows]
            raw[other, 0:n_q] = grad_q[rows:]
            for key in range(span_chips):
                for place, span in ((0, mine), (rows, other)):
                    at = pl.ds(key * 2 * rows + place, rows)
                    pair = jnp.concatenate([dk[at], dv[at]], axis=1)
                    if key == 0:
                        dkv_own[span] = pair
                    else:
                        dkv_sent[key - 1, span] = pair.astype(BF)
            return carry

        lax.fori_loop(0, micro, one, 0)
        flight = [
            links.push(dkv_sent.at[key - 1], dkv_land.at[key - 1], peer(key))
            for key in range(1, span_chips)
        ]
        for load in loads[6:]:
            load.wait()
        collect.send_half("q", q_job, upper)
        collect.own_half("o", out_job, upper)
        collect.send_half("q", q_job, lower)
        sums.to_half([0, 1])
        for copy in flight:
            copy.wait_recv()

        def key_values(start):
            span = pl.ds(start, 256)
            pair = dkv_own[span]
            for key in range(span_chips - 1):
                pair = pair + dkv_land[key, span].astype(F32)
            lane = lax.broadcasted_iota(jnp.int32, pair.shape, 1)
            turned = turn(pair, cosine[span], sine[span], True)
            raw[span, n_q:n_qkv] = jnp.where(lane < HEAD_DIM, turned, pair).astype(BF)

        by_rows(0, 2 * count, 256, key_values)

    attention()

    collect.send_half("v", kv_job, upper)
    collect.send_half("v", kv_job, lower)
    links.settle([sums.flight["low", i] for i in range(2)])
    spans = [pl.ds(i * (width // 4), width // 4) for i in range(4)]
    to_core = []
    for span in spans:
        side[:, span] = dot_last(raw[pl.ds(count, count)], attn_w[span, 0:n_qkv]).astype(BF)
        to_core.append(links.push(side.at[:, span], land_side.at[:, span], peer(core=True)))
    over = []
    for i, span in enumerate(spans):
        value = dot_last(raw[pl.ds(0, count)], attn_w[span, 0:n_qkv])
        to_core[i].wait_recv()
        summ[:, span] = (value + land_side[:, span].astype(F32)).astype(BF)
        over.append(links.push(summ.at[:, span], across.at[:, span], peer(tensor=True)))
    load_hid = load_rearranged(links, far, hid_in, land_side)

    for name, job in jobs[1:]:
        collect.own_half(name, job, upper)
    links.settle(to_core)
    sums.to_low([2, 3])
    half_unit = attn_mine.shape[0] * 2

    def low_rows(which):
        return pl.ds(pl.multiple_of(which * half_unit, half_unit), half_unit)

    low_flight = {}

    def to_low(name, job):
        columns = job[0]
        low_sent[:, columns] = total[low_rows(1 - low), columns].astype(BF)
        low_flight[name] = links.push(low_sent.at[:, columns], low_land.at[:, columns], peer(LOW))

    collect.own_half("o", out_job, lower)
    collect.finish("o", out_job)
    if not collect.more:
        to_low("o", out_job)
    for name, job in jobs[1:]:
        collect.own_half(name, job, lower)
    for name, job in jobs[1:]:
        collect.finish(name, job)
        if not collect.more:
            to_low(name, job)
    if collect.more:
        collect.finish_more()
        for name, job in jobs:
            to_low(name, job)

    for copy in over:
        copy.wait_recv()
    load_hid.wait()

    def first_norm(start):
        span = pl.ds(start, 64)
        value = land_side[span].astype(F32)
        ratio = lax.rsqrt(jnp.mean(value * value, axis=-1, keepdims=True) + epsilon)
        grad = summ[span].astype(F32) + across[span].astype(F32)
        turned = value * ratio
        near_gains[0:1] += jnp.sum(grad * turned, axis=0, keepdims=True)
        scaled = grad * gain_rows[0:1]
        inner = jnp.mean(scaled * turned, axis=-1, keepdims=True)
        grad_middle[span] = grad_middle[span] + ratio * (scaled - turned * inner)

    by_rows(0, count, 64, first_norm)
    kept, base = width, 0
    for bit in far[::-1]:
        kept //= 2
        landed = far_gains.at[:, pl.ds(base, kept)]
        copy = links.push(near_gains.at[:, pl.ds(kept, kept)], landed, peer(bit))
        if base == 0:
            sums.to_half([2, 3])
        copy.wait_recv()
        near_gains[:, 0:kept] = near_gains[:, 0:kept] + landed[...]
        base += kept
    copy = links.push(near_gains.at[:, pl.ds(0, kept)], low_gains, peer(LOW))
    ffn_flight[0].wait_recv()
    ffn_flight.append(
        links.push(ffn_low.at[core_rows(1 - core)], ffn_low_core, peer(core=True))
    )
    copy.wait_recv()
    gains[...] = near_gains[:, 0:kept] + low_gains[...]
    copy = links.push(gains, core_gains, peer(core=True))

    core_flight = []
    for name, job in jobs:
        columns = job[0]
        low_flight[name].wait_recv()
        total[0:half_unit, columns] = total[low_rows(low), columns] + low_land[:, columns].astype(
            F32
        )
        core_flight.append(
            links.push(
                total.at[core_rows(1 - core), columns], attn_came.at[:, columns], peer(core=True)
            )
        )
        attn_mine[:, columns] = total[core_rows(core), columns]
    copy.wait_recv()
    for flight in core_flight:
        flight.wait_recv()
    for flight in ffn_flight[1:]:
        flight.wait_recv()
    sums.wait()
    links.close()
    gains[...] = gains[...] + core_gains[...]


def finale(far, micro, inputs):
    (
        gain_rows,
        middle,
        cot,
        grad_two,
        across_two,
        hid,
        cosine,
        sine,
        kpos,
        rowinfo,
        queries,
        lse,
        kvs,
        attn_w,
        n1,
        mixed,
        act,
        down_w,
        ffn_own,
        ffn_other,
    ) = inputs
    count, width = middle.shape
    n_q = mixed.shape[1]
    attn_cols, ffn_cols = attn_w.shape[1], ffn_own.shape[1]
    unit = width // 2 ** len(far)
    block = unit // 4
    span_chips = kvs.shape[0]

    def shape(dtype, *dims):
        return jax.ShapeDtypeStruct(dims, dtype)

    rows = shape(BF, count, width)
    any_or_vmem = [VMEM] + [ANY] * 7 + [VMEM] * 2 + [ANY] + [VMEM] + [ANY] * 8
    return pl.pallas_call(
        functools.partial(finale_kernel, far, micro),
        in_specs=any_or_vmem,
        out_specs=[VMEM] * 6 + [ANY, VMEM] + [ANY] * 3,
        out_shape=[
            shape(F32, count, width),
            rows,
            rows,
            rows,
            rows,
            shape(F32, block, attn_cols),
            shape(F32, block, attn_cols),
            shape(F32, 8, unit),
            shape(F32, block, ffn_cols),
            shape(BF, 2 * block, ffn_cols),
            shape(BF, block, ffn_cols),
        ],
        scratch_shapes=[
            pltpu.VMEM((width, attn_cols), BF),
            pltpu.VMEM((2 * count, width), BF),
            pltpu.VMEM((2 * count, n_q), BF),
            pltpu.VMEM((2 * count, width), BF),
            pltpu.VMEM((2 * count, n_q + 128), BF),
            pltpu.VMEM((2 * count, 128), F32),
            pltpu.VMEM((span_chips - 1, 2 * count, 128), BF),
            pltpu.VMEM((span_chips - 1, 2 * count, 128), BF),
            pltpu.VMEM((count, width), BF),
            pltpu.VMEM((count, width), BF),
            pltpu.VMEM((2 * block, attn_cols), BF),
            pltpu.VMEM((2 * block, attn_cols), BF),
            pltpu.VMEM((8, width), F32),
            pltpu.VMEM((8, width), F32),
            pltpu.VMEM((8, unit), F32),
            pltpu.VMEM((8, unit), F32),
        ]
        + group_sum_scratch(count, width)[:3]
        + [pltpu.VMEM((width // 4, attn_cols), F32)]
        + collect_scratch(far, width, attn_cols)[:4]
        + [
            pltpu.VMEM(queries.shape, BF),
            pltpu.VMEM(kvs.shape, BF),
            pltpu.VMEM(cosine.shape, F32),
            pltpu.VMEM(sine.shape, F32),
            pltpu.VMEM((kpos.shape[0], rowinfo.shape[2]), F32),
            pltpu.VMEM((kpos.shape[0], HEAD_DIM), F32),
            pltpu.VMEM((kpos.shape[0], HEAD_DIM), F32),
            pltpu.VMEM(act.shape, BF),
            pltpu.VMEM(down_w.shape, BF),
        ]
        + collect_scratch(far, width, attn_cols)[4:]
        + link_scratch(192, 64),
        compiler_params=pltpu.CompilerParams(
            collective_id=3, has_side_effects=True, vmem_limit_bytes=VMEM_BIG
        ),
        name="finale",
    )(*inputs)


def place_kernel(
    main, where, mine, came, own, own_core, far_low, far_core, query, key, value, out, gate, up, down
):
    block = mine.shape[0]
    n_q = query.shape[1] // 2
    rest = gate.shape[1] // 4 - main
    base = main + 128
    for low in range(2):
        for core in range(2):

            @pl.when((where[0] == low) & (where[1] == core))
            def _():
                rows = pl.ds(core * block, block)
                attn = {core: mine, 1 - core: came}
                for side in range(2):
                    part = attn[side]
                    query[:, side * n_q : (side + 1) * n_q] = part[:, 0:n_q]
                    span = slice(side * HEAD_DIM, (side + 1) * HEAD_DIM)
                    key[:, span] = part[:, n_q : n_q + HEAD_DIM]
                    value[:, span] = part[:, n_q + HEAD_DIM : n_q + 128]
                    out[:, side * n_q : (side + 1) * n_q] = part[:, n_q + 128 : 2 * n_q + 128]
                ffn = {
                    (low, core): own.at[rows],
                    (low, 1 - core): own_core,
                    (1 - low, core): far_low.at[rows],
                    (1 - low, 1 - core): far_core,
                }
                for place in range(4):
                    part = ffn[place // 2, place % 2]
                    for ref, start, last in (
                        (down, 0, main),
                        (gate, base, base + 2 * main),
                        (up, base + main, base + 2 * main + rest),
                    ):
                        ref[:, place * main : (place + 1) * main] = part[
                            :, start : start + main
                        ].astype(F32)
                        ends = 4 * main + place * rest
                        ref[:, ends : ends + rest] = part[:, last : last + rest].astype(F32)


def place_grads(main, where, shapes, parts):
    return pl.pallas_call(
        functools.partial(place_kernel, main),
        in_specs=[pl.BlockSpec(memory_space=pltpu.SMEM)] + [VMEM] * 6,
        out_specs=[VMEM] * 7,
        out_shape=[jax.ShapeDtypeStruct(shape, F32) for shape in shapes],
        compiler_params=pltpu.CompilerParams(vmem_limit_bytes=VMEM_LIMIT),
        name="place_grads",
    )(where, *parts)


def restore_kernel(places, middle, feed, feed_across, grad, output, grad_out):
    value = middle[...] + (feed[...].astype(F32) + feed_across[...].astype(F32))
    output[...] = value.astype(BF)
    grad_out[...] = grad[...]


def restore(places, block, middle, feed, feed_across, grad):
    count, width = middle.shape
    moved = pl.BlockSpec((count, block), lambda i, places: (0, places[i]))
    kept = pl.BlockSpec((count, block), lambda i, places: (0, i))
    return pl.pallas_call(
        restore_kernel,
        grid_spec=pltpu.PrefetchScalarGridSpec(
            num_scalar_prefetch=1,
            grid=(width // block,),
            in_specs=[moved] * 4,
            out_specs=[kept] * 2,
        ),
        out_shape=[
            jax.ShapeDtypeStruct((count, width), BF),
            jax.ShapeDtypeStruct((count, width), F32),
        ],
        compiler_params=pltpu.CompilerParams(vmem_limit_bytes=VMEM_LIMIT),
        name="restore",
    )(places, middle, feed, feed_across, grad)


def body(
    tokens,
    doc_position,
    attn_gain,
    w_query,
    w_key,
    w_value,
    w_out,
    ffn_gain,
    w_gate,
    w_up,
    w_down,
    cotangent,
):
    size = lax.axis_size("dp")
    chips = size // 2
    far = [1 << place for place in range(chips.bit_length() - 1) if 1 << place != LOW][::-1]
    me = lax.axis_index("dp")
    core = me % 2
    chip = me // 2
    low = (chip // LOW) % 2
    micro, stretch, width = tokens.shape
    count = micro * stretch
    block = width // chips
    own_block = block // 2
    span_chips = SEQ_LEN // (2 * stretch)
    in_span = chip % span_chips

    keys = [0]
    for bit in far:
        keys = keys + [key | bit for key in keys]

    def rearranged(array):
        base = chip - LOW * low
        return jnp.concatenate(
            [
                lax.dynamic_slice_in_dim(
                    array, ((base ^ key) + LOW * side) * block, block, array.ndim - 1
                )
                for key in keys
                for side in range(2)
            ],
            axis=-1,
        )

    unit_of = jnp.array([keys.index(other & ~LOW) for other in range(chips)], jnp.int32)
    naturals = jnp.arange(chips, dtype=jnp.int32)
    places = unit_of[chip ^ naturals] * 2 + (naturals // LOW) % 2

    def restored(array):
        return jnp.concatenate(
            [
                lax.dynamic_slice_in_dim(array, places[natural] * block, block, array.ndim - 1)
                for natural in range(chips)
            ],
            axis=-1,
        )

    def halves(array):
        n = array.shape[1] // 2
        return array[:, :n], array[:, n:]

    attn_pack = jnp.concatenate(
        [
            halves(w)[side]
            for side in range(2)
            for w in (w_query, w_key, w_value, w_out.T)
        ],
        axis=1,
    )
    hidden_units = w_gate.shape[1] // 4
    main = hidden_units // 128 * 128
    rest = hidden_units - main
    assert rest == 64

    def rests(array, place):
        return array[:, 4 * main + place * rest : 4 * main + (place + 1) * rest]

    w_down_t = w_down.T
    empty = jnp.zeros((own_block, 128 - rest), BF)
    ends_pack = jnp.concatenate(
        [
            piece
            for place in range(4)
            for piece in (
                rests(w_gate, place),
                rests(w_up, place),
                rests(w_down_t, place),
                empty,
            )
        ],
        axis=1,
    )
    gain_pack = jnp.zeros((16, 128), BF).at[0, :own_block].set(attn_gain)
    gain_pack = gain_pack.at[1, :own_block].set(ffn_gain)
    hidden = tokens.reshape(count, width)
    grad_final = cotangent.reshape(count, width)
    if block % 128:
        hidden, grad_final = rearranged(hidden), rearranged(grad_final)

    position_both = jnp.stack([doc_position, swap_core(doc_position)])

    power = jnp.arange(HEAD_DIM // 2, dtype=F32) * (2.0 / HEAD_DIM)
    inverse = 10000.0 ** (-power)
    turned = position_both.reshape(2 * count).astype(F32)[:, None] * jnp.tile(inverse, 4)[None, :]
    cosine, sine = jnp.cos(turned), jnp.sin(turned)

    inner = jnp.arange(2 * stretch, dtype=jnp.int32) ^ (core * stretch)
    row_place = in_span * (2 * stretch) + inner
    kpos = jnp.concatenate(
        [(in_span ^ key) * (2 * stretch) + inner for key in range(span_chips)]
    ).reshape(-1, 1)
    row_position = position_both.transpose(1, 0, 2).reshape(micro, 2 * stretch)
    row_places = jnp.broadcast_to(row_place[None, :], row_position.shape)
    rowinfo = jnp.stack([row_places, row_places - row_position], axis=1)

    n_q = w_query.shape[1] // 2
    n_kv = w_key.shape[1] // 2
    n_qkv = n_q + 2 * n_kv
    (
        gain_rows,
        lse,
        middle,
        activated,
        slopes,
        mixed,
        queries,
        kvs,
        normed,
        attn_w,
        normed_two,
        gu_w,
        down_wt,
        grad_final_others,
    ) = forward(
        far,
        main,
        micro,
        span_chips,
        (gain_pack, attn_pack, w_gate, w_up, w_down_t, ends_pack, hidden, grad_final),
        (cosine, sine, kpos, rowinfo),
    )
    gain_one, gain_two = gain_rows[0:1], gain_rows[1:2]
    grad_two, grad_two_across, ffn_own, ffn_other = ffn_backward(
        far, main, grad_final, grad_final_others, activated, down_wt, slopes, normed_two, gu_w
    )
    (
        grad_hidden,
        _,
        _,
        feed,
        feed_across,
        attn_mine,
        attn_came,
        grad_gains,
        ffn_core,
        ffn_low,
        ffn_low_core,
    ) = finale(
        far,
        micro,
        (
            gain_rows,
            middle,
            grad_final,
            grad_two,
            grad_two_across,
            hidden,
            cosine,
            sine,
            kpos,
            rowinfo,
            queries,
            lse,
            kvs,
            attn_w,
            normed,
            mixed,
            activated,
            down_wt,
            ffn_own,
            ffn_other,
        ),
    )
    if block % 128:
        output = restored((middle + (feed.astype(F32) + feed_across.astype(F32))).astype(BF))
        grad_tokens = restored(grad_hidden)
    else:
        output, grad_tokens = restore(places, block, middle, feed, feed_across, grad_hidden)
    grad_gains = lax.dynamic_slice_in_dim(grad_gains, (2 * low + core) * own_block, own_block, 1)

    grad_w_query, grad_w_key, grad_w_value, grad_out_t, grad_w_gate, grad_w_up, grad_down_t = (
        place_grads(
            main,
            jnp.stack([low, core]),
            [
                w_query.shape,
                w_key.shape,
                w_value.shape,
                w_out.shape[::-1],
                w_gate.shape,
                w_up.shape,
                w_down.shape[::-1],
            ],
            (attn_mine, attn_came, ffn_own, ffn_core, ffn_low, ffn_low_core),
        )
    )
    grad_w_out, grad_w_down = grad_out_t.T, grad_down_t.T
    return (
        output.reshape(tokens.shape),
        grad_tokens.reshape(tokens.shape),
        grad_gains[0],
        grad_w_query,
        grad_w_key,
        grad_w_value,
        grad_w_out,
        grad_gains[1],
        grad_w_gate,
        grad_w_up,
        grad_w_down,
    )


def solution(mesh):
    return jax.shard_map(
        body,
        mesh=mesh,
        in_specs=(
            P(None, "dp", None),
            P(None, "dp"),
            P("dp"),
            P("dp", "tensor"),
            P("dp", "tensor"),
            P("dp", "tensor"),
            P("tensor", "dp"),
            P("dp"),
            P("dp", "tensor"),
            P("dp", "tensor"),
            P("tensor", "dp"),
            P(None, "dp", None),
        ),
        out_specs=(
            P(None, "dp", None),
            P(None, "dp", None),
            P("dp"),
            P("dp", "tensor"),
            P("dp", "tensor"),
            P("dp", "tensor"),
            P("tensor", "dp"),
            P("dp"),
            P("dp", "tensor"),
            P("dp", "tensor"),
            P("tensor", "dp"),
        ),
        check_vma=False,
    )
```

```python
import functools

import jax
import jax.numpy as jnp
from jax import lax
from jax.experimental import pallas as pl
from jax.experimental.pallas import tpu as pltpu
from jax.sharding import PartitionSpec as P

HEAD_DIM = 64
SEQ_LEN = 1024
BF = jnp.bfloat16
F32 = jnp.float32
epsilon = 1e-05
VMEM_LIMIT = 48 * 1024 * 1024
VMEM_BIG = 62 * 1024 * 1024


LOW = 2


def swap_core(block):
    size = lax.axis_size("dp")
    return lax.ppermute(block, "dp", [(i, i ^ 1) for i in range(size)])


def swap_chip(block, distance):
    size = lax.axis_size("dp")
    return lax.ppermute(block, "dp", [(i, i ^ (2 * distance)) for i in range(size)])


def flipped(index, distance):
    return index + distance * (1 - 2 * ((index // distance) % 2))


def peer(distance=0, core=False, tensor=False):
    place = lax.axis_index("dp")
    bit = 1
    while bit <= distance:
        if distance & bit:
            place = flipped(place, 2 * bit)
        bit *= 2
    if core:
        place = flipped(place, 1)
    half = lax.axis_index("tensor")
    if tensor:
        half = 1 - half
    return (place, half)


def greet(peers):
    barrier = pltpu.get_barrier_semaphore()
    for name in sorted(set(peers)):
        pl.semaphore_signal(
            barrier, inc=1, device_id=peer(*name), device_id_type=pl.DeviceIdType.MESH
        )
    pl.semaphore_wait(barrier, len(set(peers)))


CORE = (0, True, False)
TENSOR = (0, False, True)


def chips_apart(*distances):
    return [(distance, False, False) for distance in distances]


class Links:
    def __init__(self, send, recv, local):
        self.send, self.recv, self.local = send, recv, local
        self.used = 0
        self.used_local = 0
        self.sent = []

    def push(self, src, dst, device):
        copy = pltpu.make_async_remote_copy(
            src_ref=src,
            dst_ref=dst,
            send_sem=self.send.at[self.used],
            recv_sem=self.recv.at[self.used],
            device_id=device,
            device_id_type=pl.DeviceIdType.MESH,
        )
        self.used += 1
        copy.start()
        self.sent.append(copy)
        return copy

    def copy(self, src, dst):
        copy = pltpu.make_async_copy(src, dst, self.local.at[self.used_local])
        self.used_local += 1
        copy.start()
        return copy

    def settle(self, copies):
        for copy in copies:
            copy.wait_send()
            self.sent = [other for other in self.sent if other is not copy]

    def close(self):
        for copy in self.sent:
            copy.wait_send()


def link_scratch(copies, locals_):
    return [
        pltpu.SemaphoreType.DMA((copies,)),
        pltpu.SemaphoreType.DMA((copies,)),
        pltpu.SemaphoreType.DMA((locals_,)),
    ]


class Joint:
    def __init__(self, copies):
        self.copies = copies

    def wait(self):
        for copy in self.copies:
            copy.wait()


def block_start(far, unit, side, block):
    place = lax.axis_index("dp") // 2
    place = place - LOW * ((place // LOW) % 2) + LOW * side
    for level, bit in enumerate(far):
        if (unit // 2**level) % 2:
            place = flipped(place, bit)
    return pl.multiple_of(place * block, block)


def load_rearranged(links, far, src, dst):
    units = 2 ** len(far)
    block = src.shape[1] // (2 * units)
    if block % 128:
        return links.copy(src, dst)
    copies = []
    for unit in range(units):
        for side in range(2):
            start = block_start(far, unit, side, block)
            copies.append(
                links.copy(
                    src.at[:, pl.ds(start, block)],
                    dst.at[:, pl.ds((2 * unit + side) * block, block)],
                )
            )
    return Joint(copies)


def low_bit():
    return (lax.axis_index("dp") // (2 * LOW)) % 2


def core_bit():
    return lax.axis_index("dp") % 2


def group_rows(height, low, core):
    return pl.ds(pl.multiple_of((low * 2 + core) * height, height), height)


class Spread:
    def __init__(self, links, pieces, dst, height, start, far):
        self.links, self.pieces, self.dst = links, pieces, dst
        self.height, self.start, self.far = height, start, far
        self.cols = sum(cols for _, _, cols in pieces)

    def begin(self):
        low, core = low_bit(), core_bit()
        rows = group_rows(self.height, low, core)
        start = self.start
        self.local, self.stage = [], []
        for src, column, cols in self.pieces:
            mine = self.dst.at[rows, pl.ds(start, cols)]

            def part(low, core, src=src, column=column, cols=cols):
                return src.at[:, pl.ds(pl.multiple_of(column(low, core), 128), cols)]

            self.local.append(self.links.copy(part(low, core), mine))
            self.stage += [
                self.links.push(part(1 - low, core), mine, peer(LOW)),
                self.links.push(part(1 - low, 1 - core), mine, peer(LOW, core=True)),
                self.links.push(part(low, 1 - core), mine, peer(core=True)),
            ]
            start += cols

    def unit(self, index):
        size = 4 * self.height
        return self.dst.at[pl.ds(index * size, size), pl.ds(self.start, self.cols)]

    def pass_on(self, index, levels):
        for level in levels:
            reached = index + 2**level
            self.arrivals[reached] = self.links.push(
                self.unit(index), self.unit(reached), peer(self.far[level])
            )

    def launch(self, nearest=True):
        for copy in self.stage:
            copy.wait_recv()
        for copy in self.local:
            copy.wait()
        self.arrivals = {}
        self.pass_on(0, range(len(self.far) - 1))
        if nearest:
            self.launch_nearest()

    def launch_nearest(self):
        self.pass_on(0, [len(self.far) - 1])

    def forward(self):
        for index in range(1, 2 ** (len(self.far) - 1)):
            self.arrivals.pop(index).wait_recv()
            self.pass_on(index, range(index.bit_length(), len(self.far)))

    def finish(self):
        for copy in self.arrivals.values():
            copy.wait_recv()
        self.arrivals = {}


class TokenSpread:
    def __init__(self, links, own, others):
        self.links, self.own, self.others = links, own, others
        self.count = own.shape[0]

    def rows(self, slot, half=None):
        ref = self.others if slot else self.own
        base = (slot - 1) * self.count if slot else 0
        if half is None:
            return ref.at[pl.ds(base, self.count)]
        size = self.count // 2
        return ref.at[pl.ds(pl.multiple_of(base + half * size, size), size)]

    def begin(self):
        half = lax.axis_index("tensor")
        self.side = self.links.push(self.rows(0), self.rows(1), peer(core=True))
        self.low = self.links.push(self.rows(0, half), self.rows(2, half), peer(LOW))

    def second(self):
        half = lax.axis_index("tensor")
        self.low.wait_recv()
        self.across = self.links.push(self.rows(2, half), self.rows(2, half), peer(tensor=True))
        self.first = self.links.push(self.rows(2, half), self.rows(3, half), peer(core=True))

    def third(self):
        other = 1 - lax.axis_index("tensor")
        self.across.wait_recv()
        self.last = self.links.push(self.rows(2, other), self.rows(3, other), peer(core=True))

    def wait(self):
        self.side.wait_recv()
        self.first.wait_recv()
        self.last.wait_recv()


def cuts(start, tiles, parts):
    edges = [start + tiles * part // parts * 128 for part in range(parts + 1)]
    return [(edges[i], edges[i + 1] - edges[i]) for i in range(parts)]


def by_rows(start, total, step, work):
    def go(i, carry):
        work(pl.multiple_of(start + i * step, step))
        return carry

    lax.fori_loop(0, total // step, go, 0)


ANY = pl.BlockSpec(memory_space=pl.ANY)
VMEM = pl.BlockSpec(memory_space=pltpu.VMEM)


def dot_plain(left, right):
    return jnp.dot(left, right, preferred_element_type=F32)


def dot_first(left, right):
    return lax.dot_general(left, right, (((0,), (0,)), ((), ())), preferred_element_type=F32)


def dot_last(left, right):
    return lax.dot_general(left, right, (((1,), (1,)), ((), ())), preferred_element_type=F32)


def turn(value, cosine, sine, back):
    tiles = []
    lane = lax.broadcasted_iota(jnp.int32, (value.shape[0], 128), 1)
    first = (lane % 64) < 32
    for start in range(0, value.shape[1], 128):
        tile = value[:, start : start + 128]
        up = pltpu.roll(tile, 96, 1)
        down = pltpu.roll(tile, 32, 1)
        if back:
            other = jnp.where(first, up, -down)
        else:
            other = jnp.where(first, -up, down)
        tiles.append(tile * cosine + other * sine)
    return tiles[0] if len(tiles) == 1 else jnp.concatenate(tiles, axis=1)


def mask_bias(kpos, row):
    place, floor = row[0:1, :], row[1:2, :]
    allowed = (kpos <= place) & (kpos >= floor)
    return jnp.where(allowed, 0.0, -1e30).astype(F32)


def attend(bias_ref, queries, kv):
    keys = kv[:, :HEAD_DIM]
    values_t = kv.T[HEAD_DIM:, :]
    parts = []
    sums = []
    for head in range(queries.shape[1] // HEAD_DIM):
        q_head = queries[:, head * HEAD_DIM : (head + 1) * HEAD_DIM]
        scores = dot_last(keys, q_head) + bias_ref[...]
        peak = jnp.max(scores, axis=0, keepdims=True)
        expon = jnp.exp(scores - peak)
        total = jnp.sum(expon, axis=0, keepdims=True)
        parts.append(dot_plain(values_t, expon.astype(BF)) * (1.0 / total))
        sums.append(peak + jnp.log(total))
    return jnp.concatenate(parts, axis=0), jnp.concatenate(sums, axis=0)


def attend_back(bias_ref, queries, grads, lse, kv, dk_ref, dv_ref):
    keys = kv[:, :HEAD_DIM]
    values = kv[:, HEAD_DIM:]
    keys_t = kv.T[:HEAD_DIM, :]
    parts = []
    for head in range(queries.shape[1] // HEAD_DIM):
        q_head = queries[:, head * HEAD_DIM : (head + 1) * HEAD_DIM]
        g_head = grads[:, head * HEAD_DIM : (head + 1) * HEAD_DIM]
        scores = dot_last(keys, q_head) + bias_ref[...]
        probs = jnp.exp(scores - lse[head : head + 1, :])
        grad_probs = dot_last(values, g_head)
        inner = jnp.sum(probs * grad_probs, axis=0, keepdims=True)
        grad_scores = (probs * (grad_probs - inner)).astype(BF)
        grad_values = dot_plain(probs.astype(BF), g_head)
        grad_keys = dot_plain(grad_scores, q_head)
        if head == 0:
            dv_ref[...] = grad_values
            dk_ref[...] = grad_keys
        else:
            dv_ref[...] += grad_values
            dk_ref[...] += grad_keys
        parts.append(dot_plain(keys_t, grad_scores))
    return jnp.concatenate(parts, axis=0).T * HEAD_DIM ** (-0.5)


def silu_parts(gate, upward):
    sigmoid = 1.0 / (1.0 + jnp.exp(-gate))
    silu = gate * sigmoid
    return silu * upward, upward * sigmoid * (1.0 + gate * (1.0 - sigmoid)), silu


def forward_kernel(far, main, micro, *refs):
    gain_src, attn_src, gate_src, up_src, down_src, ends_src, hid_src, cot_src = refs[:8]
    cosine, sine, kpos, rowinfo = refs[8:12]
    (
        gain_rows,
        lse,
        middle,
        act,
        slope,
        mixed,
        queries,
        kvs,
        n1_out,
        attn_out,
        n2_out,
        gu_out,
        down_out,
        cot_out,
    ) = refs[12:26]
    gains, attn_w, gu_w, down_w, hid, n1, n2, bias, ratios, part, land, summ, across = refs[26:39]
    links = Links(*refs[39:])
    count = hid_src.shape[0]
    rows = count // micro
    span_chips = kvs.shape[0]
    greet(
        [CORE, TENSOR, (LOW, True, False)] + chips_apart(LOW, *far) + chips_apart(*range(1, span_chips))
    )
    attn_cols, gu_cols, down_cols = attn_w.shape[1], gu_w.shape[1], down_w.shape[1]
    total = gu_cols + down_cols
    height = attn_src.shape[0]

    def core_column(start):
        return lambda low, core: core * attn_cols + start

    def group_column(width, start):
        return lambda low, core: (low * 2 + core) * width + start

    spreads = [
        Spread(links, [(gain_src, lambda low, core: 0, 128)], gains, gain_src.shape[0], 0, far)
    ]
    n_q = queries.shape[1]
    n_qkv = n_q + 128
    for base, tiles, parts in ((0, n_qkv // 128, 2), (n_qkv, n_q // 128, 2)):
        for start, cols in cuts(base, tiles, parts):
            spreads.append(
                Spread(links, [(attn_src, core_column(start), cols)], attn_w, height, start, far)
            )
        if base == 0:
            qkv_spreads = len(spreads)
    attn_spreads = len(spreads)
    first, second = cuts(0, main // 128, 2)
    ends = (ends_src, group_column(256, 0), 128)
    for src, base in ((gate_src, 0), (up_src, main)):
        for start, cols in (first, second):
            pieces = [(src, group_column(main, start), cols)]
            if base and start:
                pieces.append(ends)
            spreads.append(Spread(links, pieces, gu_w, height, base + start, far))
    gu_spreads = len(spreads)
    ends = (ends_src, group_column(256, 128), 128)
    for start, cols in (first, second):
        pieces = [(down_src, group_column(main, start), cols)]
        if start:
            pieces.append(ends)
        spreads.append(Spread(links, pieces, down_w, height, start, far))
    attn = spreads[:attn_spreads]
    gu = spreads[attn_spreads:gu_spreads]
    down = spreads[gu_spreads:]
    for spread in attn:
        spread.begin()
    own_hid = load_rearranged(links, far, hid_src, hid.at[pl.ds(0, count)])
    tokens = TokenSpread(links, cot_src, cot_out)
    own_hid.wait()
    side_hid = links.push(
        hid.at[pl.ds(0, count)], hid.at[pl.ds(count, count)], peer(core=True)
    )
    side_hid.wait_recv()

    def first_ratio(start):
        span = pl.ds(start, 64)
        value = hid[span].astype(F32)
        ratio = lax.rsqrt(jnp.mean(value * value, axis=-1, keepdims=True) + epsilon)
        ratios[span] = jnp.broadcast_to(ratio, (64, 128))

    by_rows(0, 2 * count, 64, first_ratio)
    for spread in attn:
        spread.launch()
    for spread in gu[:2]:
        spread.begin()
    tokens.begin()
    spreads[0].forward()

    spreads[0].finish()
    n_units = 2 ** len(far)
    own_block = gain_rows.shape[1] // (4 * n_units)
    both_gains = gains[...].astype(F32)
    for place in range(4 * n_units):
        gain_rows[0:2, place * own_block : (place + 1) * own_block] = both_gains[
            place * 16 : place * 16 + 2, :own_block
        ]

    def first_norm(start):
        span = pl.ds(start, 64)
        n1[span] = (hid[span].astype(F32) * ratios[span, 0:1] * gain_rows[0:1]).astype(BF)

    by_rows(0, 2 * count, 64, first_norm)
    outs = [links.copy(n1, n1_out)]
    for spread in spreads[1:qkv_spreads]:
        spread.forward()
    for spread in spreads[1:qkv_spreads]:
        spread.finish()

    def project(start):
        span = pl.ds(start, 256)
        raw = dot_plain(n1[span], attn_w[:, 0:n_qkv])
        cos, sin = cosine[span], sine[span]
        queries[span] = (turn(raw[:, :n_q], cos, sin, False) * HEAD_DIM ** (-0.5)).astype(BF)
        pair = raw[:, n_q:]
        lane = lax.broadcasted_iota(jnp.int32, pair.shape, 1)
        kvs[0, span] = jnp.where(lane < HEAD_DIM, turn(pair, cos, sin, False), pair).astype(BF)

    by_rows(0, 2 * count, 256, project)
    came = [
        links.push(kvs.at[0], kvs.at[key], peer(key)) for key in range(1, span_chips)
    ]
    for spread in gu[2:] + down:
        spread.begin()
    gu[0].launch()
    spreads[qkv_spreads].forward()
    gu[1].launch()
    for copy in came:
        copy.wait_recv()

    tokens.second()
    half = []
    for m in range(micro):
        own, other = pl.ds(m * rows, rows), pl.ds(count + m * rows, rows)
        bias[...] = mask_bias(kpos[...], rowinfo[m])
        kv = jnp.concatenate(
            [kvs[key, span] for key in range(span_chips) for span in (own, other)], axis=0
        )
        q_both = jnp.concatenate([queries[own], queries[other]], axis=0)
        mixed_t, sums = attend(bias, q_both, kv)
        lse[m] = sums
        value = mixed_t.T.astype(BF)
        mixed[own] = value[:rows]
        mixed[other] = value[rows:]
        if m == 0:
            for spread in spreads[qkv_spreads + 1 : attn_spreads]:
                spread.forward()
            for spread in spreads[qkv_spreads:attn_spreads]:
                spread.finish()
            outs.append(links.copy(attn_w, attn_out))
        out_w = attn_w.at[:, pl.ds(n_qkv, n_q)]
        term = dot_last(value, out_w[...])
        part[own] = term[rows:].astype(BF)
        side = links.push(part.at[own], land.at[own], peer(core=True))
        side.wait_recv()
        summ[own] = (term[:rows] + land[own].astype(F32)).astype(BF)
        half.append(links.push(summ.at[own], across.at[own], peer(tensor=True)))
        if m == 0:
            for spread in gu[2:]:
                spread.launch()
        if m == 1:
            gu[0].forward()
    gu[1].forward()
    down[0].launch(nearest=False)
    tokens.third()

    def finish(start):
        span = pl.ds(start, 32)
        value = hid[span].astype(F32) + summ[span].astype(F32) + across[span].astype(F32)
        middle[span] = value
        ratio = lax.rsqrt(jnp.mean(value * value, axis=-1, keepdims=True) + epsilon)
        n2[span] = (value * ratio * gain_rows[1:2]).astype(BF)

    tensor = lax.axis_index("tensor")

    def halved(slot, m, which):
        return n2.at[
            pl.ds(pl.multiple_of(slot * count + m * rows + which * (rows // 2), 16), rows // 2)
        ]

    low, passed, sides = [], [], []
    for m in range(micro):
        half[m].wait_recv()
        by_rows(m * rows, rows, 32, finish)
        low.append(links.push(halved(0, m, tensor), halved(2, m, tensor), peer(LOW)))
        if m == 1:
            gu[2].forward()
    own_n2 = links.push(n2.at[pl.ds(0, count)], n2.at[pl.ds(count, count)], peer(core=True))
    down[1].launch(nearest=False)
    for m in range(micro):
        low[m].wait_recv()
        passed.append(links.push(halved(2, m, tensor), halved(2, m, tensor), peer(tensor=True)))
        sides.append(links.push(halved(2, m, tensor), halved(3, m, tensor), peer(core=True)))
        if m == 1:
            gu[3].forward()
            for spread in down:
                spread.launch_nearest()
    for spread in spreads[attn_spreads:gu_spreads]:
        spread.finish()

    def gates(start, size=256):
        span = pl.ds(start, size)
        raw = dot_plain(n2[span], gu_w[...])
        parts = silu_parts(raw[:, :main], raw[:, main : 2 * main])
        last = raw[:, 2 * main :]
        lane = lax.broadcasted_iota(jnp.int32, last.shape, 1)
        ends = silu_parts(last, pltpu.roll(last, 64, 1))
        for ref, base, body, end in (
            (act, 0, parts[0], ends[0]),
            (slope, 0, parts[1], ends[1]),
            (slope, main + 128, parts[2], ends[2]),
        ):
            ref[span, base : base + main] = body.astype(BF)
            ref[span, base + main : base + main + 128] = jnp.where(lane < 64, end, 0.0).astype(BF)

    own_n2.wait_recv()
    by_rows(0, 2 * count, 256, gates)
    for m in range(micro):
        passed[m].wait_recv()
        sides.append(
            links.push(halved(2, m, 1 - tensor), halved(3, m, 1 - tensor), peer(core=True))
        )
    outs.append(links.copy(gu_w, gu_out))
    for copy in sides:
        copy.wait_recv()
    outs.append(links.copy(n2, n2_out))
    by_rows(2 * count, count, 128, functools.partial(gates, size=128))
    down[0].forward()
    by_rows(3 * count, count, 128, functools.partial(gates, size=128))
    down[1].forward()
    for spread in spreads[gu_spreads:]:
        spread.finish()
    outs.append(links.copy(down_w, down_out))
    tokens.wait()
    for copy in outs:
        copy.wait()
    links.close()


def forward(far, main, micro, span_chips, sources, tables):
    gain_pack, attn_pack, _, _, _, _, hidden, _ = sources
    count, width = hidden.shape
    attn_cols = attn_pack.shape[1] // 2
    gu_cols, down_cols = 2 * main + 128, main + 128
    n_q = (attn_cols - 128) // 2
    group = 4 * count
    heads = n_q // HEAD_DIM
    span, tokens = tables[2].shape[0], tables[3].shape[2]

    def low(*shape):
        return jax.ShapeDtypeStruct(shape, BF)

    shapes = [
        jax.ShapeDtypeStruct((8, width), F32),
        jax.ShapeDtypeStruct((micro, heads, tokens), F32),
        jax.ShapeDtypeStruct((count, width), F32),
        low(group, down_cols),
        low(group, 2 * down_cols),
        low(2 * count, n_q),
        low(2 * count, n_q),
        low(span_chips, 2 * count, 128),
        low(2 * count, width),
        low(width, attn_cols),
        low(group, width),
        low(width, gu_cols),
        low(width, down_cols),
        low(3 * count, width),
    ]
    return pl.pallas_call(
        functools.partial(forward_kernel, far, main, micro),
        in_specs=[ANY] * 8 + [VMEM] * 4,
        out_specs=[VMEM] * 8 + [ANY] * 6,
        out_shape=shapes,
        scratch_shapes=[
            pltpu.VMEM((2 ** len(far) * 4 * gain_pack.shape[0], 128), BF),
            pltpu.VMEM((width, attn_cols), BF),
            pltpu.VMEM((width, gu_cols), BF),
            pltpu.VMEM((width, down_cols), BF),
            pltpu.VMEM((2 * count, width), BF),
            pltpu.VMEM((2 * count, width), BF),
            pltpu.VMEM((group, width), BF),
            pltpu.VMEM((span, tokens), F32),
            pltpu.VMEM((2 * count, 128), F32),
        ]
        + [pltpu.VMEM((count, width), BF)] * 4
        + link_scratch(256, 64),
        compiler_params=pltpu.CompilerParams(
            collective_id=0, has_side_effects=True, vmem_limit_bytes=VMEM_BIG
        ),
        name="forward",
    )(*sources, *tables)


class Collect:
    TILE = 256

    def __init__(self, links, far, width, sent, came, held, came_far, total, more):
        self.links, self.far, self.half = links, far, width // 2
        self.sent, self.came, self.held, self.came_far = sent, came, held, came_far
        self.total, self.more = total, more
        self.tiles = self.half // self.TILE
        self.arrivals = {}

    def send_half(self, name, job, which=None):
        columns, left, right = job
        tiles, tile = self.tiles, self.TILE
        if which is None:
            which = [i for i in range(tiles // 2, tiles)] + [i for i in range(tiles // 2)]
        for i in which:
            rows = pl.ds(i * tile, tile)
            start = self.half + i * tile
            self.sent[rows, columns] = dot_first(left[:, start : start + tile], right[...]).astype(
                BF
            )
            self.arrivals[name, i] = self.links.push(
                self.sent.at[rows, columns], self.came.at[rows, columns], peer(self.far[-1])
            )

    def own_half(self, name, job, which):
        columns, left, right = job
        tiles, tile = self.tiles, self.TILE
        for i in which:
            rows = pl.ds(i * tile, tile)
            self.arrivals[name, i].wait_recv()
            term = dot_first(left[:, i * tile : (i + 1) * tile], right[...])
            term = term + self.came[rows, columns].astype(F32)
            if i >= tiles // 2:
                place = pl.ds((i - tiles // 2) * tile, tile)
                self.held[place, columns] = term.astype(BF)
                self.arrivals[name, "far", i - tiles // 2] = self.links.push(
                    self.held.at[place, columns],
                    self.came_far.at[place, columns],
                    peer(self.far[-2]),
                )
            else:
                self.total[rows, columns] = term

    def upper(self):
        return range(self.tiles // 2, self.tiles)

    def lower(self):
        return range(self.tiles // 2)

    def finish(self, name, job):
        columns = job[0]
        for i in self.lower():
            rows = pl.ds(i * self.TILE, self.TILE)
            self.arrivals[name, "far", i].wait_recv()
            self.total[rows, columns] = self.total[rows, columns] + self.came_far[
                rows, columns
            ].astype(F32)

    def finish_more(self):
        kept = self.half // 2
        for bit, (sent, came) in zip(self.far[-3::-1], self.more):
            kept //= 2
            sent[...] = self.total[pl.ds(kept, kept)].astype(BF)
            copy = self.links.push(sent, came, peer(bit))
            copy.wait_recv()
            self.total[pl.ds(0, kept)] = self.total[pl.ds(0, kept)] + came[...].astype(F32)


def collect_scratch(far, width, cols):
    shapes = [
        pltpu.VMEM((width // 2, cols), BF),
        pltpu.VMEM((width // 2, cols), BF),
        pltpu.VMEM((width // 4, cols), BF),
        pltpu.VMEM((width // 4, cols), BF),
    ]
    kept = width // 4
    for _ in far[2:]:
        kept //= 2
        shapes += [pltpu.VMEM((kept, cols), BF)] * 2
    return shapes


def paired(refs):
    return [(refs[i], refs[i + 1]) for i in range(0, len(refs), 2)]


class GroupSum:
    def __init__(self, links, count, width, chunks, term, part, land, low_part, land_low, summ, across):
        self.links, self.count, self.term = links, count, term
        self.part, self.land, self.low_part, self.land_low = part, land, low_part, land_low
        self.summ, self.across = summ, across
        size = width // chunks
        self.spans = [pl.ds(i * size, size) for i in range(chunks)]
        self.flight = {}

    def outer(self, slot):
        rows = pl.ds((slot // 2) * self.count, self.count)
        own = pl.ds(0, self.count)
        if slot == 1:
            self.links.settle([self.flight[3, i] for i in range(len(self.spans))])
        for i, span in enumerate(self.spans):
            self.part[own, span] = self.term(slot, span).astype(BF)
            self.flight[slot, i] = self.links.push(
                self.part.at[own, span], self.land.at[rows, span], peer(core=True)
            )

    def to_low(self, which=None):
        for i, span in enumerate(self.spans):
            if which is not None and i not in which:
                continue
            value = self.term(2, span)
            self.flight[3, i].wait_recv()
            value = value + self.land[pl.ds(self.count, self.count), span].astype(F32)
            self.low_part[:, span] = value.astype(BF)
            self.flight["low", i] = self.links.push(
                self.low_part.at[:, span], self.land_low.at[:, span], peer(LOW)
            )

    def to_half(self, which=None):
        for i, span in enumerate(self.spans):
            if which is not None and i not in which:
                continue
            value = self.term(0, span)
            self.flight["low", i].wait_recv()
            self.flight[1, i].wait_recv()
            value = value + self.land[pl.ds(0, self.count), span].astype(F32)
            value = value + self.land_low[:, span].astype(F32)
            self.summ[:, span] = value.astype(BF)
            self.flight["half", i] = self.links.push(
                self.summ.at[:, span], self.across.at[:, span], peer(tensor=True)
            )

    def wait(self):
        for i in range(len(self.spans)):
            self.flight["half", i].wait_recv()


def group_sum_scratch(count, width):
    return [
        pltpu.VMEM((count, width), BF),
        pltpu.VMEM((2 * count, width), BF),
        pltpu.VMEM((count, width), BF),
        pltpu.VMEM((count, width), BF),
    ]


def ffn_backward_kernel(far, main, *refs):
    own_in, cot_in, act_in, down_in, slope_in, n2_in, gu_in = refs[:7]
    summ, across, own_out, other_out = refs[7:11]
    cot, act, down_w, slope, n2, gu_w = refs[11:17]
    part, land, low_part, land_low = refs[17:21]
    total, sent, came, held, came_far = refs[21:26]
    more = paired(refs[26:-3])
    links = Links(*refs[-3:])
    n_own = own_in.shape[0]
    cot_load = Joint(
        [load_rearranged(links, far, own_in, cot.at[pl.ds(0, n_own)])]
        + [
            load_rearranged(
                links, far, cot_in.at[pl.ds(i * n_own, n_own)], cot.at[pl.ds((i + 1) * n_own, n_own)]
            )
            for i in range(3)
        ]
    )
    loads = [
        links.copy(src, dst)
        for src, dst in (
            (act_in, act),
            (down_in, down_w),
            (slope_in, slope),
            (n2_in, n2),
            (gu_in, gu_w),
        )
    ]
    greet([CORE, TENSOR] + chips_apart(LOW, *far))
    group, width = cot.shape
    count = group // 4
    down_cols, gu_cols = down_w.shape[1], gu_w.shape[1]
    grads = slope.at[:, pl.ds(0, gu_cols)]
    down_job = (pl.ds(0, down_cols), cot, act)
    gu_job = (pl.ds(down_cols, gu_cols), n2, grads)
    collect = Collect(links, far, width, sent, came, held, came_far, total, more)

    cot_load.wait()
    loads[0].wait()
    upper, lower = list(collect.upper()), list(collect.lower())
    collect.send_half("d", down_job, upper)
    loads[1].wait()
    loads[2].wait()
    lane = lax.broadcasted_iota(jnp.int32, (256, 128), 1)

    def slopes(start):
        span = pl.ds(start, 256)
        grad_act = dot_plain(cot[span], down_w[...])
        gate = grad_act * slope[span, 0:down_cols].astype(F32)
        upward = grad_act * slope[span, down_cols : 2 * down_cols].astype(F32)
        slope[span, 0:main] = gate[:, :main].astype(BF)
        slope[span, main : 2 * main] = upward[:, :main].astype(BF)
        last = jnp.where(lane < 64, gate[:, main:], pltpu.roll(upward[:, main:], 64, 1))
        slope[span, 2 * main : 2 * main + 128] = last.astype(BF)

    by_rows(0, group, 256, slopes)
    loads[3].wait()
    collect.send_half("g", gu_job, upper)

    loads[4].wait()

    def term(slot, span):
        return dot_last(slope[pl.ds(slot * count, count), 0:gu_cols], gu_w[span])

    sums = GroupSum(
        links, count, width, 4, term, part, land, low_part, land_low, summ, across
    )
    sums.outer(3)
    collect.own_half("d", down_job, upper)
    sums.to_low()
    sums.outer(1)
    collect.send_half("d", down_job, lower)
    collect.send_half("g", gu_job, lower)
    collect.own_half("g", gu_job, upper)
    sums.to_half()
    collect.own_half("d", down_job, lower)
    collect.own_half("g", gu_job, lower)
    collect.finish("d", down_job)
    collect.finish("g", gu_job)
    collect.finish_more()
    half_unit = own_out.shape[0]
    low = low_bit()
    own_out[...] = total[pl.ds(pl.multiple_of(low * half_unit, half_unit), half_unit)]
    other_out[...] = total[
        pl.ds(pl.multiple_of((1 - low) * half_unit, half_unit), half_unit)
    ].astype(BF)
    sums.wait()
    links.close()


def ffn_backward(far, main, own, cot, act, down_w, slope, n2, gu_w):
    group, width = n2.shape
    count = group // 4
    cols = gu_w.shape[1] + down_w.shape[1]
    inputs = (own, cot, act, down_w, slope, n2, gu_w)
    return pl.pallas_call(
        functools.partial(ffn_backward_kernel, far, main),
        in_specs=[ANY] * 7,
        out_specs=[VMEM] * 4,
        out_shape=[
            jax.ShapeDtypeStruct((count, width), BF),
            jax.ShapeDtypeStruct((count, width), BF),
            jax.ShapeDtypeStruct((width // 2 ** (len(far) + 1), cols), F32),
            jax.ShapeDtypeStruct((width // 2 ** (len(far) + 1), cols), BF),
        ],
        scratch_shapes=[pltpu.VMEM((group, width), BF)]
        + [pltpu.VMEM(a.shape, BF) for a in inputs[2:]]
        + group_sum_scratch(count, width)
        + [pltpu.VMEM((width // 4, cols), F32)]
        + collect_scratch(far, width, cols)
        + link_scratch(128, 64),
        compiler_params=pltpu.CompilerParams(
            collective_id=2, has_side_effects=True, vmem_limit_bytes=VMEM_BIG
        ),
        name="ffn_backward",
    )(*inputs)


def finale_kernel(far, micro, *refs):
    (
        gain_rows,
        middle_in,
        cot_in,
        grad_two_in,
        across_two_in,
        hid_in,
        cos_in,
        sin_in,
        kpos,
        rowinfo,
        queries_in,
        lse,
        kvs_in,
        attn_in,
        n1_in,
        mixed_in,
        act_in,
        down_in,
        ffn_own,
        ffn_other,
    ) = refs[:20]
    (
        grad_middle,
        summ,
        across,
        feed,
        feed_across,
        attn_mine,
        attn_came,
        gains,
        ffn_core,
        ffn_low,
        ffn_low_core,
    ) = refs[20:31]
    attn_w, n1, mixed, gmid, raw = refs[31:36]
    dkv_own, dkv_sent, dkv_land, side, land_side = refs[36:41]
    low_sent, low_land = refs[41:43]
    near_gains, far_gains, low_gains, core_gains = refs[43:47]
    part, land, land_low = refs[47:50]
    total, sent, came, held, came_far = refs[50:55]
    queries, kvs, cosine, sine, bias, dk, dv, act, down_w = refs[55:64]
    more = paired(refs[64:-3])
    go = raw.at[:, pl.ds(0, mixed.shape[1])]
    links = Links(*refs[-3:])
    loads = [
        links.copy(src, dst)
        for src, dst in (
            (middle_in, grad_middle),
            (grad_two_in, feed),
            (across_two_in, part),
            (attn_in, attn_w),
            (mixed_in, mixed),
            (n1_in, n1),
        )
    ]
    loads.insert(1, load_rearranged(links, far, cot_in, summ))
    span_chips = kvs_in.shape[0]
    greet([CORE, TENSOR] + chips_apart(LOW, *far) + chips_apart(*range(1, span_chips)))
    count, width = grad_middle.shape
    rows = count // micro
    n_q = queries_in.shape[1]
    n_qkv = n_q + 128
    low, core = low_bit(), core_bit()
    block = ffn_own.shape[0] // 2

    def core_rows(which):
        return pl.ds(pl.multiple_of(which * block, block), block)

    ffn_flight = [
        links.push(ffn_other, ffn_low, peer(LOW)),
        links.push(ffn_own.at[core_rows(1 - core)], ffn_core, peer(core=True)),
    ]

    feed_loads = [links.copy(act_in, act), links.copy(down_in, down_w)]

    for load in loads[:4]:
        load.wait()
    near_gains[...] = jnp.zeros_like(near_gains)

    def second_norm(start):
        span = pl.ds(start, 64)
        grad = feed[span].astype(F32) + part[span].astype(F32)
        value = grad_middle[span]
        ratio = lax.rsqrt(jnp.mean(value * value, axis=-1, keepdims=True) + epsilon)
        turned = value * ratio
        near_gains[1:2] += jnp.sum(grad * turned, axis=0, keepdims=True)
        scaled = grad * gain_rows[1:2]
        inner = jnp.mean(scaled * turned, axis=-1, keepdims=True)
        result = summ[span].astype(F32) + ratio * (scaled - turned * inner)
        grad_middle[span] = result
        gmid[span] = result.astype(BF)

    by_rows(0, count, 64, second_norm)
    own = links.push(gmid.at[pl.ds(0, count)], gmid.at[pl.ds(count, count)], peer(core=True))
    collect = Collect(links, far, width, sent, came, held, came_far, total, more)
    out_job = (pl.ds(n_qkv, n_q), gmid, mixed)
    q_job = (pl.ds(0, n_q), n1, go)
    kv_job = (pl.ds(n_q, 128), n1, raw.at[:, pl.ds(n_q, 128)])
    jobs = (("o", out_job), ("q", q_job), ("v", kv_job))
    upper, lower = list(collect.upper()), list(collect.lower())
    loads[4].wait()
    loads[5].wait()

    def mixed_back(start):
        span = pl.ds(start, 128)
        go[span] = dot_plain(gmid[span], attn_w[:, n_qkv : n_qkv + n_q]).astype(BF)

    by_rows(0, count, 128, mixed_back)
    own.wait_recv()
    by_rows(count, count, 128, mixed_back)
    collect.send_half("o", out_job, upper)
    collect.send_half("o", out_job, lower)

    def term(slot, span):
        return dot_last(act[pl.ds(slot * count, count)], down_w[span])

    sums = GroupSum(
        links, count, width, 4, term, part, land, side, land_low, feed, feed_across
    )
    for load in feed_loads:
        load.wait()
    sums.outer(3)
    sums.to_low([0, 1])
    sums.outer(1)

    def attention():
        scoped = [
            links.copy(src, dst)
            for src, dst in (
                (queries_in, queries),
                (kvs_in, kvs),
                (cos_in, cosine),
                (sin_in, sine),
            )
        ]
        for load in scoped:
            load.wait()
        def one(m, carry):
            mine = pl.ds(pl.multiple_of(m * rows, rows), rows)
            other = pl.ds(pl.multiple_of(count + m * rows, rows), rows)
            bias[...] = mask_bias(kpos[...], rowinfo[m])

            def both(ref):
                return jnp.concatenate([ref[mine], ref[other]], axis=0)

            kv = jnp.concatenate(
                [kvs[key, span] for key in range(span_chips) for span in (mine, other)], axis=0
            )
            grad_q = attend_back(bias, both(queries), both(go), lse[m], kv, dk, dv)
            grad_q = turn(grad_q, both(cosine), both(sine), True).astype(BF)
            raw[mine, 0:n_q] = grad_q[:rows]
            raw[other, 0:n_q] = grad_q[rows:]
            for key in range(span_chips):
                for place, span in ((0, mine), (rows, other)):
                    at = pl.ds(key * 2 * rows + place, rows)
                    pair = jnp.concatenate([dk[at], dv[at]], axis=1)
                    if key == 0:
                        dkv_own[span] = pair
                    else:
                        dkv_sent[key - 1, span] = pair.astype(BF)
            return carry

        lax.fori_loop(0, micro, one, 0)
        flight = [
            links.push(dkv_sent.at[key - 1], dkv_land.at[key - 1], peer(key))
            for key in range(1, span_chips)
        ]
        for load in loads[6:]:
            load.wait()
        collect.send_half("q", q_job, upper)
        collect.own_half("o", out_job, upper)
        collect.send_half("q", q_job, lower)
        sums.to_half([0, 1])
        for copy in flight:
            copy.wait_recv()

        def key_values(start):
            span = pl.ds(start, 256)
            pair = dkv_own[span]
            for key in range(span_chips - 1):
                pair = pair + dkv_land[key, span].astype(F32)
            lane = lax.broadcasted_iota(jnp.int32, pair.shape, 1)
            turned = turn(pair, cosine[span], sine[span], True)
            raw[span, n_q:n_qkv] = jnp.where(lane < HEAD_DIM, turned, pair).astype(BF)

        by_rows(0, 2 * count, 256, key_values)

    attention()

    collect.send_half("v", kv_job, upper)
    collect.send_half("v", kv_job, lower)
    links.settle([sums.flight["low", i] for i in range(2)])
    spans = [pl.ds(i * (width // 4), width // 4) for i in range(4)]
    to_core = []
    for span in spans:
        side[:, span] = dot_last(raw[pl.ds(count, count)], attn_w[span, 0:n_qkv]).astype(BF)
        to_core.append(links.push(side.at[:, span], land_side.at[:, span], peer(core=True)))
    over = []
    for i, span in enumerate(spans):
        value = dot_last(raw[pl.ds(0, count)], attn_w[span, 0:n_qkv])
        to_core[i].wait_recv()
        summ[:, span] = (value + land_side[:, span].astype(F32)).astype(BF)
        over.append(links.push(summ.at[:, span], across.at[:, span], peer(tensor=True)))
    load_hid = load_rearranged(links, far, hid_in, land_side)

    for name, job in jobs[1:]:
        collect.own_half(name, job, upper)
    links.settle(to_core)
    sums.to_low([2, 3])
    half_unit = attn_mine.shape[0] * 2

    def low_rows(which):
        return pl.ds(pl.multiple_of(which * half_unit, half_unit), half_unit)

    low_flight = {}

    def to_low(name, job):
        columns = job[0]
        low_sent[:, columns] = total[low_rows(1 - low), columns].astype(BF)
        low_flight[name] = links.push(low_sent.at[:, columns], low_land.at[:, columns], peer(LOW))

    collect.own_half("o", out_job, lower)
    collect.finish("o", out_job)
    if not collect.more:
        to_low("o", out_job)
    for name, job in jobs[1:]:
        collect.own_half(name, job, lower)
    for name, job in jobs[1:]:
        collect.finish(name, job)
        if not collect.more:
            to_low(name, job)
    if collect.more:
        collect.finish_more()
        for name, job in jobs:
            to_low(name, job)

    for copy in over:
        copy.wait_recv()
    load_hid.wait()

    def first_norm(start):
        span = pl.ds(start, 64)
        value = land_side[span].astype(F32)
        ratio = lax.rsqrt(jnp.mean(value * value, axis=-1, keepdims=True) + epsilon)
        grad = summ[span].astype(F32) + across[span].astype(F32)
        turned = value * ratio
        near_gains[0:1] += jnp.sum(grad * turned, axis=0, keepdims=True)
        scaled = grad * gain_rows[0:1]
        inner = jnp.mean(scaled * turned, axis=-1, keepdims=True)
        grad_middle[span] = grad_middle[span] + ratio * (scaled - turned * inner)

    by_rows(0, count, 64, first_norm)
    kept, base = width, 0
    for bit in far[::-1]:
        kept //= 2
        landed = far_gains.at[:, pl.ds(base, kept)]
        copy = links.push(near_gains.at[:, pl.ds(kept, kept)], landed, peer(bit))
        if base == 0:
            sums.to_half([2, 3])
        copy.wait_recv()
        near_gains[:, 0:kept] = near_gains[:, 0:kept] + landed[...]
        base += kept
    copy = links.push(near_gains.at[:, pl.ds(0, kept)], low_gains, peer(LOW))
    ffn_flight[0].wait_recv()
    ffn_flight.append(
        links.push(ffn_low.at[core_rows(1 - core)], ffn_low_core, peer(core=True))
    )
    copy.wait_recv()
    gains[...] = near_gains[:, 0:kept] + low_gains[...]
    copy = links.push(gains, core_gains, peer(core=True))

    core_flight = []
    for name, job in jobs:
        columns = job[0]
        low_flight[name].wait_recv()
        total[0:half_unit, columns] = total[low_rows(low), columns] + low_land[:, columns].astype(
            F32
        )
        core_flight.append(
            links.push(
                total.at[core_rows(1 - core), columns], attn_came.at[:, columns], peer(core=True)
            )
        )
        attn_mine[:, columns] = total[core_rows(core), columns]
    copy.wait_recv()
    for flight in core_flight:
        flight.wait_recv()
    for flight in ffn_flight[1:]:
        flight.wait_recv()
    sums.wait()
    links.close()
    gains[...] = gains[...] + core_gains[...]


def finale(far, micro, inputs):
    (
        gain_rows,
        middle,
        cot,
        grad_two,
        across_two,
        hid,
        cosine,
        sine,
        kpos,
        rowinfo,
        queries,
        lse,
        kvs,
        attn_w,
        n1,
        mixed,
        act,
        down_w,
        ffn_own,
        ffn_other,
    ) = inputs
    count, width = middle.shape
    n_q = mixed.shape[1]
    attn_cols, ffn_cols = attn_w.shape[1], ffn_own.shape[1]
    unit = width // 2 ** len(far)
    block = unit // 4
    span_chips = kvs.shape[0]

    def shape(dtype, *dims):
        return jax.ShapeDtypeStruct(dims, dtype)

    rows = shape(BF, count, width)
    any_or_vmem = [VMEM] + [ANY] * 7 + [VMEM] * 2 + [ANY] + [VMEM] + [ANY] * 8
    return pl.pallas_call(
        functools.partial(finale_kernel, far, micro),
        in_specs=any_or_vmem,
        out_specs=[VMEM] * 6 + [ANY, VMEM] + [ANY] * 3,
        out_shape=[
            shape(F32, count, width),
            rows,
            rows,
            rows,
            rows,
            shape(F32, block, attn_cols),
            shape(F32, block, attn_cols),
            shape(F32, 8, unit),
            shape(F32, block, ffn_cols),
            shape(BF, 2 * block, ffn_cols),
            shape(BF, block, ffn_cols),
        ],
        scratch_shapes=[
            pltpu.VMEM((width, attn_cols), BF),
            pltpu.VMEM((2 * count, width), BF),
            pltpu.VMEM((2 * count, n_q), BF),
            pltpu.VMEM((2 * count, width), BF),
            pltpu.VMEM((2 * count, n_q + 128), BF),
            pltpu.VMEM((2 * count, 128), F32),
            pltpu.VMEM((span_chips - 1, 2 * count, 128), BF),
            pltpu.VMEM((span_chips - 1, 2 * count, 128), BF),
            pltpu.VMEM((count, width), BF),
            pltpu.VMEM((count, width), BF),
            pltpu.VMEM((2 * block, attn_cols), BF),
            pltpu.VMEM((2 * block, attn_cols), BF),
            pltpu.VMEM((8, width), F32),
            pltpu.VMEM((8, width), F32),
            pltpu.VMEM((8, unit), F32),
            pltpu.VMEM((8, unit), F32),
        ]
        + group_sum_scratch(count, width)[:3]
        + [pltpu.VMEM((width // 4, attn_cols), F32)]
        + collect_scratch(far, width, attn_cols)[:4]
        + [
            pltpu.VMEM(queries.shape, BF),
            pltpu.VMEM(kvs.shape, BF),
            pltpu.VMEM(cosine.shape, F32),
            pltpu.VMEM(sine.shape, F32),
            pltpu.VMEM((kpos.shape[0], rowinfo.shape[2]), F32),
            pltpu.VMEM((kpos.shape[0], HEAD_DIM), F32),
            pltpu.VMEM((kpos.shape[0], HEAD_DIM), F32),
            pltpu.VMEM(act.shape, BF),
            pltpu.VMEM(down_w.shape, BF),
        ]
        + collect_scratch(far, width, attn_cols)[4:]
        + link_scratch(192, 64),
        compiler_params=pltpu.CompilerParams(
            collective_id=3, has_side_effects=True, vmem_limit_bytes=VMEM_BIG
        ),
        name="finale",
    )(*inputs)


def place_kernel(
    main, where, mine, came, own, own_core, far_low, far_core, query, key, value, out, gate, up, down
):
    block = mine.shape[0]
    n_q = query.shape[1] // 2
    rest = gate.shape[1] // 4 - main
    base = main + 128
    for low in range(2):
        for core in range(2):

            @pl.when((where[0] == low) & (where[1] == core))
            def _():
                rows = pl.ds(core * block, block)
                attn = {core: mine, 1 - core: came}
                for side in range(2):
                    part = attn[side]
                    query[:, side * n_q : (side + 1) * n_q] = part[:, 0:n_q]
                    span = slice(side * HEAD_DIM, (side + 1) * HEAD_DIM)
                    key[:, span] = part[:, n_q : n_q + HEAD_DIM]
                    value[:, span] = part[:, n_q + HEAD_DIM : n_q + 128]
                    out[:, side * n_q : (side + 1) * n_q] = part[:, n_q + 128 : 2 * n_q + 128]
                ffn = {
                    (low, core): own.at[rows],
                    (low, 1 - core): own_core,
                    (1 - low, core): far_low.at[rows],
                    (1 - low, 1 - core): far_core,
                }
                for place in range(4):
                    part = ffn[place // 2, place % 2]
                    for ref, start, last in (
                        (down, 0, main),
                        (gate, base, base + 2 * main),
                        (up, base + main, base + 2 * main + rest),
                    ):
                        ref[:, place * main : (place + 1) * main] = part[
                            :, start : start + main
                        ].astype(F32)
                        ends = 4 * main + place * rest
                        ref[:, ends : ends + rest] = part[:, last : last + rest].astype(F32)


def place_grads(main, where, shapes, parts):
    return pl.pallas_call(
        functools.partial(place_kernel, main),
        in_specs=[pl.BlockSpec(memory_space=pltpu.SMEM)] + [VMEM] * 6,
        out_specs=[VMEM] * 7,
        out_shape=[jax.ShapeDtypeStruct(shape, F32) for shape in shapes],
        compiler_params=pltpu.CompilerParams(vmem_limit_bytes=VMEM_LIMIT),
        name="place_grads",
    )(where, *parts)


def restore_kernel(places, middle, feed, feed_across, grad, output, grad_out):
    value = middle[...] + (feed[...].astype(F32) + feed_across[...].astype(F32))
    output[...] = value.astype(BF)
    grad_out[...] = grad[...]


def restore(places, block, middle, feed, feed_across, grad):
    count, width = middle.shape
    moved = pl.BlockSpec((count, block), lambda i, places: (0, places[i]))
    kept = pl.BlockSpec((count, block), lambda i, places: (0, i))
    return pl.pallas_call(
        restore_kernel,
        grid_spec=pltpu.PrefetchScalarGridSpec(
            num_scalar_prefetch=1,
            grid=(width // block,),
            in_specs=[moved] * 4,
            out_specs=[kept] * 2,
        ),
        out_shape=[
            jax.ShapeDtypeStruct((count, width), BF),
            jax.ShapeDtypeStruct((count, width), F32),
        ],
        compiler_params=pltpu.CompilerParams(vmem_limit_bytes=VMEM_LIMIT),
        name="restore",
    )(places, middle, feed, feed_across, grad)


def body(
    tokens,
    doc_position,
    attn_gain,
    w_query,
    w_key,
    w_value,
    w_out,
    ffn_gain,
    w_gate,
    w_up,
    w_down,
    cotangent,
):
    size = lax.axis_size("dp")
    chips = size // 2
    far = [1 << place for place in range(chips.bit_length() - 1) if 1 << place != LOW][::-1]
    me = lax.axis_index("dp")
    core = me % 2
    chip = me // 2
    low = (chip // LOW) % 2
    micro, stretch, width = tokens.shape
    count = micro * stretch
    block = width // chips
    own_block = block // 2
    span_chips = SEQ_LEN // (2 * stretch)
    in_span = chip % span_chips

    keys = [0]
    for bit in far:
        keys = keys + [key | bit for key in keys]

    def rearranged(array):
        base = chip - LOW * low
        return jnp.concatenate(
            [
                lax.dynamic_slice_in_dim(
                    array, ((base ^ key) + LOW * side) * block, block, array.ndim - 1
                )
                for key in keys
                for side in range(2)
            ],
            axis=-1,
        )

    unit_of = jnp.array([keys.index(other & ~LOW) for other in range(chips)], jnp.int32)
    naturals = jnp.arange(chips, dtype=jnp.int32)
    places = unit_of[chip ^ naturals] * 2 + (naturals // LOW) % 2

    def restored(array):
        return jnp.concatenate(
            [
                lax.dynamic_slice_in_dim(array, places[natural] * block, block, array.ndim - 1)
                for natural in range(chips)
            ],
            axis=-1,
        )

    def halves(array):
        n = array.shape[1] // 2
        return array[:, :n], array[:, n:]

    attn_pack = jnp.concatenate(
        [
            halves(w)[side]
            for side in range(2)
            for w in (w_query, w_key, w_value, w_out.T)
        ],
        axis=1,
    )
    hidden_units = w_gate.shape[1] // 4
    main = hidden_units // 128 * 128
    rest = hidden_units - main
    assert rest == 64

    def rests(array, place):
        return array[:, 4 * main + place * rest : 4 * main + (place + 1) * rest]

    w_down_t = w_down.T
    empty = jnp.zeros((own_block, 128 - rest), BF)
    ends_pack = jnp.concatenate(
        [
            piece
            for place in range(4)
            for piece in (
                rests(w_gate, place),
                rests(w_up, place),
                rests(w_down_t, place),
                empty,
            )
        ],
        axis=1,
    )
    gain_pack = jnp.zeros((16, 128), BF).at[0, :own_block].set(attn_gain)
    gain_pack = gain_pack.at[1, :own_block].set(ffn_gain)
    hidden = tokens.reshape(count, width)
    grad_final = cotangent.reshape(count, width)
    if block % 128:
        hidden, grad_final = rearranged(hidden), rearranged(grad_final)

    position_both = jnp.stack([doc_position, swap_core(doc_position)])

    power = jnp.arange(HEAD_DIM // 2, dtype=F32) * (2.0 / HEAD_DIM)
    inverse = 10000.0 ** (-power)
    turned = position_both.reshape(2 * count).astype(F32)[:, None] * jnp.tile(inverse, 4)[None, :]
    cosine, sine = jnp.cos(turned), jnp.sin(turned)

    inner = jnp.arange(2 * stretch, dtype=jnp.int32) ^ (core * stretch)
    row_place = in_span * (2 * stretch) + inner
    kpos = jnp.concatenate(
        [(in_span ^ key) * (2 * stretch) + inner for key in range(span_chips)]
    ).reshape(-1, 1)
    row_position = position_both.transpose(1, 0, 2).reshape(micro, 2 * stretch)
    row_places = jnp.broadcast_to(row_place[None, :], row_position.shape)
    rowinfo = jnp.stack([row_places, row_places - row_position], axis=1)

    n_q = w_query.shape[1] // 2
    n_kv = w_key.shape[1] // 2
    n_qkv = n_q + 2 * n_kv
    (
        gain_rows,
        lse,
        middle,
        activated,
        slopes,
        mixed,
        queries,
        kvs,
        normed,
        attn_w,
        normed_two,
        gu_w,
        down_wt,
        grad_final_others,
    ) = forward(
        far,
        main,
        micro,
        span_chips,
        (gain_pack, attn_pack, w_gate, w_up, w_down_t, ends_pack, hidden, grad_final),
        (cosine, sine, kpos, rowinfo),
    )
    gain_one, gain_two = gain_rows[0:1], gain_rows[1:2]
    grad_two, grad_two_across, ffn_own, ffn_other = ffn_backward(
        far, main, grad_final, grad_final_others, activated, down_wt, slopes, normed_two, gu_w
    )
    (
        grad_hidden,
        _,
        _,
        feed,
        feed_across,
        attn_mine,
        attn_came,
        grad_gains,
        ffn_core,
        ffn_low,
        ffn_low_core,
    ) = finale(
        far,
        micro,
        (
            gain_rows,
            middle,
            grad_final,
            grad_two,
            grad_two_across,
            hidden,
            cosine,
            sine,
            kpos,
            rowinfo,
            queries,
            lse,
            kvs,
            attn_w,
            normed,
            mixed,
            activated,
            down_wt,
            ffn_own,
            ffn_other,
        ),
    )
    if block % 128:
        output = restored((middle + (feed.astype(F32) + feed_across.astype(F32))).astype(BF))
        grad_tokens = restored(grad_hidden)
    else:
        output, grad_tokens = restore(places, block, middle, feed, feed_across, grad_hidden)
    grad_gains = lax.dynamic_slice_in_dim(grad_gains, (2 * low + core) * own_block, own_block, 1)

    grad_w_query, grad_w_key, grad_w_value, grad_out_t, grad_w_gate, grad_w_up, grad_down_t = (
        place_grads(
            main,
            jnp.stack([low, core]),
            [
                w_query.shape,
                w_key.shape,
                w_value.shape,
                w_out.shape[::-1],
                w_gate.shape,
                w_up.shape,
                w_down.shape[::-1],
            ],
            (attn_mine, attn_came, ffn_own, ffn_core, ffn_low, ffn_low_core),
        )
    )
    grad_w_out, grad_w_down = grad_out_t.T, grad_down_t.T
    return (
        output.reshape(tokens.shape),
        grad_tokens.reshape(tokens.shape),
        grad_gains[0],
        grad_w_query,
        grad_w_key,
        grad_w_value,
        grad_w_out,
        grad_gains[1],
        grad_w_gate,
        grad_w_up,
        grad_w_down,
    )


def solution(mesh):
    return jax.shard_map(
        body,
        mesh=mesh,
        in_specs=(
            P(None, "dp", None),
            P(None, "dp"),
            P("dp"),
            P("dp", "tensor"),
            P("dp", "tensor"),
            P("dp", "tensor"),
            P("tensor", "dp"),
            P("dp"),
            P("dp", "tensor"),
            P("dp", "tensor"),
            P("tensor", "dp"),
            P(None, "dp", None),
        ),
        out_specs=(
            P(None, "dp", None),
            P(None, "dp", None),
            P("dp"),
            P("dp", "tensor"),
            P("dp", "tensor"),
            P("dp", "tensor"),
            P("tensor", "dp"),
            P("dp"),
            P("dp", "tensor"),
            P("dp", "tensor"),
            P("tensor", "dp"),
        ),
        check_vma=False,
    )
```
